512 devices in a mesh: tm: 8 (over x, core), series: 64 (over y, z).
Axes of the slice: x: 4, y: 8, z: 8, core: 2. Of those that a mesh axis runs over, the one named last changes fastest.
Arguments:
- leaf_outlook_matrix: float32 [384, 131072], P('tm', 'series'), may hold values from -6 to 6
- seasonal_leaf_outlook: float32 [5, 131072], P(None, 'series'), may hold values from -640 to 640
- lowest_tier_ancestor: int32 [131072, 1], P('series'), may hold values from 0 to 4095, as said below
- middle_tier_ancestor: int32 [131072, 1], P('series'), may hold values from 0 to 511
- uppermost_ancestor: int32 [131072, 1], P('series'), may hold values from 0 to 63
- lowest_tier_outlook: float32 [384, 4096], P('tm', 'series'), may hold values from -48 to 48
- middle_tier_outlook: float32 [384, 512], P('tm', 'series'), may hold values from -128 to 128
- uppermost_outlook: float32 [384, 64], P('tm', 'series'), may hold values from -384 to 384
Outputs:
- reconciled: float32 [384, 131072], P('tm', 'series')
The draws below stay inside these ranges and needn't reach their ends.
Inputs may be any that keep to these rules, and one draw needn't show every extreme that they name: `lowest_tier_ancestor`: every node has at least one series; the owner of a node n is n // 64, and each aligned block of 2048 series holds exactly 32 series of the nodes of each owner. `middle_tier_ancestor`: every node of the level has at least one series. `uppermost_ancestor`: every node of the level has at least one series.
All inputs are finite; a program needn't handle non-finite values.
Results may differ from the reference program's by a relative error of at most 0.0013.
Values may be sent and summed in bfloat16 or wider, within the bound.
No kernel may reach another device: no remote copies, remote signals or barrier semaphores. Data moves between devices by JAX's collectives and lax.ppermute only.
A program may use at most 64 MiB of HBM per device.

```python
import jax
import jax.numpy as jnp
from jax import lax

ROWS = 2048
NODE_DEV = 64
LEAF_TALLY = 131072
CALENDAR_LENGTH = 384
SEASON_LENGTH = 96
LOWEST_TIER = 4096
MIDDLE_TIER = 512
UPPERMOST_TIER = 64


def draw_lowest_tier_ancestor(key, part):
    key = jax.random.fold_in(key, 11)
    owners = LEAF_TALLY // ROWS
    slots = ROWS // owners
    first_key, second_key, third_key, order_key, place_key = jax.random.split(key, 5)
    one = jax.random.randint(first_key, (owners, ROWS), 0, NODE_DEV)
    two = jax.random.randint(second_key, (owners, ROWS), 0, NODE_DEV)
    three = jax.random.randint(third_key, (owners, ROWS), 0, NODE_DEV)
    skewed = jnp.minimum(jnp.minimum(one, two), three)
    orders = jax.vmap(lambda k: jax.random.permutation(k, NODE_DEV))(jax.random.split(order_key, owners))
    column = jnp.arange(ROWS, dtype=jnp.int32)
    covered = orders[:, jnp.minimum(column, NODE_DEV - 1)]
    heavy = jnp.take_along_axis(orders, skewed, axis=1)
    local = jnp.where(column[None, :] < NODE_DEV, covered, heavy)
    whole = jnp.arange(owners, dtype=jnp.int32)[:, None] * NODE_DEV + local
    values = jnp.transpose(whole.reshape(owners, owners, slots), (1, 0, 2)).reshape(owners, ROWS)
    places = jax.vmap(lambda k: jax.random.permutation(k, ROWS))(jax.random.split(place_key, owners))
    result = jnp.zeros((owners, ROWS), jnp.int32)
    result = result.at[jnp.arange(owners, dtype=jnp.int32)[:, None], places].set(values)
    return result.reshape(LEAF_TALLY, 1)


def shard_levels(own_key, dims, cuts, least, largest):
    loudness = 1.0
    for axis_at, parts in cuts:
        draws = jax.random.uniform(jax.random.fold_in(jax.random.fold_in(own_key, 6), axis_at), (parts,), jnp.float32, least / len(cuts), largest / len(cuts))
        loudness = loudness * jnp.repeat(jnp.exp(draws), dims[axis_at] // parts).reshape((-1,) + (1,) * (len(dims) - 1 - axis_at))
    return loudness


def choose_distinct(key, rows, amount, top, lift):
    ranking = jax.random.permutation(jax.random.fold_in(key, 1), amount)
    pull = ranking
    for power in range(3):
        pull = pull * pull // amount
    pull = pull * lift // amount
    tickets = jax.random.randint(jax.random.fold_in(key, 2), (rows, amount), 0, 4096) + pull
    holders = jax.random.permutation(jax.random.fold_in(key, 3), rows)[jnp.arange(amount) % rows]
    tickets = jnp.where(jnp.arange(rows)[:, None] == holders[None, :], 1 << 14, tickets)
    merit = tickets * amount + jnp.arange(amount)
    return lax.top_k(merit.astype(jnp.int32), top)[1].astype(jnp.int32)


def normal_values(own_key, extent, deviation, limit, pieces=(), kind=jnp.bfloat16):
    level = shard_levels(own_key, extent, pieces, -0.22, 0.18) if pieces else 1.0
    values = jax.random.normal(own_key, extent, jnp.float32) * deviation * level
    return jnp.minimum(jnp.maximum(values, -limit), limit).astype(kind)


def setup_inputs(seed: int = 0) -> dict:
    splits = jax.random.split(jax.random.key(seed), 9)
    leaf_outlook_matrix = normal_values(splits[0], (CALENDAR_LENGTH, LEAF_TALLY), 1.0, 6.0, ((0, 8), (1, 64)), jnp.float32)
    seasonal_leaf_outlook = normal_values(splits[1], (5, LEAF_TALLY), 100.0, 640.0, ((1, 64),), jnp.float32)
    lowest_tier_ancestor = draw_lowest_tier_ancestor(jax.random.fold_in(splits[8], 71), 0)
    middle_tier_ancestor = choose_distinct(splits[3], LEAF_TALLY, MIDDLE_TIER, 1, 32)
    uppermost_ancestor = choose_distinct(splits[4], LEAF_TALLY, UPPERMOST_TIER, 1, 128)
    lowest_tier_outlook = normal_values(splits[5], (CALENDAR_LENGTH, LOWEST_TIER), 8.0, 48.0, ((0, 8), (1, 64)), jnp.float32)
    middle_tier_outlook = normal_values(splits[6], (CALENDAR_LENGTH, MIDDLE_TIER), 20.0, 128.0, ((0, 8), (1, 64)), jnp.float32)
    uppermost_outlook = normal_values(splits[7], (CALENDAR_LENGTH, UPPERMOST_TIER), 60.0, 384.0, ((0, 8), (1, 64)), jnp.float32)
    return {"leaf_outlook_matrix": leaf_outlook_matrix, "seasonal_leaf_outlook": seasonal_leaf_outlook, "lowest_tier_ancestor": lowest_tier_ancestor, "middle_tier_ancestor": middle_tier_ancestor, "uppermost_ancestor": uppermost_ancestor, "lowest_tier_outlook": lowest_tier_outlook, "middle_tier_outlook": middle_tier_outlook, "uppermost_outlook": uppermost_outlook}


def tier_piece(nearest_integer, ids, base, nodes):
    totals = jax.ops.segment_sum(nearest_integer.T, ids, nodes)
    count = jax.ops.segment_sum(jnp.ones(ids.shape, jnp.float32), ids, nodes)
    gap = ((base.T - totals) / (count[:, None] + 1.0)).astype(jnp.bfloat16)
    gap = lax.optimization_barrier(gap).astype(jnp.float32)
    return gap[ids].T


def reference(leaf_outlook_matrix, seasonal_leaf_outlook, lowest_tier_ancestor, middle_tier_ancestor, uppermost_ancestor, lowest_tier_outlook, middle_tier_outlook, uppermost_outlook):
    seasonal_summed_values = jnp.sum(leaf_outlook_matrix.reshape(4, SEASON_LENGTH, LEAF_TALLY), axis=1)
    seasonal_discrepancy = 0.5 * (seasonal_leaf_outlook[:4] - seasonal_summed_values) / SEASON_LENGTH
    harmonize_over_calendar = leaf_outlook_matrix + jnp.repeat(seasonal_discrepancy, SEASON_LENGTH, axis=0)
    calendar_accumulation = jnp.sum(0.5 * seasonal_summed_values + 0.5 * seasonal_leaf_outlook[:4], axis=0)
    per_diem = harmonize_over_calendar + 0.5 * (seasonal_leaf_outlook[4] - calendar_accumulation) / CALENDAR_LENGTH
    nearest_integer = lax.optimization_barrier(per_diem.astype(jnp.bfloat16)).astype(jnp.float32)
    lowest_tier_piece = tier_piece(nearest_integer, lowest_tier_ancestor[:, 0], lowest_tier_outlook, LOWEST_TIER)
    middle_tier_piece = tier_piece(nearest_integer, middle_tier_ancestor[:, 0], middle_tier_outlook, MIDDLE_TIER)
    uppermost_piece = tier_piece(nearest_integer, uppermost_ancestor[:, 0], uppermost_outlook, UPPERMOST_TIER)
    return per_diem + lowest_tier_piece + middle_tier_piece + uppermost_piece
```

```python
import jax
import jax.numpy as jnp
from jax import lax
from jax.experimental import pallas as pl
from jax.experimental.pallas import tpu as pltpu
from jax.sharding import PartitionSpec as P

f32 = jnp.float32
bf16 = jnp.bfloat16
i32 = jnp.int32

PARAMS = pltpu.CompilerParams(vmem_limit_bytes=48 * 1024 * 1024)


def iota(shape, dim):
    return lax.broadcasted_iota(i32, shape, dim)


def ones_where(mask):
    return jnp.where(mask, 1.0, 0.0).astype(bf16)


def dot(a, b):
    return jnp.dot(a, b, preferred_element_type=f32)


def corrections(seas, parts, quarter, days):
    n_parts = parts.shape[0]
    per = n_parts // 4
    season_days = days * per
    own = jnp.sum(jnp.where(iota(parts.shape, 0) // per == quarter, parts, 0.0), axis=0, keepdims=True)
    rows = iota(seas.shape, 0)
    seas_own = jnp.sum(jnp.where(rows == quarter, seas, 0.0), axis=0, keepdims=True)
    seas_four = jnp.sum(jnp.where(rows < 4, seas, 0.0), axis=0, keepdims=True)
    year = 0.5 * jnp.sum(parts, axis=0, keepdims=True) + 0.5 * seas_four
    first = 0.5 * (seas_own - own) / season_days
    second = 0.5 * (seas[4:5, :] - year) / (season_days * 4)
    return first, second


def day_sum_kernel(leaf_ref, out_ref):
    out_ref[...] = jnp.sum(leaf_ref[...], axis=0, keepdims=True)


def send_kernel(quarter_ref, leaf_ref, seas_ref, parts_ref, fine_ref, mid_ref, top_ref, pay_ref, places_ref, shift_ref, wide_ref):
    days, rows = leaf_ref.shape
    owners = pay_ref.shape[0]
    first, second = corrections(seas_ref[...], parts_ref[...], quarter_ref[0], days)
    shift_ref[0:1, :] = first
    shift_ref[1:2, :] = second
    daily = (leaf_ref[...] + first) + second
    fine = fine_ref[...]
    node_dev = 64
    owner = fine // node_dev
    local = fine - owner * node_dev

    step = min(256, rows)
    before = ones_where(iota((step, step), 0) < iota((step, step), 1))
    base = jnp.zeros((owners, 1), f32)
    ranks = []
    for at in range(0, rows, step):
        hit = owner[:, at:at + step] == iota((owners, step), 0)
        hit_f = jnp.where(hit, 1.0, 0.0)
        seen = dot(hit_f.astype(bf16), before) + base
        ranks.append(jnp.sum(jnp.where(hit, seen, 0.0), axis=0, keepdims=True))
        base = base + jnp.sum(hit_f, axis=1, keepdims=True)
    rank = jnp.concatenate(ranks, axis=1).astype(i32)
    place = owner * 16 + (rank & 15)
    place_low = jnp.where(rank < 16, place, -1)
    place_high = jnp.where(rank < 16, -1, place)
    mid = mid_ref[...]
    place_mid = (mid // 8) * 16 + (mid & 7)
    place_top = top_ref[...] * 16 + 8
    places_ref[0:1, :] = place_low
    places_ref[1:2, :] = place_high
    places_ref[2:3, :] = place_mid
    places_ref[3:4, :] = place_top

    rounded = daily.astype(bf16).astype(f32)
    ext = jnp.concatenate([rounded, local.astype(f32), jnp.ones((1, rows), f32), jnp.zeros((14, rows), f32)], axis=0)
    for at in range(0, rows, 128):
        turned = jnp.transpose(ext[:, at:at + 128])
        wide_ref[at:at + 128, :] = jnp.concatenate([turned, turned], axis=1).astype(bf16)
    wide = wide_ref[...]

    group = min(8, owners)
    chunk = group * 16
    low_half = iota((chunk, 128), 1) < 64
    for g in range(owners // group):
        row = iota((chunk, rows), 0) + g * chunk
        slots = jnp.where(
            low_half,
            dot(ones_where(row == place_low), wide),
            dot(ones_where(row == place_high), wide),
        ).astype(bf16)
        sums = dot(ones_where((row == place_mid) | (row == place_top)), wide)
        high = sums.astype(bf16)
        sums = jnp.where(low_half, high.astype(f32), sums - high.astype(f32)).astype(bf16)
        pay_ref[pl.ds(g * group, group), 0:16, :] = slots.reshape(group, 16, 128)
        pay_ref[pl.ds(g * group, group), 16:32, :] = sums.reshape(group, 16, 128)


def owner_kernel(got_ref, base_fine_ref, base_rest_ref, back_ref):
    owners = got_ref.shape[0]
    days, nodes = base_fine_ref.shape
    slots = got_ref[:, 0:16, :].reshape(owners * 16, 128).astype(f32)
    low_half = iota((owners * 16, 128), 1) < 64
    lane = iota((owners * 16, nodes), 1).astype(f32)
    pick_low = ones_where(slots[:, days:days + 1] == lane)
    pick_high = ones_where(slots[:, 64 + days:65 + days] == lane)
    turned = jnp.transpose(slots).astype(bf16)
    totals = dot(turned[0:64, :], pick_low) + dot(turned[64:128, :], pick_high)
    gap = (base_fine_ref[...] - totals[0:days, :]) / (totals[days + 1:days + 2, :] + 1.0)
    gap = jnp.concatenate([gap, jnp.zeros((64 - days, nodes), f32)], axis=0)
    gap = jnp.transpose(jnp.concatenate([gap, gap], axis=0)).astype(bf16)
    spread = jnp.where(low_half, dot(pick_low, gap), dot(pick_high, gap)).astype(bf16)
    back_ref[:, 0:16, :] = spread.reshape(owners, 16, 128)

    rest = jnp.sum(got_ref[:, 16:32, :].astype(f32), axis=0)
    rest = rest[:, 0:64] + rest[:, 64:128]
    gap_rest = (base_rest_ref[...] - rest) / (rest[:, days + 1:days + 2] + 1.0)
    gap_rest = jnp.where(iota((16, 64), 1) < days, gap_rest, 0.0)
    gap_rest = jnp.concatenate([gap_rest, jnp.zeros((16, 64), f32)], axis=1).astype(bf16)
    back_ref[:, 16:32, :] = jnp.broadcast_to(gap_rest[None], (owners, 16, 128))


def finish_kernel(leaf_ref, shift_ref, places_ref, back_ref, out_ref):
    days, rows = leaf_ref.shape
    owners = back_ref.shape[0]
    height = owners * 16
    slots = jnp.transpose(back_ref[:, 0:16, :].reshape(height, 128).astype(f32)).astype(bf16)
    rest = jnp.transpose(back_ref[:, 16:32, :].reshape(height, 128).astype(f32)).astype(bf16)
    low, high, rest = slots[0:days, :], slots[64:64 + days, :], rest[0:days, :]
    step = min(256, rows)
    for at in range(0, rows, step):
        row = iota((height, step), 0)
        daily = (leaf_ref[:, at:at + step] + shift_ref[0:1, at:at + step]) + shift_ref[1:2, at:at + step]
        place = places_ref[:, at:at + step]
        fine = dot(low, ones_where(row == place[0:1, :])) + dot(high, ones_where(row == place[1:2, :]))
        others = dot(rest, ones_where((row == place[2:3, :]) | (row == place[3:4, :])))
        out_ref[:, at:at + step] = (daily + fine) + others


def per_device(leaf, seas, fine, mid, top, base_fine, base_mid, base_top):
    days, rows = leaf.shape
    owners = lax.axis_size("series")
    quarter = (lax.axis_index("tm") // 2).astype(i32).reshape(1)
    base_rest = jnp.concatenate([base_mid, base_top], axis=1).T
    base_rest = jnp.pad(base_rest, ((0, 16 - base_rest.shape[0]), (0, 64 - days)))
    fine, mid, top = (ids.reshape(1, rows) for ids in (fine, mid, top))

    sums = pl.pallas_call(
        day_sum_kernel, out_shape=jax.ShapeDtypeStruct((1, rows), f32), compiler_params=PARAMS, name="day_sums"
    )(leaf)
    parts = lax.all_gather(sums, "tm", axis=0, tiled=True)

    vmem = pl.BlockSpec(memory_space=pltpu.VMEM)
    payload, places, shift = pl.pallas_call(
        send_kernel,
        out_shape=(
            jax.ShapeDtypeStruct((owners, 32, 128), bf16),
            jax.ShapeDtypeStruct((4, rows), i32),
            jax.ShapeDtypeStruct((2, rows), f32),
        ),
        in_specs=[pl.BlockSpec(memory_space=pltpu.SMEM)] + [vmem] * 6,
        scratch_shapes=[pltpu.VMEM((rows, 128), bf16)],
        compiler_params=PARAMS,
        name="pack",
    )(quarter, leaf, seas, parts, fine, mid, top)
    got = lax.all_to_all(payload, "series", 0, 0, tiled=True)
    back = pl.pallas_call(
        owner_kernel,
        out_shape=jax.ShapeDtypeStruct((owners, 32, 128), bf16),
        compiler_params=PARAMS,
        name="gaps",
    )(got, base_fine, base_rest)
    back = lax.all_to_all(back, "series", 0, 0, tiled=True)
    return pl.pallas_call(
        finish_kernel,
        out_shape=jax.ShapeDtypeStruct((days, rows), f32),
        compiler_params=PARAMS,
        name="finish",
    )(leaf, shift, places, back)


def solution(mesh):
    return jax.shard_map(
        per_device,
        mesh=mesh,
        in_specs=(
            P("tm", "series"),
            P(None, "series"),
            P("series", None),
            P("series", None),
            P("series", None),
            P("tm", "series"),
            P("tm", "series"),
            P("tm", "series"),
        ),
        out_specs=P("tm", "series"),
        check_vma=False,
    )
```

```python
import math

import jax
import jax.numpy as jnp
from jax import lax
from jax.experimental import pallas as pl
from jax.experimental.pallas import tpu as pltpu
from jax.sharding import Mesh
from jax.sharding import PartitionSpec as P

f32 = jnp.float32
bf16 = jnp.bfloat16
i32 = jnp.int32

PARAMS = pltpu.CompilerParams(vmem_limit_bytes=48 * 1024 * 1024)


def iota(shape, dim):
    return lax.broadcasted_iota(i32, shape, dim)


def ones_where(mask):
    return jnp.where(mask, 1.0, 0.0).astype(bf16)


def dot(a, b):
    return jnp.dot(a, b, preferred_element_type=f32)


def corrections(seas, parts, quarter, days):
    n_parts = parts.shape[0]
    per = n_parts // 4
    season_days = days * per
    own = jnp.sum(jnp.where(iota(parts.shape, 0) // per == quarter, parts, 0.0), axis=0, keepdims=True)
    rows = iota(seas.shape, 0)
    seas_own = jnp.sum(jnp.where(rows == quarter, seas, 0.0), axis=0, keepdims=True)
    seas_four = jnp.sum(jnp.where(rows < 4, seas, 0.0), axis=0, keepdims=True)
    year = 0.5 * jnp.sum(parts, axis=0, keepdims=True) + 0.5 * seas_four
    first = 0.5 * (seas_own - own) / season_days
    second = 0.5 * (seas[4:5, :] - year) / (season_days * 4)
    return first, second


def day_sum_kernel(leaf_ref, out_ref):
    out_ref[...] = jnp.sum(leaf_ref[...], axis=0, keepdims=True)


def send_kernel(quarter_ref, leaf_ref, seas_ref, parts_ref, fine_ref, mid_ref, top_ref, pay_ref, places_ref, shift_ref, wide_ref):
    days, rows = leaf_ref.shape
    owners = pay_ref.shape[0]
    first, second = corrections(seas_ref[...], parts_ref[...], quarter_ref[0], days)
    shift_ref[0:1, :] = first
    shift_ref[1:2, :] = second
    daily = (leaf_ref[...] + first) + second
    fine = fine_ref[...]
    node_dev = 64
    owner = fine // node_dev
    local = fine - owner * node_dev

    step = min(256, rows)
    before = ones_where(iota((step, step), 0) < iota((step, step), 1))
    base = jnp.zeros((owners, 1), f32)
    ranks = []
    for at in range(0, rows, step):
        hit = owner[:, at:at + step] == iota((owners, step), 0)
        hit_f = jnp.where(hit, 1.0, 0.0)
        seen = dot(hit_f.astype(bf16), before) + base
        ranks.append(jnp.sum(jnp.where(hit, seen, 0.0), axis=0, keepdims=True))
        base = base + jnp.sum(hit_f, axis=1, keepdims=True)
    rank = jnp.concatenate(ranks, axis=1).astype(i32)
    place = owner * 16 + (rank & 15)
    place_low = jnp.where(rank < 16, place, -1)
    place_high = jnp.where(rank < 16, -1, place)
    mid = mid_ref[...]
    place_mid = (mid // 8) * 16 + (mid & 7)
    place_top = top_ref[...] * 16 + 8
    places_ref[0:1, :] = place_low
    places_ref[1:2, :] = place_high
    places_ref[2:3, :] = place_mid
    places_ref[3:4, :] = place_top

    rounded = daily.astype(bf16).astype(f32)
    ext = jnp.concatenate([rounded, local.astype(f32), jnp.ones((1, rows), f32), jnp.zeros((14, rows), f32)], axis=0)
    for at in range(0, rows, 128):
        turned = jnp.transpose(ext[:, at:at + 128])
        wide_ref[at:at + 128, :] = jnp.concatenate([turned, turned], axis=1).astype(bf16)
    wide = wide_ref[...]

    group = min(8, owners)
    chunk = group * 16
    low_half = iota((chunk, 128), 1) < 64
    for g in range(owners // group):
        row = iota((chunk, rows), 0) + g * chunk
        slots = jnp.where(
            low_half,
            dot(ones_where(row == place_low), wide),
            dot(ones_where(row == place_high), wide),
        ).astype(bf16)
        sums = dot(ones_where((row == place_mid) | (row == place_top)), wide)
        high = sums.astype(bf16)
        sums = jnp.where(low_half, high.astype(f32), sums - high.astype(f32)).astype(bf16)
        pay_ref[pl.ds(g * group, group), 0:16, :] = slots.reshape(group, 16, 128)
        pay_ref[pl.ds(g * group, group), 16:32, :] = sums.reshape(group, 16, 128)


def owner_kernel(got_ref, base_fine_ref, base_rest_ref, back_ref):
    owners = got_ref.shape[0]
    days, nodes = base_fine_ref.shape
    slots = got_ref[:, 0:16, :].reshape(owners * 16, 128).astype(f32)
    low_half = iota((owners * 16, 128), 1) < 64
    lane = iota((owners * 16, nodes), 1).astype(f32)
    pick_low = ones_where(slots[:, days:days + 1] == lane)
    pick_high = ones_where(slots[:, 64 + days:65 + days] == lane)
    turned = jnp.transpose(slots).astype(bf16)
    totals = dot(turned[0:64, :], pick_low) + dot(turned[64:128, :], pick_high)
    gap = (base_fine_ref[...] - totals[0:days, :]) / (totals[days + 1:days + 2, :] + 1.0)
    gap = jnp.concatenate([gap, jnp.zeros((64 - days, nodes), f32)], axis=0)
    gap = jnp.transpose(jnp.concatenate([gap, gap], axis=0)).astype(bf16)
    spread = jnp.where(low_half, dot(pick_low, gap), dot(pick_high, gap)).astype(bf16)
    back_ref[:, 0:16, :] = spread.reshape(owners, 16, 128)

    rest = jnp.sum(got_ref[:, 16:32, :].astype(f32), axis=0)
    rest = rest[:, 0:64] + rest[:, 64:128]
    gap_rest = (base_rest_ref[...] - rest) / (rest[:, days + 1:days + 2] + 1.0)
    gap_rest = jnp.where(iota((16, 64), 1) < days, gap_rest, 0.0)
    gap_rest = jnp.concatenate([gap_rest, jnp.zeros((16, 64), f32)], axis=1).astype(bf16)
    back_ref[:, 16:32, :] = jnp.broadcast_to(gap_rest[None], (owners, 16, 128))


def finish_kernel(leaf_ref, shift_ref, places_ref, back_ref, out_ref):
    days, rows = leaf_ref.shape
    owners = back_ref.shape[0]
    height = owners * 16
    slots = jnp.transpose(back_ref[:, 0:16, :].reshape(height, 128).astype(f32)).astype(bf16)
    rest = jnp.transpose(back_ref[:, 16:32, :].reshape(height, 128).astype(f32)).astype(bf16)
    low, high, rest = slots[0:days, :], slots[64:64 + days, :], rest[0:days, :]
    step = min(256, rows)
    for at in range(0, rows, step):
        row = iota((height, step), 0)
        daily = (leaf_ref[:, at:at + step] + shift_ref[0:1, at:at + step]) + shift_ref[1:2, at:at + step]
        place = places_ref[:, at:at + step]
        fine = dot(low, ones_where(row == place[0:1, :])) + dot(high, ones_where(row == place[1:2, :]))
        others = dot(rest, ones_where((row == place[2:3, :]) | (row == place[3:4, :])))
        out_ref[:, at:at + step] = (daily + fine) + others


def exchange(blocks):
    over_y, over_z = lax.axis_size("y"), lax.axis_size("z")
    shape = blocks.shape
    blocks = lax.all_to_all(blocks.reshape((over_y, over_z) + shape[1:]), "y", 0, 0, tiled=True)
    blocks = lax.all_to_all(jnp.swapaxes(blocks, 0, 1), "z", 0, 0, tiled=True)
    return jnp.swapaxes(blocks, 0, 1).reshape(shape)


def per_device(leaf, seas, fine, mid, top, base_fine, base_mid, base_top):
    days, rows = leaf.shape
    owners = lax.axis_size("y") * lax.axis_size("z")
    quarter = (lax.axis_index("tm") // 2).astype(i32).reshape(1)
    base_rest = jnp.concatenate([base_mid, base_top], axis=1).T
    base_rest = jnp.pad(base_rest, ((0, 16 - base_rest.shape[0]), (0, 64 - days)))
    fine, mid, top = (ids.reshape(1, rows) for ids in (fine, mid, top))

    sums = pl.pallas_call(
        day_sum_kernel, out_shape=jax.ShapeDtypeStruct((1, rows), f32), compiler_params=PARAMS, name="day_sums"
    )(leaf)
    parts = lax.all_to_all(jnp.broadcast_to(sums, (lax.axis_size("tm"), rows)), "tm", 0, 0, tiled=True)

    vmem = pl.BlockSpec(memory_space=pltpu.VMEM)
    payload, places, shift = pl.pallas_call(
        send_kernel,
        out_shape=(
            jax.ShapeDtypeStruct((owners, 32, 128), bf16),
            jax.ShapeDtypeStruct((4, rows), i32),
            jax.ShapeDtypeStruct((2, rows), f32),
        ),
        in_specs=[pl.BlockSpec(memory_space=pltpu.SMEM)] + [vmem] * 6,
        scratch_shapes=[pltpu.VMEM((rows, 128), bf16)],
        compiler_params=PARAMS,
        name="pack",
    )(quarter, leaf, seas, parts, fine, mid, top)
    got = exchange(payload)
    back = pl.pallas_call(
        owner_kernel,
        out_shape=jax.ShapeDtypeStruct((owners, 32, 128), bf16),
        compiler_params=PARAMS,
        name="gaps",
    )(got, base_fine, base_rest)
    back = lax.all_to_all(back, ("y", "z"), 0, 0, tiled=True)
    return pl.pallas_call(
        finish_kernel,
        out_shape=jax.ShapeDtypeStruct((days, rows), f32),
        compiler_params=PARAMS,
        name="finish",
    )(leaf, shift, places, back)


def solution(mesh):
    devices = mesh.devices
    side = math.isqrt(devices.shape[1])
    mesh = Mesh(devices.reshape(devices.shape[0], side, side), ("tm", "y", "z"))
    series = ("y", "z")
    return jax.shard_map(
        per_device,
        mesh=mesh,
        in_specs=(
            P("tm", series),
            P(None, series),
            P(series, None),
            P(series, None),
            P(series, None),
            P("tm", series),
            P("tm", series),
            P("tm", series),
        ),
        out_specs=P("tm", series),
        check_vma=False,
    )
```

```python
import jax
import jax.numpy as jnp
from jax import lax
from jax.experimental import pallas as pl
from jax.experimental.pallas import tpu as pltpu
from jax.sharding import PartitionSpec as P

f32 = jnp.float32
bf16 = jnp.bfloat16
i32 = jnp.int32

PARAMS = pltpu.CompilerParams(vmem_limit_bytes=40 * 1024 * 1024)

ID = 48
ONE = 49
MID_COUNT = 122
TOP_COUNT = 126


def iota(shape, dim):
    return lax.broadcasted_iota(i32, shape, dim)


def lane_of(x):
    return jnp.where(x < 15, x + 49, x + 98)


def ones_where(mask):
    return jnp.where(mask, 1.0, 0.0).astype(bf16)


def dot(a, b):
    return jnp.dot(a, b, preferred_element_type=f32)


def slot_lanes(shape, dim):
    return (iota(shape, dim) & 63) <= ID


def corrections(seas, parts, quarter, days):
    per = parts.shape[0] // 4
    season_days = days * per
    own = jnp.sum(jnp.where(iota(parts.shape, 0) // per == quarter, parts, 0.0), axis=0, keepdims=True)
    rows = iota(seas.shape, 0)
    seas_own = jnp.sum(jnp.where(rows == quarter, seas, 0.0), axis=0, keepdims=True)
    seas_four = jnp.sum(jnp.where(rows < 4, seas, 0.0), axis=0, keepdims=True)
    year = 0.5 * jnp.sum(parts, axis=0, keepdims=True) + 0.5 * seas_four
    first = 0.5 * (seas_own - own) / season_days
    second = 0.5 * (seas[4:5, :] - year) / (season_days * 4)
    return first, second


def day_sum_kernel(leaf_ref, out_ref):
    out_ref[...] = jnp.broadcast_to(jnp.sum(leaf_ref[...], axis=0, keepdims=True)[None], out_ref.shape)


def rank_kernel(owners, fine_ref, places_ref):
    rows = fine_ref.shape[1]
    owner = fine_ref[...] >> 6
    step = min(256, rows)
    before = ones_where(iota((step, step), 0) < iota((step, step), 1))
    base = jnp.zeros((owners, 1), f32)
    for at in range(0, rows, step):
        own = owner[:, at:at + step]
        hit = own == iota((owners, step), 0)
        hit_f = jnp.where(hit, 1.0, 0.0)
        seen = dot(hit_f.astype(bf16), before) + base
        rank = jnp.sum(jnp.where(hit, seen, 0.0), axis=0, keepdims=True).astype(i32)
        base = base + jnp.sum(hit_f, axis=1, keepdims=True)
        place = own * 16 + (rank & 15)
        places_ref[0:1, at:at + step] = jnp.where(rank < 16, place, -1)
        places_ref[1:2, at:at + step] = jnp.where(rank < 16, -1, place)


def split_count(sums):
    high = sums.astype(bf16).astype(f32)
    return jnp.where(iota(sums.shape, 1) == 64 + ONE, sums - high, high).astype(bf16)


def send_kernel(quarter_ref, leaf_ref, seas_ref, parts_ref, places_ref, fine_ref, mid_ref, top_ref, pay_ref, shift_ref, wide_ref):
    days, rows = leaf_ref.shape
    owners = pay_ref.shape[0]
    first, second = corrections(seas_ref[...], parts_ref[...], quarter_ref[0], days)
    shift_ref[0:1, :] = first
    shift_ref[1:2, :] = second
    daily = (leaf_ref[...] + first) + second
    local = fine_ref[...] & 63

    rounded = daily.astype(bf16).astype(f32)
    ext = jnp.concatenate([rounded, local.astype(f32), jnp.ones((1, rows), f32), jnp.zeros((14, rows), f32)], axis=0)
    for at in range(0, rows, 128):
        turned = jnp.transpose(ext[:, at:at + 128])
        wide_ref[at:at + 128, :] = jnp.concatenate([turned, turned], axis=1).astype(bf16)
    wide = wide_ref[...]

    place_low, place_high = places_ref[0:1, :], places_ref[1:2, :]
    mid = mid_ref[...]
    square = (128, 128)
    source, lane = iota(square, 0), iota(square, 1)
    mid_even = ones_where(((source < 24) & (lane == lane_of(source))) | ((source == ONE) & (lane == MID_COUNT)))
    mid_odd = ones_where(
        ((source >= 88) & (source < 112) & (lane == lane_of(source - 88))) | ((source == 64 + ONE) & (lane == MID_COUNT))
    )
    third = source // 3
    top_move = ones_where(
        ((source < 48) & (lane == lane_of(25 + source - 3 * third)))
        | (((source == ONE) | (source == 64 + ONE)) & (lane == TOP_COUNT))
    )
    weave = ones_where(lane == (source >> 1) + 64 * (source & 1))
    row_in = source & 15
    keep_top = (
        ((lane < 48) & (lane // 3 == row_in))
        | ((lane == ONE) & ((source & 1) == 0))
        | ((lane == 64 + ONE) & ((source & 1) == 1))
    )

    tops = split_count(dot(ones_where(iota((owners, rows), 0) == top_ref[...]), wide))
    group = min(8, owners)
    chunk = group * 16
    low_half = iota((chunk, 128), 1) < 64
    for g in range(owners // group):
        row = iota((chunk, rows), 0) + g * chunk
        slots = jnp.where(
            low_half,
            dot(ones_where(row == place_low), wide),
            dot(ones_where(row == place_high), wide),
        )
        mid_row = iota((group * 8, rows), 0) + g * (group * 8)
        mids = split_count(dot(ones_where(mid_row == mid), wide))
        mids = jnp.concatenate([dot(mids, mid_even), dot(mids, mid_odd)], axis=0).astype(bf16)
        own = ones_where(iota((chunk, owners), 1) == (iota((chunk, owners), 0) >> 4) + g * group)
        top = jnp.where(keep_top, dot(own, tops), 0.0).astype(bf16)
        rest = dot(weave, mids) + dot(top, top_move)
        tile = jnp.where(slot_lanes(square, 1), slots, rest).astype(bf16)
        pay_ref[pl.ds(g * group, group), :, :] = tile.reshape(group, 16, 128)


def owner_kernel(got_ref, base_fine_ref, base_rest_ref, back_ref):
    owners = got_ref.shape[0]
    days, nodes = base_fine_ref.shape
    got = got_ref[...].astype(f32)
    flat = got.reshape(owners * 16, 128)
    lanes = iota(flat.shape, 1)
    node = iota((owners * 16, nodes), 1).astype(f32)
    pick_low = ones_where(flat[:, ID:ID + 1] == node)
    pick_high = ones_where(flat[:, 64 + ID:65 + ID] == node)
    turned = jnp.transpose(jnp.where((lanes & 63) == ONE, 1.0, flat)).astype(bf16)
    totals = dot(turned[0:64, :], pick_low) + dot(turned[64:128, :], pick_high)
    gap = (base_fine_ref[...] - totals[0:days, :]) / (totals[ONE:ONE + 1, :] + 1.0)
    gap = jnp.concatenate([gap, jnp.zeros((64 - days, nodes), f32)], axis=0)
    gap = jnp.transpose(jnp.concatenate([gap, gap], axis=0)).astype(bf16)
    spread = jnp.where(lanes < 64, dot(pick_low, gap), dot(pick_high, gap))

    rest = jnp.sum(got, axis=0)
    up = jnp.concatenate([rest[1:16, :], rest[0:1, :]], axis=0)
    down = jnp.concatenate([rest[15:16, :], rest[0:15, :]], axis=0)
    pair = rest + jnp.where((iota(rest.shape, 0) & 1) == 0, up, down)
    top_lane = iota(rest.shape, 1) > MID_COUNT
    count = jnp.where(top_lane, pair[:, TOP_COUNT:TOP_COUNT + 1], pair[:, MID_COUNT:MID_COUNT + 1])
    gap_rest = jnp.where(slot_lanes(rest.shape, 1), 0.0, (base_rest_ref[...] - rest) / (count + 1.0))
    spread = jnp.where(slot_lanes(flat.shape, 1), spread, 0.0).reshape(owners, 16, 128)
    back_ref[...] = (spread + gap_rest[None]).astype(bf16)


def finish_kernel(leaf_ref, shift_ref, places_ref, mid_ref, top_ref, back_ref, out_ref):
    days, rows = leaf_ref.shape
    owners = back_ref.shape[0]
    height = owners * 16
    turned = jnp.transpose(back_ref[...].astype(f32).reshape(height, 128)).astype(bf16)
    day, lane = iota((days, 128), 0), iota((days, 128), 1)
    from_even = dot(ones_where((day < 24) & (lane == lane_of(day))), turned)
    from_odd = dot(ones_where((day >= 24) & (lane == lane_of(day - 24))), turned)
    column = iota((days, height), 1)
    mids = jnp.where((column & 1) == 0, from_even, from_odd).astype(bf16)
    chunk = min(128, height)
    pair = ones_where(iota((chunk, chunk // 2), 0) >> 1 == iota((chunk, chunk // 2), 1))
    mids = [dot(mids[:, at:at + chunk], pair) for at in range(0, height, chunk)]
    third = day // 3
    tops = dot(ones_where(lane == lane_of(25 + day - 3 * third)), turned)
    tops = jnp.where(iota((days, height), 0) // 3 == (column & 15), tops, 0.0).astype(bf16)
    tops = dot(tops, ones_where(iota((height, owners), 0) >> 4 == iota((height, owners), 1)))
    low, high = turned[0:days, :], turned[64:64 + days, :]
    mids = jnp.concatenate(mids, axis=1).astype(bf16)
    tops = tops.astype(bf16)
    step = min(256, rows)
    for at in range(0, rows, step):
        row = iota((height, step), 0)
        mid_row = iota((owners * 8, step), 0)
        top_row = iota((owners, step), 0)
        daily = (leaf_ref[:, at:at + step] + shift_ref[0:1, at:at + step]) + shift_ref[1:2, at:at + step]
        place = places_ref[:, at:at + step]
        fine = dot(low, ones_where(row == place[0:1, :])) + dot(high, ones_where(row == place[1:2, :]))
        mid = dot(mids, ones_where(mid_row == mid_ref[:, at:at + step]))
        top = dot(tops, ones_where(top_row == top_ref[:, at:at + step]))
        out_ref[:, at:at + step] = ((daily + fine) + mid) + top


def per_device(leaf, seas, fine, mid, top, base_fine, base_mid, base_top):
    days, rows = leaf.shape
    owners = lax.axis_size("series")
    blocks = lax.axis_size("tm")
    quarter = (lax.axis_index("tm") // (blocks // 4)).astype(i32).reshape(1)
    fine, mid, top = (ids.reshape(1, rows) for ids in (fine, mid, top))
    base_mids = base_mid.T.reshape(16, 24)
    base_rest = jnp.concatenate([base_mids, jnp.zeros((16, 1), f32), base_top.reshape(16, 3), jnp.zeros((16, 2), f32)], axis=1)
    gap = jnp.zeros((16, 49), f32)
    base_rest = jnp.concatenate([gap, base_rest[:, :15], gap, base_rest[:, 15:]], axis=1)

    sums = pl.pallas_call(
        day_sum_kernel, out_shape=jax.ShapeDtypeStruct((blocks, 1, rows), f32), compiler_params=PARAMS, name="day_sums"
    )(leaf)
    parts = lax.all_to_all(sums, "tm", 0, 0, tiled=True).reshape(blocks, rows)
    places = pl.pallas_call(
        lambda *refs: rank_kernel(owners, *refs),
        out_shape=jax.ShapeDtypeStruct((2, rows), i32),
        compiler_params=PARAMS,
        cost_estimate=pl.CostEstimate(flops=2 * owners * rows * 256, bytes_accessed=12 * rows, transcendentals=0),
        name="ranks",
    )(fine)

    vmem = pl.BlockSpec(memory_space=pltpu.VMEM)
    payload, shift = pl.pallas_call(
        send_kernel,
        out_shape=(jax.ShapeDtypeStruct((owners, 16, 128), bf16), jax.ShapeDtypeStruct((2, rows), f32)),
        in_specs=[pl.BlockSpec(memory_space=pltpu.SMEM)] + [vmem] * 7,
        scratch_shapes=[pltpu.VMEM((rows, 128), bf16)],
        compiler_params=PARAMS,
        name="pack",
    )(quarter, leaf, seas, parts, places, fine, mid, top)
    got = lax.all_to_all(payload, "series", 0, 0, tiled=True)
    back = pl.pallas_call(
        owner_kernel,
        out_shape=jax.ShapeDtypeStruct((owners, 16, 128), bf16),
        compiler_params=PARAMS,
        name="gaps",
    )(got, base_fine, base_rest)
    back = lax.all_to_all(back, "series", 0, 0, tiled=True)
    return pl.pallas_call(
        finish_kernel,
        out_shape=jax.ShapeDtypeStruct((days, rows), f32),
        compiler_params=PARAMS,
        name="finish",
    )(leaf, shift, places, mid, top, back)


def solution(mesh):
    return jax.shard_map(
        per_device,
        mesh=mesh,
        in_specs=(
            P("tm", "series"),
            P(None, "series"),
            P("series", None),
            P("series", None),
            P("series", None),
            P("tm", "series"),
            P("tm", "series"),
            P("tm", "series"),
        ),
        out_specs=P("tm", "series"),
        check_vma=False,
    )
```

```python
import jax
import jax.numpy as jnp
from jax import lax
from jax.experimental import pallas as pl
from jax.experimental.pallas import tpu as pltpu
from jax.sharding import PartitionSpec as P

f32 = jnp.float32
bf16 = jnp.bfloat16
i32 = jnp.int32

PARAMS = pltpu.CompilerParams(vmem_limit_bytes=40 * 1024 * 1024)

ID = 48
ONE = 49
MID_COUNT = 122
TOP_COUNT = 126


def iota(shape, dim):
    return lax.broadcasted_iota(i32, shape, dim)


def lane_of(x):
    return jnp.where(x < 15, x + 49, x + 98)


def ones_where(mask):
    return jnp.where(mask, 1.0, 0.0).astype(bf16)


def dot(a, b):
    return jnp.dot(a, b, preferred_element_type=f32)


def slot_lanes(shape, dim):
    return (iota(shape, dim) & 63) <= ID


def corrections(seas, parts, block, days):
    blocks = parts.shape[0]
    per = blocks // 4
    season_days = days * per
    quarter = block // per
    row = block - iota(parts.shape, 0)
    row = jnp.where(row < 0, row + blocks, row)
    own = jnp.sum(jnp.where(row // per == quarter, parts, 0.0), axis=0, keepdims=True)
    rows = iota(seas.shape, 0)
    seas_own = jnp.sum(jnp.where(rows == quarter, seas, 0.0), axis=0, keepdims=True)
    seas_four = jnp.sum(jnp.where(rows < 4, seas, 0.0), axis=0, keepdims=True)
    year = 0.5 * jnp.sum(parts, axis=0, keepdims=True) + 0.5 * seas_four
    first = 0.5 * (seas_own - own) / season_days
    second = 0.5 * (seas[4:5, :] - year) / (season_days * 4)
    return first, second


def day_sum_kernel(leaf_ref, out_ref):
    out_ref[...] = jnp.sum(leaf_ref[...], axis=0, keepdims=True)


def rank_kernel(owners, fine_ref, places_ref):
    rows = fine_ref.shape[1]
    owner = fine_ref[...] >> 6
    step = min(256, rows)
    before = ones_where(iota((step, step), 0) < iota((step, step), 1))
    base = jnp.zeros((owners, 1), f32)
    for at in range(0, rows, step):
        own = owner[:, at:at + step]
        hit = own == iota((owners, step), 0)
        hit_f = jnp.where(hit, 1.0, 0.0)
        seen = dot(hit_f.astype(bf16), before) + base
        rank = jnp.sum(jnp.where(hit, seen, 0.0), axis=0, keepdims=True).astype(i32)
        base = base + jnp.sum(hit_f, axis=1, keepdims=True)
        place = own * 16 + (rank & 15)
        places_ref[0:1, at:at + step] = jnp.where(rank < 16, place, -1)
        places_ref[1:2, at:at + step] = jnp.where(rank < 16, -1, place)


def split_count(sums):
    high = sums.astype(bf16).astype(f32)
    return jnp.where(iota(sums.shape, 1) == 64 + ONE, sums - high, high).astype(bf16)


def send_kernel(block_ref, leaf_ref, seas_ref, places_ref, fine_ref, mid_ref, top_ref, rest_ref, *refs):
    *part_refs, pay_ref, shift_ref, rest_out_ref, wide_ref = refs
    days, rows = leaf_ref.shape
    owners = pay_ref.shape[0]
    parts = jnp.concatenate([ref[...] for ref in part_refs], axis=0)
    first, second = corrections(seas_ref[...], parts, block_ref[0], days)
    rest_out_ref[...] = rest_ref[...]
    shift_ref[0:1, :] = first
    shift_ref[1:2, :] = second
    daily = (leaf_ref[...] + first) + second
    local = fine_ref[...] & 63

    rounded = daily.astype(bf16).astype(f32)
    ext = jnp.concatenate([rounded, local.astype(f32), jnp.ones((1, rows), f32), jnp.zeros((14, rows), f32)], axis=0)
    for at in range(0, rows, 128):
        turned = jnp.transpose(ext[:, at:at + 128])
        wide_ref[at:at + 128, :] = jnp.concatenate([turned, turned], axis=1).astype(bf16)
    wide = wide_ref[...]

    place_low, place_high = places_ref[0:1, :], places_ref[1:2, :]
    mid = mid_ref[...]
    square = (128, 128)
    source, lane = iota(square, 0), iota(square, 1)
    mid_even = ones_where(((source < 24) & (lane == lane_of(source))) | ((source == ONE) & (lane == MID_COUNT)))
    mid_odd = ones_where(
        ((source >= 88) & (source < 112) & (lane == lane_of(source - 88))) | ((source == 64 + ONE) & (lane == MID_COUNT))
    )
    third = source // 3
    top_move = ones_where(
        ((source < 48) & (lane == lane_of(25 + source - 3 * third)))
        | (((source == ONE) | (source == 64 + ONE)) & (lane == TOP_COUNT))
    )
    weave = ones_where(lane == (source >> 1) + 64 * (source & 1))
    row_in = source & 15
    keep_top = (
        ((lane < 48) & (lane // 3 == row_in))
        | ((lane == ONE) & ((source & 1) == 0))
        | ((lane == 64 + ONE) & ((source & 1) == 1))
    )

    tops = split_count(dot(ones_where(iota((owners, rows), 0) == top_ref[...]), wide))
    group = min(8, owners)
    chunk = group * 16
    low_half = iota((chunk, 128), 1) < 64
    for g in range(owners // group):
        row = iota((chunk, rows), 0) + g * chunk
        slots = jnp.where(
            low_half,
            dot(ones_where(row == place_low), wide),
            dot(ones_where(row == place_high), wide),
        )
        mid_row = iota((group * 8, rows), 0) + g * (group * 8)
        mids = split_count(dot(ones_where(mid_row == mid), wide))
        mids = jnp.concatenate([dot(mids, mid_even), dot(mids, mid_odd)], axis=0).astype(bf16)
        own = ones_where(iota((chunk, owners), 1) == (iota((chunk, owners), 0) >> 4) + g * group)
        top = jnp.where(keep_top, dot(own, tops), 0.0).astype(bf16)
        rest = dot(weave, mids) + dot(top, top_move)
        tile = jnp.where(slot_lanes(square, 1), slots, rest).astype(bf16)
        pay_ref[pl.ds(g * group, group), :, :] = tile.reshape(group, 16, 128)


def owner_kernel(got_ref, base_fine_ref, base_rest_ref, back_ref):
    owners = got_ref.shape[0]
    days, nodes = base_fine_ref.shape
    got = got_ref[...].astype(f32)
    flat = got.reshape(owners * 16, 128)
    lanes = iota(flat.shape, 1)
    node = iota((owners * 16, nodes), 1).astype(f32)
    pick_low = ones_where(flat[:, ID:ID + 1] == node)
    pick_high = ones_where(flat[:, 64 + ID:65 + ID] == node)
    turned = jnp.transpose(jnp.where((lanes & 63) == ONE, 1.0, flat)).astype(bf16)
    totals = dot(turned[0:64, :], pick_low) + dot(turned[64:128, :], pick_high)
    gap = (base_fine_ref[...] - totals[0:days, :]) / (totals[ONE:ONE + 1, :] + 1.0)
    gap = jnp.concatenate([gap, jnp.zeros((64 - days, nodes), f32)], axis=0)
    gap = jnp.transpose(jnp.concatenate([gap, gap], axis=0)).astype(bf16)
    spread = jnp.where(lanes < 64, dot(pick_low, gap), dot(pick_high, gap))

    rest = jnp.sum(got, axis=0)
    up = jnp.concatenate([rest[1:16, :], rest[0:1, :]], axis=0)
    down = jnp.concatenate([rest[15:16, :], rest[0:15, :]], axis=0)
    pair = rest + jnp.where((iota(rest.shape, 0) & 1) == 0, up, down)
    top_lane = iota(rest.shape, 1) > MID_COUNT
    count = jnp.where(top_lane, pair[:, TOP_COUNT:TOP_COUNT + 1], pair[:, MID_COUNT:MID_COUNT + 1])
    gap_rest = jnp.where(slot_lanes(rest.shape, 1), 0.0, (base_rest_ref[...] - rest) / (count + 1.0))
    spread = jnp.where(slot_lanes(flat.shape, 1), spread, 0.0).reshape(owners, 16, 128)
    back_ref[...] = (spread + gap_rest[None]).astype(bf16)


def finish_kernel(leaf_ref, shift_ref, places_ref, mid_ref, top_ref, back_ref, out_ref):
    days, rows = leaf_ref.shape
    owners = back_ref.shape[0]
    height = owners * 16
    turned = jnp.transpose(back_ref[...].astype(f32).reshape(height, 128)).astype(bf16)
    day, lane = iota((days, 128), 0), iota((days, 128), 1)
    from_even = dot(ones_where((day < 24) & (lane == lane_of(day))), turned)
    from_odd = dot(ones_where((day >= 24) & (lane == lane_of(day - 24))), turned)
    column = iota((days, height), 1)
    mids = jnp.where((column & 1) == 0, from_even, from_odd).astype(bf16)
    chunk = min(128, height)
    pair = ones_where(iota((chunk, chunk // 2), 0) >> 1 == iota((chunk, chunk // 2), 1))
    mids = [dot(mids[:, at:at + chunk], pair) for at in range(0, height, chunk)]
    third = day // 3
    tops = dot(ones_where(lane == lane_of(25 + day - 3 * third)), turned)
    tops = jnp.where(iota((days, height), 0) // 3 == (column & 15), tops, 0.0).astype(bf16)
    tops = dot(tops, ones_where(iota((height, owners), 0) >> 4 == iota((height, owners), 1)))
    low, high = turned[0:days, :], turned[64:64 + days, :]
    mids = jnp.concatenate(mids, axis=1).astype(bf16)
    tops = tops.astype(bf16)
    step = min(256, rows)
    for at in range(0, rows, step):
        row = iota((height, step), 0)
        mid_row = iota((owners * 8, step), 0)
        top_row = iota((owners, step), 0)
        daily = (leaf_ref[:, at:at + step] + shift_ref[0:1, at:at + step]) + shift_ref[1:2, at:at + step]
        place = places_ref[:, at:at + step]
        fine = dot(low, ones_where(row == place[0:1, :])) + dot(high, ones_where(row == place[1:2, :]))
        mid = dot(mids, ones_where(mid_row == mid_ref[:, at:at + step]))
        top = dot(tops, ones_where(top_row == top_ref[:, at:at + step]))
        out_ref[:, at:at + step] = ((daily + fine) + mid) + top


def per_device(leaf, seas, fine, mid, top, base_fine, base_mid, base_top):
    days, rows = leaf.shape
    owners = lax.axis_size("series")
    blocks = lax.axis_size("tm")
    block = lax.axis_index("tm").astype(i32).reshape(1)
    fine, mid, top = (ids.reshape(1, rows) for ids in (fine, mid, top))
    base_mids = base_mid.T.reshape(16, 24)
    base_rest = jnp.concatenate([base_mids, jnp.zeros((16, 1), f32), base_top.reshape(16, 3), jnp.zeros((16, 2), f32)], axis=1)
    gap = jnp.zeros((16, 49), f32)
    base_rest = jnp.concatenate([gap, base_rest[:, :15], gap, base_rest[:, 15:]], axis=1)

    sums = pl.pallas_call(
        day_sum_kernel, out_shape=jax.ShapeDtypeStruct((1, rows), f32), compiler_params=PARAMS, name="day_sums"
    )(leaf)
    parts = [sums] + [
        lax.ppermute(sums, "tm", [(at, (at + hop) % blocks) for at in range(blocks)]) for hop in range(1, blocks)
    ]
    places = pl.pallas_call(
        lambda *refs: rank_kernel(owners, *refs),
        out_shape=jax.ShapeDtypeStruct((2, rows), i32),
        compiler_params=PARAMS,
        cost_estimate=pl.CostEstimate(flops=2 * owners * rows * 256, bytes_accessed=12 * rows, transcendentals=0),
        name="ranks",
    )(fine)

    vmem = pl.BlockSpec(memory_space=pltpu.VMEM)
    payload, shift, base_rest = pl.pallas_call(
        send_kernel,
        out_shape=(jax.ShapeDtypeStruct((owners, 16, 128), bf16), jax.ShapeDtypeStruct((2, rows), f32), jax.ShapeDtypeStruct((16, 128), f32)),
        in_specs=[pl.BlockSpec(memory_space=pltpu.SMEM)] + [vmem] * (7 + blocks),
        scratch_shapes=[pltpu.VMEM((rows, 128), bf16)],
        compiler_params=PARAMS,
        name="pack",
    )(block, leaf, seas, places, fine, mid, top, base_rest, *parts)
    got = lax.all_to_all(payload, "series", 0, 0, tiled=True)
    back = pl.pallas_call(
        owner_kernel,
        out_shape=jax.ShapeDtypeStruct((owners, 16, 128), bf16),
        compiler_params=PARAMS,
        name="gaps",
    )(got, base_fine, base_rest)
    back = lax.all_to_all(back, "series", 0, 0, tiled=True)
    return pl.pallas_call(
        finish_kernel,
        out_shape=jax.ShapeDtypeStruct((days, rows), f32),
        compiler_params=PARAMS,
        name="finish",
    )(leaf, shift, places, mid, top, back)


def solution(mesh):
    return jax.shard_map(
        per_device,
        mesh=mesh,
        in_specs=(
            P("tm", "series"),
            P(None, "series"),
            P("series", None),
            P("series", None),
            P("series", None),
            P("tm", "series"),
            P("tm", "series"),
            P("tm", "series"),
        ),
        out_specs=P("tm", "series"),
        check_vma=False,
    )
```

```python
import jax
import jax.numpy as jnp
from jax import lax
from jax.experimental import pallas as pl
from jax.experimental.pallas import tpu as pltpu
from jax.sharding import PartitionSpec as P

f32 = jnp.float32
bf16 = jnp.bfloat16
i32 = jnp.int32

PARAMS = pltpu.CompilerParams(vmem_limit_bytes=28 * 1024 * 1024)

ID = 48
ONE = 49
LOW = 50
MID_COUNT = 122
TOP_COUNT = 126
TOP_ROWS = 128


def iota(shape, dim):
    return lax.broadcasted_iota(i32, shape, dim)


def lane_of(x):
    return jnp.where(x < 15, x + 49, x + 98)


def top_lane(day):
    return lane_of(25 + day - 3 * (day // 3))


def ones_where(mask):
    return jnp.where(mask, 1.0, 0.0).astype(bf16)


def dot(a, b):
    return jnp.dot(a, b, preferred_element_type=f32)


def dot_nt(a, b, precision=None):
    return lax.dot_general(a, b, (((1,), (1,)), ((), ())), precision=precision, preferred_element_type=f32)


def slot_lanes(shape, dim):
    return (iota(shape, dim) & 63) <= ID


def row_of(dense):
    return jnp.concatenate([dense[at:at + 1, :] for at in range(dense.shape[0])], axis=1)


def corrections(seas, parts, quarter, days):
    per = parts.shape[0] // 4
    season_days = days * per
    own = row_of(jnp.sum(jnp.where(iota(parts.shape, 0) // per == quarter, parts, 0.0), axis=0))
    rows = iota(seas.shape, 0)
    seas_own = jnp.sum(jnp.where(rows == quarter, seas, 0.0), axis=0, keepdims=True)
    seas_four = jnp.sum(jnp.where(rows < 4, seas, 0.0), axis=0, keepdims=True)
    year = 0.5 * row_of(jnp.sum(parts, axis=0)) + 0.5 * seas_four
    first = 0.5 * (seas_own - own) / season_days
    second = 0.5 * (seas[4:5, :] - year) / (season_days * 4)
    return first, second


def day_sum_kernel(leaf_ref, out_ref):
    sums = jnp.sum(leaf_ref[...], axis=0, keepdims=True)
    dense = jnp.concatenate([sums[:, at:at + 128] for at in range(0, sums.shape[1], 128)], axis=0)
    out_ref[...] = jnp.broadcast_to(dense[None], out_ref.shape)


def tables_kernel(owners, fine_ref, mid_ref, top_ref, base_mid_ref, base_top_ref, hits_ref, base_ref):
    rows = fine_ref.shape[1]
    owner = fine_ref[...] >> 6
    step = min(256, rows)
    before = ones_where(iota((step, step), 0) < iota((step, step), 1))
    base = jnp.zeros((owners, 1), f32)
    ranks = []
    for at in range(0, rows, step):
        hit = owner[:, at:at + step] == iota((owners, step), 0)
        hit_f = jnp.where(hit, 1.0, 0.0)
        seen = dot(hit_f.astype(bf16), before) + base
        ranks.append(jnp.sum(jnp.where(hit, seen, 0.0), axis=0, keepdims=True))
        base = base + jnp.sum(hit_f, axis=1, keepdims=True)
    rank = jnp.concatenate(ranks, axis=1).astype(i32)
    place = owner * 16 + (rank & 15)
    place_low = jnp.where(rank < 16, place, -1)
    place_high = jnp.where(rank < 16, -1, place)
    at = 0
    for place, height in ((place_low, owners * 16), (place_high, owners * 16), (mid_ref[...], owners * 8), (top_ref[...], TOP_ROWS)):
        chunk = min(64, height)
        for start in range(0, height, chunk):
            hits_ref[at:at + chunk, :] = ones_where(iota((chunk, rows), 0) + start == place)
            at += chunk

    days = base_mid_ref.shape[1]
    half = days // 2
    day, lane = iota((days, 128), 0), iota((days, 128), 1)
    moves = (
        (day < half) & (lane == lane_of(day)),
        (day >= half) & (lane == lane_of(day - half)),
        lane == top_lane(day),
    )
    moves = [jnp.where(move, 1.0, 0.0) for move in moves]
    top = jnp.where(iota((16, days), 1) // 3 == iota((16, days), 0), base_top_ref[...], 0.0)
    exact = lax.Precision.HIGHEST
    mids = [jnp.dot(base_mid_ref[...], move, precision=exact, preferred_element_type=f32) for move in moves[:2]]
    base_ref[...] = jnp.concatenate(mids, axis=0) + jnp.dot(top, moves[2], precision=exact, preferred_element_type=f32)


def split_count(sums):
    high = sums.astype(bf16).astype(f32)
    return jnp.where(iota(sums.shape, 0) == LOW, sums - high, high)


def send_kernel(quarter_ref, leaf_ref, seas_ref, parts_ref, fine_ref, hits_ref, pay_ref, shift_ref):
    days, rows = leaf_ref.shape
    owners = pay_ref.shape[0]
    slots, mids = owners * 16, owners * 8
    first, second = corrections(seas_ref[...], parts_ref[...], quarter_ref[0], days)
    shift_ref[0:1, :] = first
    shift_ref[1:2, :] = second
    daily = (leaf_ref[...] + first) + second
    local = fine_ref[...] & 63
    ext = jnp.concatenate([daily, local.astype(f32), jnp.ones((2, rows), f32), jnp.zeros((13, rows), f32)], axis=0)
    sums = dot_nt(ext.astype(bf16), hits_ref[...])

    tops = split_count(sums[:, 2 * slots + mids:]).astype(bf16)
    tops = dot(tops, ones_where(iota((TOP_ROWS, slots), 0) == iota((TOP_ROWS, slots), 1) >> 4))
    row, column = iota((64, slots), 0), iota((64, slots), 1) & 15
    keep = (
        ((row < days) & (row // 3 == column))
        | ((row == ONE) & (column < 8))
        | ((row == LOW) & (column >= 8))
    )
    tops = jnp.where(keep, tops, 0.0).astype(bf16)
    lane, day = iota((128, 64), 0), iota((128, 64), 1)
    top_move = ((day < days) & (lane == top_lane(day))) | (((day == ONE) | (day == LOW)) & (lane == TOP_COUNT))
    tops = dot(ones_where(top_move), tops)
    tiles = jnp.concatenate([sums[:, :slots], sums[:, slots:2 * slots]], axis=0)
    tiles = jnp.where(slot_lanes((128, slots), 0), tiles, tops)

    half = days // 2
    mid_sums = split_count(sums[:, 2 * slots:2 * slots + mids])
    day, lane = iota((64, 128), 0), iota((64, 128), 1)
    moves = (
        ((day < half) & (lane == lane_of(day))) | ((day == ONE) & (lane == MID_COUNT)),
        ((day >= half) & (day < days) & (lane == lane_of(day - half))) | ((day == LOW) & (lane == MID_COUNT)),
    )
    moves = [ones_where(move) for move in moves]
    group = min(16, owners)
    for g in range(owners // group):
        own = jnp.transpose(mid_sums[:, g * group * 8:(g + 1) * group * 8]).astype(bf16)
        extra = jnp.concatenate([dot(own, move).reshape(group, 8, 128) for move in moves], axis=1)
        start, stop = g * group * 16, (g + 1) * group * 16
        tile = jnp.concatenate([jnp.transpose(tiles[:, at:at + 128]) for at in range(start, stop, 128)], axis=0)
        pay_ref[g * group:(g + 1) * group, :, :] = (tile.reshape(group, 16, 128) + extra).astype(bf16)


def owner_kernel(got_ref, base_fine_ref, base_rest_ref, back_ref):
    owners = got_ref.shape[0]
    days, nodes = base_fine_ref.shape
    got = got_ref[...].astype(f32)
    flat = got.reshape(owners * 16, 128)
    lanes = iota(flat.shape, 1)
    node = iota((owners * 16, nodes), 1).astype(f32)
    pick_low = ones_where(flat[:, ID:ID + 1] == node)
    pick_high = ones_where(flat[:, 64 + ID:65 + ID] == node)
    turned = jnp.transpose(jnp.where((lanes & 63) == ONE, 1.0, flat)).astype(bf16)
    totals = dot(turned[0:64, :], pick_low) + dot(turned[64:128, :], pick_high)
    gap = (base_fine_ref[...] - totals[0:days, :]) / (totals[ONE:ONE + 1, :] + 1.0)
    gap = jnp.concatenate([gap, jnp.zeros((64 - days, nodes), f32)], axis=0)
    gap = jnp.transpose(jnp.concatenate([gap, gap], axis=0)).astype(bf16)
    spread = jnp.where(lanes < 64, dot(pick_low, gap), dot(pick_high, gap))

    rest = jnp.sum(got, axis=0)
    pair = rest + jnp.concatenate([rest[8:16, :], rest[0:8, :]], axis=0)
    of_top = iota(rest.shape, 1) > MID_COUNT
    count = jnp.where(of_top, pair[:, TOP_COUNT:TOP_COUNT + 1], pair[:, MID_COUNT:MID_COUNT + 1])
    gap_rest = jnp.where(slot_lanes(rest.shape, 1), 0.0, (base_rest_ref[...] - rest) / (count + 1.0))
    spread = jnp.where(slot_lanes(flat.shape, 1), spread, 0.0).reshape(owners, 16, 128)
    back_ref[...] = (spread + gap_rest[None]).astype(bf16)


def finish_kernel(leaf_ref, shift_ref, hits_ref, back_ref, out_ref):
    days, rows = leaf_ref.shape
    owners = back_ref.shape[0]
    slots, mids = owners * 16, owners * 8
    half = days // 2
    back = back_ref[...].astype(f32)
    day, lane = iota((days, 128), 0), iota((days, 128), 1)
    take = jnp.concatenate([ones_where(lane == day), ones_where(lane == day + 64), ones_where(lane == top_lane(day))], axis=0)
    taken = dot_nt(take, back.reshape(slots, 128).astype(bf16))
    tops = jnp.where(iota((days, slots), 0) // 3 == (iota((days, slots), 1) & 15), taken[2 * days:, :], 0.0).astype(bf16)
    tops = dot(tops, ones_where(iota((slots, TOP_ROWS), 0) >> 4 == iota((slots, TOP_ROWS), 1)))
    first, last = (back[:, at:at + 8, :].reshape(mids, 128).astype(bf16) for at in (0, 8))
    mid = dot_nt(ones_where((day < half) & (lane == lane_of(day))), first)
    mid = mid + dot_nt(ones_where((day >= half) & (lane == lane_of(day - half))), last)
    gaps = jnp.concatenate([taken[:days, :], taken[days:2 * days, :], mid, tops], axis=1).astype(bf16)
    step = min(256, rows)
    for at in range(0, rows, step):
        daily = (leaf_ref[:, at:at + step] + shift_ref[0:1, at:at + step]) + shift_ref[1:2, at:at + step]
        out_ref[:, at:at + step] = daily + dot(gaps, hits_ref[:, at:at + step])


def per_device(leaf, seas, fine, mid, top, base_fine, base_mid, base_top):
    days, rows = leaf.shape
    owners = lax.axis_size("series")
    blocks = lax.axis_size("tm")
    quarter = (lax.axis_index("tm") // (blocks // 4)).astype(i32).reshape(1)
    fine, mid, top = (ids.reshape(1, rows) for ids in (fine, mid, top))
    height = owners * 40 + TOP_ROWS

    sums = pl.pallas_call(
        day_sum_kernel,
        out_shape=jax.ShapeDtypeStruct((blocks, rows // 128, 128), f32),
        compiler_params=PARAMS,
        name="day_sums",
    )(leaf)
    parts = lax.all_to_all(sums, "tm", 0, 0, tiled=True)
    hits, base_rest = pl.pallas_call(
        lambda *refs: tables_kernel(owners, *refs),
        out_shape=(jax.ShapeDtypeStruct((height, rows), bf16), jax.ShapeDtypeStruct((16, 128), f32)),
        compiler_params=PARAMS,
        cost_estimate=pl.CostEstimate(flops=2 * owners * rows * 256, bytes_accessed=2 * height * rows, transcendentals=0),
        name="tables",
    )(fine, mid, top, base_mid.T, base_top.reshape(1, days))

    vmem = pl.BlockSpec(memory_space=pltpu.VMEM)
    payload, shift = pl.pallas_call(
        send_kernel,
        out_shape=(jax.ShapeDtypeStruct((owners, 16, 128), bf16), jax.ShapeDtypeStruct((2, rows), f32)),
        in_specs=[pl.BlockSpec(memory_space=pltpu.SMEM)] + [vmem] * 5,
        compiler_params=PARAMS,
        name="pack",
    )(quarter, leaf, seas, parts, fine, hits)
    got = lax.all_to_all(payload, "series", 0, 0, tiled=True)
    back = pl.pallas_call(
        owner_kernel,
        out_shape=jax.ShapeDtypeStruct((owners, 16, 128), bf16),
        compiler_params=PARAMS,
        name="gaps",
    )(got, base_fine, base_rest)
    back = lax.all_to_all(back, "series", 0, 0, tiled=True)
    return pl.pallas_call(
        finish_kernel,
        out_shape=jax.ShapeDtypeStruct((days, rows), f32),
        compiler_params=PARAMS,
        name="finish",
    )(leaf, shift, hits, back)


def solution(mesh):
    return jax.shard_map(
        per_device,
        mesh=mesh,
        in_specs=(
            P("tm", "series"),
            P(None, "series"),
            P("series", None),
            P("series", None),
            P("series", None),
            P("tm", "series"),
            P("tm", "series"),
            P("tm", "series"),
        ),
        out_specs=P("tm", "series"),
        check_vma=False,
    )
```

```python
import jax
import jax.numpy as jnp
from jax import lax
from jax.experimental import pallas as pl
from jax.experimental.pallas import tpu as pltpu
from jax.sharding import PartitionSpec as P

f32 = jnp.float32
bf16 = jnp.bfloat16
i32 = jnp.int32

PARAMS = pltpu.CompilerParams(vmem_limit_bytes=24 * 1024 * 1024)

ID = 48
ONE = 49
LOW = 50
MID_COUNT = 122
TOP_COUNT = 126
TOP_ROWS = 128


def iota(shape, dim):
    return lax.broadcasted_iota(i32, shape, dim)


def lane_of(x):
    return jnp.where(x < 15, x + 49, x + 98)


def top_lane(day):
    return lane_of(25 + day - 3 * (day // 3))


def ones_where(mask):
    return jnp.where(mask, 1.0, 0.0).astype(bf16)


def dot(a, b):
    return jnp.dot(a, b, preferred_element_type=f32)


def dot_nt(a, b, precision=None):
    return lax.dot_general(a, b, (((1,), (1,)), ((), ())), precision=precision, preferred_element_type=f32)


def slot_lanes(shape, dim):
    return (iota(shape, dim) & 63) <= ID


def row_of(dense):
    return jnp.concatenate([dense[at:at + 1, :] for at in range(dense.shape[0])], axis=1)


def dense_of(row):
    return jnp.concatenate([row[:, at:at + 128] for at in range(0, row.shape[1], 128)], axis=0)


def start_kernel(*refs):
    count = (len(refs) - 2) // 2
    sources, places, sums_ref, sems = refs[:count], refs[count:2 * count], refs[-2], refs[-1]
    copies = [pltpu.make_async_copy(src, dst, sems.at[k]) for k, (src, dst) in enumerate(zip(sources, places))]
    for copy in copies:
        copy.start()
    copies[0].wait()
    sums = dense_of(jnp.sum(places[0][...], axis=0, keepdims=True))
    sums_ref[...] = jnp.broadcast_to(sums[None], sums_ref.shape)
    for copy in copies[1:]:
        copy.wait()


def ranks_of(owner, owners):
    rows = owner.shape[1]
    step = min(256, rows)
    before = ones_where(iota((step, step), 0) < iota((step, step), 1))
    base = jnp.zeros((owners, 1), f32)
    ranks = []
    for at in range(0, rows, step):
        hit = owner[:, at:at + step] == iota((owners, step), 0)
        hit_f = jnp.where(hit, 1.0, 0.0)
        seen = dot(hit_f.astype(bf16), before) + base
        ranks.append(jnp.sum(jnp.where(hit, seen, 0.0), axis=0, keepdims=True))
        base = base + jnp.sum(hit_f, axis=1, keepdims=True)
    return jnp.concatenate(ranks, axis=1).astype(i32)


def sort_kernel(
    owners, quarter_ref, leaf_ref, seas_ref, fine_ref, mid_ref, top_ref, base_mid_ref, base_top_ref,
    slots_ref, nodes_ref, places_ref, from_ref, known_ref, base_ref,
):
    days, rows = leaf_ref.shape
    owner = fine_ref[...] >> 6
    rank = ranks_of(owner, owners)
    place = owner * 16 + (rank & 15)
    place_low = jnp.where(rank < 16, place, -1)
    place_high = jnp.where(rank < 16, -1, place)
    places_ref[0:1, :] = place_low
    places_ref[1:2, :] = place_high

    leaf = leaf_ref[...]
    high = leaf.astype(bf16).astype(f32)
    series = iota((1, rows), 1)
    ones = jnp.ones((1, rows), f32)
    known = [(fine_ref[...] & 63).astype(f32), ones, ones, (series >> 7).astype(f32), (series & 127).astype(f32)]
    ext = jnp.concatenate([high] + known + [jnp.zeros((3, rows), f32), leaf - high], axis=0).astype(bf16)
    at = 0
    for ids, out_ref, height in (
        (place_low, slots_ref, owners * 16), (place_high, slots_ref, owners * 16),
        (mid_ref[...], nodes_ref, owners * 8), (top_ref[...], nodes_ref, TOP_ROWS),
    ):
        chunk = min(256, height)
        for start in range(0, height, chunk):
            sums = dot_nt(ext, ones_where(iota((chunk, rows), 0) + start == ids))
            tail = jnp.concatenate([sums[days + 8:, :], jnp.zeros((8, chunk), f32)], axis=0)
            out_ref[:, at:at + chunk] = sums[:days + 8, :] + tail
            at += chunk
        if ids is place_high:
            at = 0
    from_ref[0, :, :] = dense_of(slots_ref[LOW + 1:LOW + 2, :]).astype(i32)
    from_ref[1, :, :] = dense_of(slots_ref[LOW + 2:LOW + 3, :]).astype(i32)

    seas = seas_ref[...]
    season_days = days * 2
    line = iota(seas.shape, 0)
    own = jnp.sum(jnp.where(line == quarter_ref[0], seas, 0.0), axis=0, keepdims=True)
    four = jnp.sum(jnp.where(line < 4, seas, 0.0), axis=0, keepdims=True)
    known_ref[...] = dense_of(0.5 * own / season_days + 0.5 * (seas[4:5, :] - 0.5 * four) / (season_days * 4))

    half = days // 2
    day, lane = iota((days, 128), 0), iota((days, 128), 1)
    moves = (
        (day < half) & (lane == lane_of(day)),
        (day >= half) & (lane == lane_of(day - half)),
        lane == top_lane(day),
    )
    moves = [jnp.where(move, 1.0, 0.0) for move in moves]
    top = jnp.where(iota((16, days), 1) // 3 == iota((16, days), 0), base_top_ref[...], 0.0)
    exact = lax.Precision.HIGHEST
    mids = [jnp.dot(base_mid_ref[...], move, precision=exact, preferred_element_type=f32) for move in moves[:2]]
    base_ref[...] = jnp.concatenate(mids, axis=0) + jnp.dot(top, moves[2], precision=exact, preferred_element_type=f32)


def split_count(sums):
    high = sums.astype(bf16).astype(f32)
    return jnp.where(iota(sums.shape, 0) == LOW, sums - high, high)


def send_kernel(quarter_ref, parts_ref, known_ref, from_ref, slots_ref, nodes_ref, mid_ref, top_ref, pay_ref, shift_ref):
    owners = pay_ref.shape[0]
    rows = mid_ref.shape[1]
    slots, mids = owners * 16, owners * 8
    days = slots_ref.shape[0] - 8
    season_days = days * 2
    parts = parts_ref[...]
    own = jnp.sum(jnp.where(iota(parts.shape, 0) >> 1 == quarter_ref[0], parts, 0.0), axis=0)
    total = jnp.sum(parts, axis=0)
    shift = known_ref[...] - (0.5 * own / season_days + 0.25 * total / (season_days * 4))
    shift_row = row_of(shift)
    shift_ref[...] = shift_row

    line, lane = from_ref[0, :, :], from_ref[1, :, :]
    moved = jnp.zeros(shift.shape, f32)
    for at in range(shift.shape[0]):
        taken = jnp.take_along_axis(
            jnp.broadcast_to(shift[at:at + 1, :], shift.shape), lane, axis=1, mode="promise_in_bounds"
        )
        moved = jnp.where(line == at, taken, moved)
    moved = row_of(moved)

    high = shift_row.astype(bf16).astype(f32)
    ext = jnp.concatenate([high, shift_row - high, jnp.zeros((6, rows), f32)], axis=0).astype(bf16)
    node_sums = []
    for ids, height in ((mid_ref[...], mids), (top_ref[...], TOP_ROWS)):
        chunk = min(256, height)
        for start in range(0, height, chunk):
            hits = ones_where(iota((chunk, rows), 0) + start == ids)
            node_sums.append(jnp.sum(dot_nt(ext, hits), axis=0, keepdims=True))
    node_sums = jnp.concatenate(node_sums, axis=1)
    is_day = iota((days + 8, 1), 0) < days
    pad = jnp.zeros((8, rows + mids + TOP_ROWS), f32)
    sums = jnp.concatenate([slots_ref[...], nodes_ref[...]], axis=1)
    sums = sums + jnp.where(is_day, jnp.concatenate([moved, node_sums], axis=1), 0.0)
    sums = jnp.concatenate([sums, pad], axis=0)

    tops = split_count(sums[:, 2 * slots + mids:]).astype(bf16)
    tops = dot(tops, ones_where(iota((TOP_ROWS, slots), 0) == iota((TOP_ROWS, slots), 1) >> 4))
    row, column = iota((64, slots), 0), iota((64, slots), 1) & 15
    keep = (
        ((row < days) & (row // 3 == column))
        | ((row == ONE) & (column < 8))
        | ((row == LOW) & (column >= 8))
    )
    tops = jnp.where(keep, tops, 0.0).astype(bf16)
    lane, day = iota((128, 64), 0), iota((128, 64), 1)
    top_move = ((day < days) & (lane == top_lane(day))) | (((day == ONE) | (day == LOW)) & (lane == TOP_COUNT))
    tops = dot(ones_where(top_move), tops)
    tiles = jnp.concatenate([sums[:, :slots], sums[:, slots:2 * slots]], axis=0)
    tiles = jnp.where(slot_lanes((128, slots), 0), tiles, tops)

    half = days // 2
    mid_sums = split_count(sums[:, 2 * slots:2 * slots + mids])
    day, lane = iota((64, 128), 0), iota((64, 128), 1)
    moves = (
        ((day < half) & (lane == lane_of(day))) | ((day == ONE) & (lane == MID_COUNT)),
        ((day >= half) & (day < days) & (lane == lane_of(day - half))) | ((day == LOW) & (lane == MID_COUNT)),
    )
    moves = [ones_where(move) for move in moves]
    group = min(16, owners)
    for g in range(owners // group):
        own = jnp.transpose(mid_sums[:, g * group * 8:(g + 1) * group * 8]).astype(bf16)
        extra = jnp.concatenate([dot(own, move).reshape(group, 8, 128) for move in moves], axis=1)
        start, stop = g * group * 16, (g + 1) * group * 16
        tile = jnp.concatenate([jnp.transpose(tiles[:, at:at + 128]) for at in range(start, stop, 128)], axis=0)
        pay_ref[g * group:(g + 1) * group, :, :] = (tile.reshape(group, 16, 128) + extra).astype(bf16)


def owner_kernel(got_ref, base_fine_ref, base_rest_ref, back_ref):
    owners = got_ref.shape[0]
    days, nodes = base_fine_ref.shape
    got = got_ref[...].astype(f32)
    flat = got.reshape(owners * 16, 128)
    lanes = iota(flat.shape, 1)
    node = iota((owners * 16, nodes), 1).astype(f32)
    pick_low = ones_where(flat[:, ID:ID + 1] == node)
    pick_high = ones_where(flat[:, 64 + ID:65 + ID] == node)
    turned = jnp.transpose(jnp.where((lanes & 63) == ONE, 1.0, flat)).astype(bf16)
    totals = dot(turned[0:64, :], pick_low) + dot(turned[64:128, :], pick_high)
    gap = (base_fine_ref[...] - totals[0:days, :]) / (totals[ONE:ONE + 1, :] + 1.0)
    gap = jnp.concatenate([gap, jnp.zeros((64 - days, nodes), f32)], axis=0)
    gap = jnp.transpose(jnp.concatenate([gap, gap], axis=0)).astype(bf16)
    spread = jnp.where(lanes < 64, dot(pick_low, gap), dot(pick_high, gap))

    rest = jnp.sum(got, axis=0)
    pair = rest + jnp.concatenate([rest[8:16, :], rest[0:8, :]], axis=0)
    of_top = iota(rest.shape, 1) > MID_COUNT
    count = jnp.where(of_top, pair[:, TOP_COUNT:TOP_COUNT + 1], pair[:, MID_COUNT:MID_COUNT + 1])
    gap_rest = jnp.where(slot_lanes(rest.shape, 1), 0.0, (base_rest_ref[...] - rest) / (count + 1.0))
    spread = jnp.where(slot_lanes(flat.shape, 1), spread, 0.0).reshape(owners, 16, 128)
    back_ref[...] = (spread + gap_rest[None]).astype(bf16)


def finish_kernel(leaf_ref, shift_ref, places_ref, mid_ref, top_ref, back_ref, out_ref):
    days, rows = leaf_ref.shape
    owners = back_ref.shape[0]
    slots, mids = owners * 16, owners * 8
    half = days // 2
    back = back_ref[...].astype(f32)
    day, lane = iota((days, 128), 0), iota((days, 128), 1)
    take = jnp.concatenate([ones_where(lane == day), ones_where(lane == day + 64), ones_where(lane == top_lane(day))], axis=0)
    taken = dot_nt(take, back.reshape(slots, 128).astype(bf16))
    tops = jnp.where(iota((days, slots), 0) // 3 == (iota((days, slots), 1) & 15), taken[2 * days:, :], 0.0).astype(bf16)
    tops = dot(tops, ones_where(iota((slots, TOP_ROWS), 0) >> 4 == iota((slots, TOP_ROWS), 1)))
    first, last = (back[:, at:at + 8, :].reshape(mids, 128).astype(bf16) for at in (0, 8))
    mid = dot_nt(ones_where((day < half) & (lane == lane_of(day))), first)
    mid = mid + dot_nt(ones_where((day >= half) & (lane == lane_of(day - half))), last)
    gaps = [part.astype(bf16) for part in (taken[:days, :], taken[days:2 * days, :], mid, tops)]
    step = min(256, rows)
    for at in range(0, rows, step):
        ids = (
            places_ref[0:1, at:at + step], places_ref[1:2, at:at + step], mid_ref[:, at:at + step], top_ref[:, at:at + step]
        )
        out = leaf_ref[:, at:at + step] + shift_ref[:, at:at + step]
        for gap, place in zip(gaps, ids):
            out = out + dot(gap, ones_where(iota((gap.shape[1], step), 0) == place))
        out_ref[:, at:at + step] = out


def per_device(leaf, seas, fine, mid, top, base_fine, base_mid, base_top):
    days, rows = leaf.shape
    owners = lax.axis_size("series")
    blocks = lax.axis_size("tm")
    quarter = (lax.axis_index("tm") // (blocks // 4)).astype(i32).reshape(1)
    any_space = pl.BlockSpec(memory_space=pl.ANY)
    vmem = pl.BlockSpec(memory_space=pltpu.VMEM)
    smem = pl.BlockSpec(memory_space=pltpu.SMEM)

    arrays = (leaf, seas, *(ids.reshape(1, rows) for ids in (fine, mid, top)), base_mid.T, base_top.reshape(1, days))
    *arrays, sums = pl.pallas_call(
        start_kernel,
        out_shape=[jax.ShapeDtypeStruct(x.shape, x.dtype) for x in arrays]
        + [jax.ShapeDtypeStruct((blocks, rows // 128, 128), f32)],
        in_specs=[any_space] * len(arrays),
        scratch_shapes=[pltpu.SemaphoreType.DMA((len(arrays),))],
        compiler_params=PARAMS,
        name="start",
    )(*arrays)
    parts = lax.all_to_all(sums, "tm", 0, 0, tiled=True)
    leaf, seas, fine, mid, top, base_mid, base_top = arrays
    dense = (rows // 128, 128)
    slots, nodes, places, come_from, known, base_rest = pl.pallas_call(
        lambda *refs: sort_kernel(owners, *refs),
        out_shape=(
            jax.ShapeDtypeStruct((days + 8, rows), f32),
            jax.ShapeDtypeStruct((days + 8, owners * 8 + TOP_ROWS), f32),
            jax.ShapeDtypeStruct((2, rows), i32),
            jax.ShapeDtypeStruct((2,) + dense, i32),
            jax.ShapeDtypeStruct(dense, f32),
            jax.ShapeDtypeStruct((16, 128), f32),
        ),
        in_specs=[smem] + [vmem] * 7,
        compiler_params=PARAMS,
        cost_estimate=pl.CostEstimate(flops=2 * 104 * owners * 42 * rows, bytes_accessed=4 * days * rows, transcendentals=0),
        name="sort",
    )(quarter, *arrays)

    payload, shift = pl.pallas_call(
        send_kernel,
        out_shape=(jax.ShapeDtypeStruct((owners, 16, 128), bf16), jax.ShapeDtypeStruct((1, rows), f32)),
        in_specs=[smem] + [vmem] * 7,
        compiler_params=PARAMS,
        name="pack",
    )(quarter, parts, known, come_from, slots, nodes, mid, top)
    got = lax.all_to_all(payload, "series", 0, 0, tiled=True)
    back = pl.pallas_call(
        owner_kernel,
        out_shape=jax.ShapeDtypeStruct((owners, 16, 128), bf16),
        compiler_params=PARAMS,
        name="gaps",
    )(got, base_fine, base_rest)
    back = lax.all_to_all(back, "series", 0, 0, tiled=True)
    return pl.pallas_call(
        finish_kernel,
        out_shape=jax.ShapeDtypeStruct((days, rows), f32),
        compiler_params=PARAMS,
        name="finish",
    )(leaf, shift, places, mid, top, back)


def solution(mesh):
    return jax.shard_map(
        per_device,
        mesh=mesh,
        in_specs=(
            P("tm", "series"),
            P(None, "series"),
            P("series", None),
            P("series", None),
            P("series", None),
            P("tm", "series"),
            P("tm", "series"),
            P("tm", "series"),
        ),
        out_specs=P("tm", "series"),
        check_vma=False,
    )
```

```python
import jax
import jax.numpy as jnp
from jax import lax
from jax.experimental import pallas as pl
from jax.experimental.pallas import tpu as pltpu
from jax.sharding import PartitionSpec as P

f32 = jnp.float32
bf16 = jnp.bfloat16
i32 = jnp.int32

PARAMS = pltpu.CompilerParams(vmem_limit_bytes=24 * 1024 * 1024)

ID = 48
ONE = 49
LOW = 50
MID_COUNT = 122
TOP_COUNT = 126
TOP_ROWS = 128


def iota(shape, dim):
    return lax.broadcasted_iota(i32, shape, dim)


def lane_of(x):
    return jnp.where(x < 15, x + 49, x + 98)


def top_lane(day):
    return lane_of(25 + day - 3 * (day // 3))


def ones_where(mask):
    return jnp.where(mask, 1.0, 0.0).astype(bf16)


def hits(ids, start, height):
    low = jnp.where((ids >> 8) == (start >> 8), ids & 255, -1).astype(f32).astype(bf16)
    row = iota((height, 128), 0).astype(f32).astype(bf16)
    row = jnp.concatenate([row] * (ids.shape[1] // 128), axis=1)
    return jnp.where(row == low, jnp.ones((), bf16), jnp.zeros((), bf16))


def dot(a, b):
    return jnp.dot(a, b, preferred_element_type=f32)


def dot_nt(a, b, precision=None):
    return lax.dot_general(a, b, (((1,), (1,)), ((), ())), precision=precision, preferred_element_type=f32)


def slot_lanes(shape, dim):
    return (iota(shape, dim) & 63) <= ID


def row_of(dense):
    return jnp.concatenate([dense[at:at + 1, :] for at in range(dense.shape[0])], axis=1)


def dense_of(row):
    return jnp.concatenate([row[:, at:at + 128] for at in range(0, row.shape[1], 128)], axis=0)


def start_kernel(quarter_ref, leaf_ref, seas_ref, fine_ref, mid_ref, top_ref, sums_ref, ids_ref, known_ref):
    sums = dense_of(jnp.sum(leaf_ref[...], axis=0, keepdims=True))
    sums_ref[...] = jnp.broadcast_to(sums[None], sums_ref.shape)
    for at, ref in enumerate((fine_ref, mid_ref, top_ref)):
        ids_ref[at:at + 1, :] = ref[...]
    seas = seas_ref[...]
    season_days = leaf_ref.shape[0] * 2
    line = iota(seas.shape, 0)
    own = jnp.sum(jnp.where(line == quarter_ref[0], seas, 0.0), axis=0, keepdims=True)
    four = jnp.sum(jnp.where(line < 4, seas, 0.0), axis=0, keepdims=True)
    known_ref[...] = dense_of(0.5 * own / season_days + 0.5 * (seas[4:5, :] - 0.5 * four) / (season_days * 4))


def ranks_of(owner, owners):
    rows = owner.shape[1]
    step = min(256, rows)
    before = ones_where(iota((step, step), 0) < iota((step, step), 1))
    base = jnp.zeros((owners, 1), f32)
    ranks = []
    for at in range(0, rows, step):
        hit = owner[:, at:at + step] == iota((owners, step), 0)
        hit_f = jnp.where(hit, 1.0, 0.0)
        seen = dot(hit_f.astype(bf16), before) + base
        ranks.append(jnp.sum(jnp.where(hit, seen, 0.0), axis=0, keepdims=True))
        base = base + jnp.sum(hit_f, axis=1, keepdims=True)
    return jnp.concatenate(ranks, axis=1).astype(i32)


def sort_kernel(owners, leaf_ref, ids_ref, slots_ref, nodes_ref, places_ref, from_ref):
    days, rows = leaf_ref.shape
    fine, mid, top = (ids_ref[at:at + 1, :] for at in range(3))
    owner = fine >> 6
    rank = ranks_of(owner, owners)
    place = owner * 16 + (rank & 15)
    place_low = jnp.where(rank < 16, place, -1)
    place_high = jnp.where(rank < 16, -1, place)
    places_ref[0:1, :] = place_low
    places_ref[1:2, :] = place_high
    places_ref[2:3, :] = mid
    places_ref[3:4, :] = top

    leaf = leaf_ref[...]
    high = leaf.astype(bf16).astype(f32)
    series = iota((1, rows), 1)
    ones = jnp.ones((1, rows), f32)
    known = [(fine & 63).astype(f32), ones, ones, (series >> 7).astype(f32), (series & 127).astype(f32)]
    ext = jnp.concatenate([high] + known + [jnp.zeros((3, rows), f32), leaf - high], axis=0).astype(bf16)
    at = 0
    for ids, out_ref, height in (
        (place_low, slots_ref, owners * 16), (place_high, slots_ref, owners * 16),
        (mid, nodes_ref, owners * 8), (top, nodes_ref, TOP_ROWS),
    ):
        chunk = min(256, height)
        for start in range(0, height, chunk):
            sums = dot_nt(ext, hits(ids, start, chunk))
            tail = jnp.concatenate([sums[days + 8:, :], jnp.zeros((8, chunk), f32)], axis=0)
            out_ref[:, at:at + chunk] = sums[:days + 8, :] + tail
            at += chunk
        if ids is place_high:
            at = 0
    from_ref[0, :, :] = dense_of(slots_ref[LOW + 1:LOW + 2, :]).astype(i32)
    from_ref[1, :, :] = dense_of(slots_ref[LOW + 2:LOW + 3, :]).astype(i32)


def rest_in_lanes(base_mid, base_top):
    days = base_mid.shape[1]
    half = days // 2
    day, lane = iota((days, 128), 0), iota((days, 128), 1)
    moves = (
        (day < half) & (lane == lane_of(day)),
        (day >= half) & (lane == lane_of(day - half)),
        lane == top_lane(day),
    )
    moves = [jnp.where(move, 1.0, 0.0) for move in moves]
    top = jnp.where(iota((16, days), 1) // 3 == iota((16, days), 0), base_top, 0.0)
    exact = lax.Precision.HIGHEST
    mids = [jnp.dot(base_mid, move, precision=exact, preferred_element_type=f32) for move in moves[:2]]
    return jnp.concatenate(mids, axis=0) + jnp.dot(top, moves[2], precision=exact, preferred_element_type=f32)


def split_count(sums):
    high = sums.astype(bf16).astype(f32)
    return jnp.where(iota(sums.shape, 0) == LOW, sums - high, high)


def send_kernel(quarter_ref, parts_ref, known_ref, from_ref, slots_ref, nodes_ref, places_ref, pay_ref, shift_ref):
    owners = pay_ref.shape[0]
    rows = places_ref.shape[1]
    slots, mids = owners * 16, owners * 8
    days = slots_ref.shape[0] - 8
    season_days = days * 2
    parts = parts_ref[...]
    own = jnp.sum(jnp.where(iota(parts.shape, 0) >> 1 == quarter_ref[0], parts, 0.0), axis=0)
    total = jnp.sum(parts, axis=0)
    shift = known_ref[...] - (0.5 * own / season_days + 0.25 * total / (season_days * 4))
    shift_row = row_of(shift)
    shift_ref[...] = shift_row

    line, lane = from_ref[0, :, :], from_ref[1, :, :]
    moved = jnp.zeros(shift.shape, f32)
    for at in range(shift.shape[0]):
        taken = jnp.take_along_axis(
            jnp.broadcast_to(shift[at:at + 1, :], shift.shape), lane, axis=1, mode="promise_in_bounds"
        )
        moved = jnp.where(line == at, taken, moved)
    moved = row_of(moved)

    high = shift_row.astype(bf16).astype(f32)
    ext = jnp.concatenate([high, shift_row - high, jnp.zeros((6, rows), f32)], axis=0).astype(bf16)
    node_sums = []
    for ids, height in ((places_ref[2:3, :], mids), (places_ref[3:4, :], TOP_ROWS)):
        chunk = min(256, height)
        for start in range(0, height, chunk):
            node_sums.append(jnp.sum(dot_nt(ext, hits(ids, start, chunk)), axis=0, keepdims=True))
    node_sums = jnp.concatenate(node_sums, axis=1)
    is_day = iota((days + 8, 1), 0) < days
    pad = jnp.zeros((8, rows + mids + TOP_ROWS), f32)
    sums = jnp.concatenate([slots_ref[...], nodes_ref[...]], axis=1)
    sums = sums + jnp.where(is_day, jnp.concatenate([moved, node_sums], axis=1), 0.0)
    sums = jnp.concatenate([sums, pad], axis=0)

    tops = split_count(sums[:, 2 * slots + mids:]).astype(bf16)
    tops = dot(tops, ones_where(iota((TOP_ROWS, slots), 0) == iota((TOP_ROWS, slots), 1) >> 4))
    row, column = iota((64, slots), 0), iota((64, slots), 1) & 15
    keep = (
        ((row < days) & (row // 3 == column))
        | ((row == ONE) & (column < 8))
        | ((row == LOW) & (column >= 8))
    )
    tops = jnp.where(keep, tops, 0.0).astype(bf16)
    lane, day = iota((128, 64), 0), iota((128, 64), 1)
    top_move = ((day < days) & (lane == top_lane(day))) | (((day == ONE) | (day == LOW)) & (lane == TOP_COUNT))
    tops = dot(ones_where(top_move), tops)
    tiles = jnp.concatenate([sums[:, :slots], sums[:, slots:2 * slots]], axis=0)
    tiles = jnp.where(slot_lanes((128, slots), 0), tiles, tops)

    half = days // 2
    mid_sums = split_count(sums[:, 2 * slots:2 * slots + mids])
    day, lane = iota((64, 128), 0), iota((64, 128), 1)
    moves = (
        ((day < half) & (lane == lane_of(day))) | ((day == ONE) & (lane == MID_COUNT)),
        ((day >= half) & (day < days) & (lane == lane_of(day - half))) | ((day == LOW) & (lane == MID_COUNT)),
    )
    moves = [ones_where(move) for move in moves]
    group = min(16, owners)
    for g in range(owners // group):
        own = jnp.transpose(mid_sums[:, g * group * 8:(g + 1) * group * 8]).astype(bf16)
        extra = jnp.concatenate([dot(own, move).reshape(group, 8, 128) for move in moves], axis=1)
        start, stop = g * group * 16, (g + 1) * group * 16
        tile = jnp.concatenate([jnp.transpose(tiles[:, at:at + 128]) for at in range(start, stop, 128)], axis=0)
        pay_ref[g * group:(g + 1) * group, :, :] = (tile.reshape(group, 16, 128) + extra).astype(bf16)


def owner_kernel(got_ref, base_fine_ref, base_mid_ref, base_top_ref, back_ref):
    owners = got_ref.shape[0]
    days, nodes = base_fine_ref.shape
    got = got_ref[...].astype(f32)
    flat = got.reshape(owners * 16, 128)
    lanes = iota(flat.shape, 1)
    node = iota((owners * 16, nodes), 1).astype(f32)
    pick_low = ones_where(flat[:, ID:ID + 1] == node)
    pick_high = ones_where(flat[:, 64 + ID:65 + ID] == node)
    turned = jnp.transpose(jnp.where((lanes & 63) == ONE, 1.0, flat)).astype(bf16)
    totals = dot(turned[0:64, :], pick_low) + dot(turned[64:128, :], pick_high)
    gap = (base_fine_ref[...] - totals[0:days, :]) / (totals[ONE:ONE + 1, :] + 1.0)
    gap = jnp.concatenate([gap, jnp.zeros((64 - days, nodes), f32)], axis=0)
    gap = jnp.transpose(jnp.concatenate([gap, gap], axis=0)).astype(bf16)
    spread = jnp.where(lanes < 64, dot(pick_low, gap), dot(pick_high, gap))

    rest = jnp.sum(got, axis=0)
    pair = rest + jnp.concatenate([rest[8:16, :], rest[0:8, :]], axis=0)
    of_top = iota(rest.shape, 1) > MID_COUNT
    count = jnp.where(of_top, pair[:, TOP_COUNT:TOP_COUNT + 1], pair[:, MID_COUNT:MID_COUNT + 1])
    gap_rest = jnp.where(slot_lanes(rest.shape, 1), 0.0, (rest_in_lanes(base_mid_ref[...], base_top_ref[...]) - rest) / (count + 1.0))
    spread = jnp.where(slot_lanes(flat.shape, 1), spread, 0.0).reshape(owners, 16, 128)
    back_ref[...] = (spread + gap_rest[None]).astype(bf16)


def finish_kernel(leaf_ref, shift_ref, places_ref, back_ref, out_ref):
    days, rows = leaf_ref.shape
    owners = back_ref.shape[0]
    slots, mids = owners * 16, owners * 8
    half = days // 2
    back = back_ref[...].astype(f32)
    day, lane = iota((days, 128), 0), iota((days, 128), 1)
    take = jnp.concatenate([ones_where(lane == day), ones_where(lane == day + 64), ones_where(lane == top_lane(day))], axis=0)
    taken = dot_nt(take, back.reshape(slots, 128).astype(bf16))
    tops = jnp.where(iota((days, slots), 0) // 3 == (iota((days, slots), 1) & 15), taken[2 * days:, :], 0.0).astype(bf16)
    tops = dot(tops, ones_where(iota((slots, TOP_ROWS), 0) >> 4 == iota((slots, TOP_ROWS), 1)))
    first, last = (back[:, at:at + 8, :].reshape(mids, 128).astype(bf16) for at in (0, 8))
    mid = dot_nt(ones_where((day < half) & (lane == lane_of(day))), first)
    mid = mid + dot_nt(ones_where((day >= half) & (lane == lane_of(day - half))), last)
    gaps = [part.astype(bf16) for part in (taken[:days, :], taken[days:2 * days, :], mid, tops)]
    step = min(256, rows)
    for at in range(0, rows, step):
        ids = [places_ref[k:k + 1, at:at + step] for k in range(4)]
        out = leaf_ref[:, at:at + step] + shift_ref[:, at:at + step]
        for gap, place in zip(gaps, ids):
            height = gap.shape[1]
            chunk = min(256, height)
            blocks = [hits(place, start, chunk) for start in range(0, height, chunk)]
            out = out + dot(gap, jnp.concatenate(blocks, axis=0))
        out_ref[:, at:at + step] = out


def per_device(leaf, seas, fine, mid, top, base_fine, base_mid, base_top):
    days, rows = leaf.shape
    owners = lax.axis_size("series")
    blocks = lax.axis_size("tm")
    quarter = (lax.axis_index("tm") // (blocks // 4)).astype(i32).reshape(1)
    vmem = pl.BlockSpec(memory_space=pltpu.VMEM)
    smem = pl.BlockSpec(memory_space=pltpu.SMEM)
    dense = (rows // 128, 128)

    sums, ids, known = pl.pallas_call(
        start_kernel,
        out_shape=(
            jax.ShapeDtypeStruct((blocks,) + dense, f32),
            jax.ShapeDtypeStruct((3, rows), i32),
            jax.ShapeDtypeStruct(dense, f32),
        ),
        in_specs=[smem] + [vmem] * 5,
        compiler_params=PARAMS,
        name="start",
    )(quarter, leaf, seas, *(ids.reshape(1, rows) for ids in (fine, mid, top)))
    parts = lax.all_to_all(sums, "tm", 0, 0, tiled=True)
    slots, nodes, places, come_from = pl.pallas_call(
        lambda *refs: sort_kernel(owners, *refs),
        out_shape=(
            jax.ShapeDtypeStruct((days + 8, rows), f32),
            jax.ShapeDtypeStruct((days + 8, owners * 8 + TOP_ROWS), f32),
            jax.ShapeDtypeStruct((4, rows), i32),
            jax.ShapeDtypeStruct((2,) + dense, i32),
        ),
        compiler_params=PARAMS,
        cost_estimate=pl.CostEstimate(flops=2 * 104 * owners * 42 * rows, bytes_accessed=4 * days * rows, transcendentals=0),
        name="sort",
    )(leaf, ids)

    payload, shift = pl.pallas_call(
        send_kernel,
        out_shape=(jax.ShapeDtypeStruct((owners, 16, 128), bf16), jax.ShapeDtypeStruct((1, rows), f32)),
        in_specs=[smem] + [vmem] * 6,
        compiler_params=PARAMS,
        name="pack",
    )(quarter, parts, known, come_from, slots, nodes, places)
    got = lax.all_to_all(payload, "series", 0, 0, tiled=True)
    back = pl.pallas_call(
        owner_kernel,
        out_shape=jax.ShapeDtypeStruct((owners, 16, 128), bf16),
        compiler_params=PARAMS,
        name="gaps",
    )(got, base_fine, base_mid.T, base_top.reshape(1, days))
    back = lax.all_to_all(back, "series", 0, 0, tiled=True)
    return pl.pallas_call(
        finish_kernel,
        out_shape=jax.ShapeDtypeStruct((days, rows), f32),
        compiler_params=PARAMS,
        name="finish",
    )(leaf, shift, places, back)


def solution(mesh):
    return jax.shard_map(
        per_device,
        mesh=mesh,
        in_specs=(
            P("tm", "series"),
            P(None, "series"),
            P("series", None),
            P("series", None),
            P("series", None),
            P("tm", "series"),
            P("tm", "series"),
            P("tm", "series"),
        ),
        out_specs=P("tm", "series"),
        check_vma=False,
    )
```

```python
import jax
import jax.numpy as jnp
from jax import lax
from jax.experimental import pallas as pl
from jax.experimental.pallas import tpu as pltpu
from jax.sharding import PartitionSpec as P

f32 = jnp.float32
bf16 = jnp.bfloat16
i32 = jnp.int32

PARAMS = pltpu.CompilerParams(vmem_limit_bytes=24 * 1024 * 1024)

ID = 48
ONE = 49
LOW = 50
MID_COUNT = 122
TOP_COUNT = 126
TOP_ROWS = 128


def iota(shape, dim):
    return lax.broadcasted_iota(i32, shape, dim)


def lane_of(x):
    return jnp.where(x < 15, x + 49, x + 98)


def top_lane(day):
    return lane_of(25 + day - 3 * (day // 3))


def ones_where(mask):
    return jnp.where(mask, 1.0, 0.0).astype(bf16)


def hits(codes, height):
    row = iota((height, 128), 0).astype(f32).astype(bf16)
    row = jnp.concatenate([row] * (codes.shape[1] // 128), axis=1)
    return jnp.where(row == codes.astype(f32).astype(bf16), jnp.ones((), bf16), jnp.zeros((), bf16))


def node_hits(mid, top, width):
    return jnp.concatenate([hits(mid & (width - 1), width), hits(top, TOP_ROWS)], axis=0)


def by_group(rows, group, count):
    return jnp.concatenate([rows * ones_where(group == g) for g in range(count)], axis=0)


def dot(a, b):
    return jnp.dot(a, b, preferred_element_type=f32)


def dot_nt(a, b, precision=None):
    return lax.dot_general(a, b, (((1,), (1,)), ((), ())), precision=precision, preferred_element_type=f32)


def slot_lanes(shape, dim):
    return (iota(shape, dim) & 63) <= ID


def row_of(dense):
    return jnp.concatenate([dense[at:at + 1, :] for at in range(dense.shape[0])], axis=1)


def dense_of(row):
    return jnp.concatenate([row[:, at:at + 128] for at in range(0, row.shape[1], 128)], axis=0)


def start_kernel(leaf_ref, fine_ref, mid_ref, top_ref, base_mid_ref, base_top_ref, sums_ref, ids_ref, base_ref):
    sums = dense_of(jnp.sum(leaf_ref[...], axis=0, keepdims=True))
    sums_ref[...] = jnp.broadcast_to(sums[None], sums_ref.shape)
    for at, ref in enumerate((fine_ref, mid_ref, top_ref)):
        ids_ref[at:at + 1, :] = ref[...]
    base_ref[0:8, :] = base_mid_ref[...]
    base_ref[8:9, :] = base_top_ref[...]


def ranks_of(owner, owners):
    rows = owner.shape[1]
    step = min(256, rows)
    before = ones_where(iota((step, step), 0) < iota((step, step), 1))
    base = jnp.zeros((owners, 1), f32)
    ranks = []
    for at in range(0, rows, step):
        hit = owner[:, at:at + step] == iota((owners, step), 0)
        hit_f = jnp.where(hit, 1.0, 0.0)
        seen = dot(hit_f.astype(bf16), before) + base
        ranks.append(jnp.sum(jnp.where(hit, seen, 0.0), axis=0, keepdims=True))
        base = base + jnp.sum(hit_f, axis=1, keepdims=True)
    return jnp.concatenate(ranks, axis=1).astype(i32)


def sort_kernel(owners, leaf_ref, ids_ref, slots_ref, nodes_ref, places_ref, from_ref):
    days, rows = leaf_ref.shape
    fine, mid, top = (ids_ref[at:at + 1, :] for at in range(3))
    owner = fine >> 6
    rank = ranks_of(owner, owners)
    place = (rank >> 4) * (owners * 16) + owner * 16 + (rank & 15)
    places_ref[0:1, :] = place
    places_ref[1:2, :] = mid
    places_ref[2:3, :] = top

    leaf = leaf_ref[...]
    high = leaf.astype(bf16).astype(f32)
    series = iota((1, rows), 1)
    ones = jnp.ones((1, rows), f32)
    known = [(fine & 63).astype(f32), ones, ones, (series >> 7).astype(f32), (series & 127).astype(f32)]
    zeros = [jnp.zeros((3, rows), f32), jnp.zeros((8, rows), f32)]
    ext = jnp.concatenate([high] + known + [zeros[0], leaf - high, zeros[1]], axis=0).astype(bf16)
    height = days + 8

    def add_low(part):
        return part[:height, :] + jnp.concatenate([part[height:height + days, :], jnp.zeros((8, part.shape[1]), f32)], axis=0)

    count = rows // 256
    sums = dot_nt(by_group(ext, place >> 8, count), hits(place & 255, 256))
    for g in range(count):
        slots_ref[:, g * 256:(g + 1) * 256] = add_low(sums[g * 2 * height:(g + 1) * 2 * height, :])
    mids = owners * 8
    width = min(128, mids)
    count = mids // width
    sums = dot_nt(by_group(ext, mid // width, count), node_hits(mid, top, width))
    tops = jnp.zeros((height, TOP_ROWS), f32)
    for g in range(count):
        part = add_low(sums[g * 2 * height:(g + 1) * 2 * height, :])
        nodes_ref[:, g * width:(g + 1) * width] = part[:, :width]
        tops = tops + part[:, width:]
    nodes_ref[:, mids:] = tops
    from_ref[0, :, :] = dense_of(slots_ref[LOW + 1:LOW + 2, :]).astype(i32)
    from_ref[1, :, :] = dense_of(slots_ref[LOW + 2:LOW + 3, :]).astype(i32)


def rest_in_lanes(base_mid, base_top):
    days = base_mid.shape[1]
    half = days // 2
    day, lane = iota((days, 128), 0), iota((days, 128), 1)
    moves = (
        (day < half) & (lane == lane_of(day)),
        (day >= half) & (lane == lane_of(day - half)),
        lane == top_lane(day),
    )
    moves = [jnp.where(move, 1.0, 0.0) for move in moves]
    top = jnp.where(iota((16, days), 1) // 3 == iota((16, days), 0), base_top, 0.0)
    exact = lax.Precision.HIGHEST
    mids = [jnp.dot(base_mid, move, precision=exact, preferred_element_type=f32) for move in moves[:2]]
    return jnp.concatenate(mids, axis=0) + jnp.dot(top, moves[2], precision=exact, preferred_element_type=f32)


def split_count(sums):
    high = sums.astype(bf16).astype(f32)
    return jnp.where(iota(sums.shape, 0) == LOW, sums - high, high)


def send_kernel(quarter_ref, parts_ref, seas_ref, from_ref, slots_ref, nodes_ref, places_ref, pay_ref, shift_ref):
    owners = pay_ref.shape[0]
    rows = places_ref.shape[1]
    slots, mids = owners * 16, owners * 8
    days = slots_ref.shape[0] - 8
    season_days = days * 2
    parts = parts_ref[...]
    own = jnp.sum(jnp.where(iota(parts.shape, 0) >> 1 == quarter_ref[0], parts, 0.0), axis=0)
    total = jnp.sum(parts, axis=0)
    seas = seas_ref[...]
    line = iota(seas.shape, 0)
    seas_own = jnp.sum(jnp.where(line == quarter_ref[0], seas, 0.0), axis=0, keepdims=True)
    seas_four = jnp.sum(jnp.where(line < 4, seas, 0.0), axis=0, keepdims=True)
    known = dense_of(0.5 * seas_own / season_days + 0.5 * (seas[4:5, :] - 0.5 * seas_four) / (season_days * 4))
    shift = known - (0.5 * own / season_days + 0.25 * total / (season_days * 4))
    shift_row = row_of(shift)
    shift_ref[...] = shift_row

    line, lane = from_ref[0, :, :], from_ref[1, :, :]
    moved = jnp.zeros(shift.shape, f32)
    for at in range(shift.shape[0]):
        taken = jnp.take_along_axis(
            jnp.broadcast_to(shift[at:at + 1, :], shift.shape), lane, axis=1, mode="promise_in_bounds"
        )
        moved = jnp.where(line == at, taken, moved)
    moved = row_of(moved)

    high = shift_row.astype(bf16).astype(f32)
    ext = jnp.concatenate([high, shift_row - high, jnp.zeros((14, rows), f32)], axis=0).astype(bf16)
    mid, top = places_ref[1:2, :], places_ref[2:3, :]
    width = min(128, mids)
    count = mids // width
    found = dot_nt(by_group(ext, mid // width, count), node_hits(mid, top, width))
    found = [jnp.sum(found[g * 16:(g + 1) * 16, :], axis=0, keepdims=True) for g in range(count)]
    node_sums = jnp.concatenate([part[:, :width] for part in found] + [sum(part[:, width:] for part in found)], axis=1)
    is_day = iota((days + 8, 1), 0) < days
    pad = jnp.zeros((8, rows + mids + TOP_ROWS), f32)
    sums = jnp.concatenate([slots_ref[...], nodes_ref[...]], axis=1)
    sums = sums + jnp.where(is_day, jnp.concatenate([moved, node_sums], axis=1), 0.0)
    sums = jnp.concatenate([sums, pad], axis=0)

    tops = split_count(sums[:, 2 * slots + mids:]).astype(bf16)
    tops = dot(tops, ones_where(iota((TOP_ROWS, slots), 0) == iota((TOP_ROWS, slots), 1) >> 4))
    row, column = iota((64, slots), 0), iota((64, slots), 1) & 15
    keep = (
        ((row < days) & (row // 3 == column))
        | ((row == ONE) & (column < 8))
        | ((row == LOW) & (column >= 8))
    )
    tops = jnp.where(keep, tops, 0.0).astype(bf16)
    lane, day = iota((128, 64), 0), iota((128, 64), 1)
    top_move = ((day < days) & (lane == top_lane(day))) | (((day == ONE) | (day == LOW)) & (lane == TOP_COUNT))
    tops = dot(ones_where(top_move), tops)
    tiles = jnp.concatenate([sums[:, :slots], sums[:, slots:2 * slots]], axis=0)
    tiles = jnp.where(slot_lanes((128, slots), 0), tiles, tops)

    half = days // 2
    mid_sums = split_count(sums[:, 2 * slots:2 * slots + mids])
    day, lane = iota((64, 128), 0), iota((64, 128), 1)
    moves = (
        ((day < half) & (lane == lane_of(day))) | ((day == ONE) & (lane == MID_COUNT)),
        ((day >= half) & (day < days) & (lane == lane_of(day - half))) | ((day == LOW) & (lane == MID_COUNT)),
    )
    moves = [ones_where(move) for move in moves]
    group = min(16, owners)
    for g in range(owners // group):
        own = jnp.transpose(mid_sums[:, g * group * 8:(g + 1) * group * 8]).astype(bf16)
        extra = jnp.concatenate([dot(own, move).reshape(group, 8, 128) for move in moves], axis=1)
        start, stop = g * group * 16, (g + 1) * group * 16
        tile = jnp.concatenate([jnp.transpose(tiles[:, at:at + 128]) for at in range(start, stop, 128)], axis=0)
        pay_ref[g * group:(g + 1) * group, :, :] = (tile.reshape(group, 16, 128) + extra).astype(bf16)


def owner_kernel(got_ref, base_fine_ref, base_ref, back_ref):
    owners = got_ref.shape[0]
    days, nodes = base_fine_ref.shape
    got = got_ref[...].astype(f32)
    flat = got.reshape(owners * 16, 128)
    lanes = iota(flat.shape, 1)
    node = iota((owners * 16, nodes), 1).astype(f32)
    pick_low = ones_where(flat[:, ID:ID + 1] == node)
    pick_high = ones_where(flat[:, 64 + ID:65 + ID] == node)
    turned = jnp.transpose(jnp.where((lanes & 63) == ONE, 1.0, flat)).astype(bf16)
    totals = dot(turned[0:64, :], pick_low) + dot(turned[64:128, :], pick_high)
    gap = (base_fine_ref[...] - totals[0:days, :]) / (totals[ONE:ONE + 1, :] + 1.0)
    gap = jnp.concatenate([gap, jnp.zeros((64 - days, nodes), f32)], axis=0)
    gap = jnp.transpose(jnp.concatenate([gap, gap], axis=0)).astype(bf16)
    spread = jnp.where(lanes < 64, dot(pick_low, gap), dot(pick_high, gap))

    rest = jnp.sum(got, axis=0)
    pair = rest + jnp.concatenate([rest[8:16, :], rest[0:8, :]], axis=0)
    of_top = iota(rest.shape, 1) > MID_COUNT
    count = jnp.where(of_top, pair[:, TOP_COUNT:TOP_COUNT + 1], pair[:, MID_COUNT:MID_COUNT + 1])
    gap_rest = jnp.where(slot_lanes(rest.shape, 1), 0.0, (rest_in_lanes(base_ref[0:8, :], base_ref[8:9, :]) - rest) / (count + 1.0))
    spread = jnp.where(slot_lanes(flat.shape, 1), spread, 0.0).reshape(owners, 16, 128)
    back_ref[...] = (spread + gap_rest[None]).astype(bf16)


def finish_kernel(leaf_ref, shift_ref, places_ref, back_ref, out_ref):
    days, rows = leaf_ref.shape
    owners = back_ref.shape[0]
    slots, mids = owners * 16, owners * 8
    half = days // 2
    back = back_ref[...].astype(f32)
    day, lane = iota((days, 128), 0), iota((days, 128), 1)
    take = jnp.concatenate([ones_where(lane == day), ones_where(lane == day + 64), ones_where(lane == top_lane(day))], axis=0)
    taken = dot_nt(take, back.reshape(slots, 128).astype(bf16))
    tops = jnp.where(iota((days, slots), 0) // 3 == (iota((days, slots), 1) & 15), taken[2 * days:, :], 0.0).astype(bf16)
    tops = dot(tops, ones_where(iota((slots, TOP_ROWS), 0) >> 4 == iota((slots, TOP_ROWS), 1)))
    first, last = (back[:, at:at + 8, :].reshape(mids, 128).astype(bf16) for at in (0, 8))
    mid = dot_nt(ones_where((day < half) & (lane == lane_of(day))), first)
    mid = mid + dot_nt(ones_where((day >= half) & (lane == lane_of(day - half))), last)
    slot_count, width = rows // 256, min(128, mids)
    mid_count = mids // width
    taken = jnp.concatenate([taken[:days, :], taken[days:2 * days, :]], axis=1)
    slot_gaps = jnp.concatenate([taken[:, g * 256:(g + 1) * 256] for g in range(slot_count)], axis=0).astype(bf16)
    node_gaps = [jnp.concatenate([mid[:, g * width:(g + 1) * width], tops], axis=1) for g in range(mid_count)]
    node_gaps = jnp.concatenate(node_gaps, axis=0).astype(bf16)
    step = min(512, rows)
    for at in range(0, rows, step):
        place, mid, top = (places_ref[k:k + 1, at:at + step] for k in range(3))
        out = leaf_ref[:, at:at + step] + shift_ref[:, at:at + step]
        for gaps, hit, group, count in (
            (slot_gaps, hits(place & 255, 256), place >> 8, slot_count),
            (node_gaps, node_hits(mid, top, width), mid // width, mid_count),
        ):
            found = dot(gaps, hit)
            chosen = found[:days, :]
            for g in range(1, count):
                chosen = jnp.where(group == g, found[g * days:(g + 1) * days, :], chosen)
            out = out + chosen
        out_ref[:, at:at + step] = out


def per_device(leaf, seas, fine, mid, top, base_fine, base_mid, base_top):
    days, rows = leaf.shape
    owners = lax.axis_size("series")
    blocks = lax.axis_size("tm")
    quarter = (lax.axis_index("tm") // (blocks // 4)).astype(i32).reshape(1)
    vmem = pl.BlockSpec(memory_space=pltpu.VMEM)
    smem = pl.BlockSpec(memory_space=pltpu.SMEM)
    dense = (rows // 128, 128)

    sums, ids, base = pl.pallas_call(
        start_kernel,
        out_shape=(
            jax.ShapeDtypeStruct((blocks,) + dense, f32),
            jax.ShapeDtypeStruct((3, rows), i32),
            jax.ShapeDtypeStruct((16, days), f32),
        ),
        compiler_params=PARAMS,
        name="start",
    )(leaf, *(ids.reshape(1, rows) for ids in (fine, mid, top)), base_mid.T, base_top.reshape(1, days))
    parts = lax.all_to_all(sums, "tm", 0, 0, tiled=True)
    slots, nodes, places, come_from = pl.pallas_call(
        lambda *refs: sort_kernel(owners, *refs),
        out_shape=(
            jax.ShapeDtypeStruct((days + 8, rows), f32),
            jax.ShapeDtypeStruct((days + 8, owners * 8 + TOP_ROWS), f32),
            jax.ShapeDtypeStruct((3, rows), i32),
            jax.ShapeDtypeStruct((2,) + dense, i32),
        ),
        compiler_params=PARAMS,
        cost_estimate=pl.CostEstimate(flops=2 * 104 * owners * 42 * rows, bytes_accessed=4 * days * rows, transcendentals=0),
        name="sort",
    )(leaf, ids)

    payload, shift = pl.pallas_call(
        send_kernel,
        out_shape=(jax.ShapeDtypeStruct((owners, 16, 128), bf16), jax.ShapeDtypeStruct((1, rows), f32)),
        in_specs=[smem] + [vmem] * 6,
        compiler_params=PARAMS,
        name="pack",
    )(quarter, parts, seas, come_from, slots, nodes, places)
    got = lax.all_to_all(payload, "series", 0, 0, tiled=True)
    back = pl.pallas_call(
        owner_kernel,
        out_shape=jax.ShapeDtypeStruct((owners, 16, 128), bf16),
        compiler_params=PARAMS,
        name="gaps",
    )(got, base_fine, base)
    back = lax.all_to_all(back, "series", 0, 0, tiled=True)
    return pl.pallas_call(
        finish_kernel,
        out_shape=jax.ShapeDtypeStruct((days, rows), f32),
        compiler_params=PARAMS,
        name="finish",
    )(leaf, shift, places, back)


def solution(mesh):
    return jax.shard_map(
        per_device,
        mesh=mesh,
        in_specs=(
            P("tm", "series"),
            P(None, "series"),
            P("series", None),
            P("series", None),
            P("series", None),
            P("tm", "series"),
            P("tm", "series"),
            P("tm", "series"),
        ),
        out_specs=P("tm", "series"),
        check_vma=False,
    )
```

```python
import jax
import jax.numpy as jnp
from jax import lax
from jax.experimental import pallas as pl
from jax.experimental.pallas import tpu as pltpu
from jax.sharding import PartitionSpec as P

f32 = jnp.float32
bf16 = jnp.bfloat16
i32 = jnp.int32

PARAMS = pltpu.CompilerParams(vmem_limit_bytes=24 * 1024 * 1024)

ID = 48
ONE = 49
LOW = 50
MID_COUNT = 122
TOP_COUNT = 126
TOP_ROWS = 128


def iota(shape, dim):
    return lax.broadcasted_iota(i32, shape, dim)


def lane_of(x):
    return jnp.where(x < 15, x + 49, x + 98)


def top_lane(day):
    return lane_of(25 + day - 3 * (day // 3))


def ones_where(mask):
    return jnp.where(mask, 1.0, 0.0).astype(bf16)


def hits(codes, height):
    row = iota((height, 128), 0).astype(f32).astype(bf16)
    row = jnp.concatenate([row] * (codes.shape[1] // 128), axis=1)
    return jnp.where(row == codes.astype(f32).astype(bf16), jnp.ones((), bf16), jnp.zeros((), bf16))


def node_hits(mid, top, width):
    return jnp.concatenate([hits(mid & (width - 1), width), hits(top, TOP_ROWS)], axis=0)


def by_group(rows, group, count):
    return jnp.concatenate([rows * ones_where(group == g) for g in range(count)], axis=0)


def dot(a, b):
    return jnp.dot(a, b, preferred_element_type=f32)


def dot_nt(a, b, precision=None):
    return lax.dot_general(a, b, (((1,), (1,)), ((), ())), precision=precision, preferred_element_type=f32)


def slot_lanes(shape, dim):
    return (iota(shape, dim) & 63) <= ID


def row_of(dense):
    return jnp.concatenate([dense[at:at + 1, :] for at in range(dense.shape[0])], axis=1)


def dense_of(row):
    return jnp.concatenate([row[:, at:at + 128] for at in range(0, row.shape[1], 128)], axis=0)


def start_kernel(quarter_ref, leaf_ref, fine_ref, mid_ref, top_ref, base_mid_ref, base_top_ref, sums_ref, ids_ref, base_ref):
    sums = dense_of(jnp.sum(leaf_ref[...], axis=0, keepdims=True))
    sums_ref[...] = jnp.broadcast_to(sums[None], sums_ref.shape)
    for at, ref in enumerate((fine_ref, mid_ref, top_ref)):
        ids_ref[at:at + 1, :] = ref[...]
    ids_ref[3:4, :] = jnp.zeros_like(fine_ref[...]) + quarter_ref[0]
    base_ref[0:8, :] = base_mid_ref[...]
    base_ref[8:9, :] = base_top_ref[...]


def ranks_of(owner, owners):
    rows = owner.shape[1]
    step = min(256, rows)
    before = ones_where(iota((step, step), 0) < iota((step, step), 1))
    base = jnp.zeros((owners, 1), f32)
    ranks = []
    for at in range(0, rows, step):
        hit = owner[:, at:at + step] == iota((owners, step), 0)
        hit_f = jnp.where(hit, 1.0, 0.0)
        seen = dot(hit_f.astype(bf16), before) + base
        ranks.append(jnp.sum(jnp.where(hit, seen, 0.0), axis=0, keepdims=True))
        base = base + jnp.sum(hit_f, axis=1, keepdims=True)
    return jnp.concatenate(ranks, axis=1).astype(i32)


def sort_kernel(owners, leaf_ref, ids_ref, base_ref, slots_ref, nodes_ref, places_ref, from_ref, rest_ref):
    days, rows = leaf_ref.shape
    fine, mid, top = (ids_ref[at:at + 1, :] for at in range(3))
    owner = fine >> 6
    rank = ranks_of(owner, owners)
    place = (rank >> 4) * (owners * 16) + owner * 16 + (rank & 15)
    places_ref[0:1, :] = place
    places_ref[1:4, :] = ids_ref[1:4, :]

    leaf = leaf_ref[...]
    high = leaf.astype(bf16).astype(f32)
    series = iota((1, rows), 1)
    ones = jnp.ones((1, rows), f32)
    known = [(fine & 63).astype(f32), ones, ones, (series >> 7).astype(f32), (series & 127).astype(f32)]
    zeros = [jnp.zeros((3, rows), f32), jnp.zeros((8, rows), f32)]
    ext = jnp.concatenate([high] + known + [zeros[0], leaf - high, zeros[1]], axis=0).astype(bf16)
    height = days + 8

    def add_low(part):
        return part[:height, :] + jnp.concatenate([part[height:height + days, :], jnp.zeros((8, part.shape[1]), f32)], axis=0)

    count = rows // 256
    sums = dot_nt(by_group(ext, place >> 8, count), hits(place & 255, 256))
    for g in range(count):
        slots_ref[:, g * 256:(g + 1) * 256] = add_low(sums[g * 2 * height:(g + 1) * 2 * height, :])
    mids = owners * 8
    width = min(128, mids)
    count = mids // width
    sums = dot_nt(by_group(ext, mid // width, count), node_hits(mid, top, width))
    tops = jnp.zeros((height, TOP_ROWS), f32)
    for g in range(count):
        part = add_low(sums[g * 2 * height:(g + 1) * 2 * height, :])
        nodes_ref[:, g * width:(g + 1) * width] = part[:, :width]
        tops = tops + part[:, width:]
    nodes_ref[:, mids:] = tops
    from_ref[0, :, :] = dense_of(slots_ref[LOW + 1:LOW + 2, :]).astype(i32)
    from_ref[1, :, :] = dense_of(slots_ref[LOW + 2:LOW + 3, :]).astype(i32)
    rest_ref[...] = rest_in_lanes(base_ref[0:8, :], base_ref[8:9, :])


def rest_in_lanes(base_mid, base_top):
    days = base_mid.shape[1]
    half = days // 2
    day, lane = iota((days, 128), 0), iota((days, 128), 1)
    moves = (
        (day < half) & (lane == lane_of(day)),
        (day >= half) & (lane == lane_of(day - half)),
        lane == top_lane(day),
    )
    moves = [jnp.where(move, 1.0, 0.0) for move in moves]
    top = jnp.where(iota((16, days), 1) // 3 == iota((16, days), 0), base_top, 0.0)
    exact = lax.Precision.HIGHEST
    mids = [jnp.dot(base_mid, move, precision=exact, preferred_element_type=f32) for move in moves[:2]]
    return jnp.concatenate(mids, axis=0) + jnp.dot(top, moves[2], precision=exact, preferred_element_type=f32)


def split_count(sums):
    high = sums.astype(bf16).astype(f32)
    return jnp.where(iota(sums.shape, 0) == LOW, sums - high, high)


def send_kernel(parts_ref, seas_ref, from_ref, slots_ref, nodes_ref, places_ref, pay_ref, shift_ref):
    owners = pay_ref.shape[0]
    rows = places_ref.shape[1]
    slots, mids = owners * 16, owners * 8
    days = slots_ref.shape[0] - 8
    season_days = days * 2
    parts = parts_ref[...]
    quarter = places_ref[3:4, 0:128]
    own = jnp.sum(jnp.where(iota(parts.shape, 0) >> 1 == quarter[None], parts, 0.0), axis=0)
    total = jnp.sum(parts, axis=0)
    seas = seas_ref[...]
    line = iota(seas.shape, 0)
    seas_own = jnp.sum(jnp.where(line == places_ref[3:4, :], seas, 0.0), axis=0, keepdims=True)
    seas_four = jnp.sum(jnp.where(line < 4, seas, 0.0), axis=0, keepdims=True)
    known = dense_of(0.5 * seas_own / season_days + 0.5 * (seas[4:5, :] - 0.5 * seas_four) / (season_days * 4))
    shift = known - (0.5 * own / season_days + 0.25 * total / (season_days * 4))
    shift_row = row_of(shift)
    shift_ref[...] = shift_row

    line, lane = from_ref[0, :, :], from_ref[1, :, :]
    moved = jnp.zeros(shift.shape, f32)
    for at in range(shift.shape[0]):
        taken = jnp.take_along_axis(
            jnp.broadcast_to(shift[at:at + 1, :], shift.shape), lane, axis=1, mode="promise_in_bounds"
        )
        moved = jnp.where(line == at, taken, moved)
    moved = row_of(moved)

    high = shift_row.astype(bf16).astype(f32)
    ext = jnp.concatenate([high, shift_row - high, jnp.zeros((14, rows), f32)], axis=0).astype(bf16)
    mid, top = places_ref[1:2, :], places_ref[2:3, :]
    width = min(128, mids)
    count = mids // width
    found = dot_nt(by_group(ext, mid // width, count), node_hits(mid, top, width))
    found = [jnp.sum(found[g * 16:(g + 1) * 16, :], axis=0, keepdims=True) for g in range(count)]
    node_sums = jnp.concatenate([part[:, :width] for part in found] + [sum(part[:, width:] for part in found)], axis=1)
    is_day = iota((days + 8, 1), 0) < days
    pad = jnp.zeros((8, rows + mids + TOP_ROWS), f32)
    sums = jnp.concatenate([slots_ref[...], nodes_ref[...]], axis=1)
    sums = sums + jnp.where(is_day, jnp.concatenate([moved, node_sums], axis=1), 0.0)
    sums = jnp.concatenate([sums, pad], axis=0)

    tops = split_count(sums[:, 2 * slots + mids:]).astype(bf16)
    tops = dot(tops, ones_where(iota((TOP_ROWS, slots), 0) == iota((TOP_ROWS, slots), 1) >> 4))
    row, column = iota((64, slots), 0), iota((64, slots), 1) & 15
    keep = (
        ((row < days) & (row // 3 == column))
        | ((row == ONE) & (column < 8))
        | ((row == LOW) & (column >= 8))
    )
    tops = jnp.where(keep, tops, 0.0).astype(bf16)
    lane, day = iota((128, 64), 0), iota((128, 64), 1)
    top_move = ((day < days) & (lane == top_lane(day))) | (((day == ONE) | (day == LOW)) & (lane == TOP_COUNT))
    tops = dot(ones_where(top_move), tops)
    tiles = jnp.concatenate([sums[:, :slots], sums[:, slots:2 * slots]], axis=0)
    tiles = jnp.where(slot_lanes((128, slots), 0), tiles, tops)

    half = days // 2
    mid_sums = split_count(sums[:, 2 * slots:2 * slots + mids])
    day, lane = iota((64, 128), 0), iota((64, 128), 1)
    moves = (
        ((day < half) & (lane == lane_of(day))) | ((day == ONE) & (lane == MID_COUNT)),
        ((day >= half) & (day < days) & (lane == lane_of(day - half))) | ((day == LOW) & (lane == MID_COUNT)),
    )
    moves = [ones_where(move) for move in moves]
    group = min(16, owners)
    for g in range(owners // group):
        own = jnp.transpose(mid_sums[:, g * group * 8:(g + 1) * group * 8]).astype(bf16)
        extra = jnp.concatenate([dot(own, move).reshape(group, 8, 128) for move in moves], axis=1)
        start, stop = g * group * 16, (g + 1) * group * 16
        tile = jnp.concatenate([jnp.transpose(tiles[:, at:at + 128]) for at in range(start, stop, 128)], axis=0)
        pay_ref[g * group:(g + 1) * group, :, :] = (tile.reshape(group, 16, 128) + extra).astype(bf16)


def owner_kernel(got_ref, base_fine_ref, base_rest_ref, back_ref):
    owners = got_ref.shape[0]
    days, nodes = base_fine_ref.shape
    got = got_ref[...].astype(f32)
    flat = got.reshape(owners * 16, 128)
    lanes = iota(flat.shape, 1)
    node = iota((owners * 16, nodes), 1).astype(f32)
    pick_low = ones_where(flat[:, ID:ID + 1] == node)
    pick_high = ones_where(flat[:, 64 + ID:65 + ID] == node)
    turned = jnp.transpose(jnp.where((lanes & 63) == ONE, 1.0, flat)).astype(bf16)
    totals = dot(turned[0:64, :], pick_low) + dot(turned[64:128, :], pick_high)
    gap = (base_fine_ref[...] - totals[0:days, :]) / (totals[ONE:ONE + 1, :] + 1.0)
    gap = jnp.concatenate([gap, jnp.zeros((64 - days, nodes), f32)], axis=0)
    gap = jnp.transpose(jnp.concatenate([gap, gap], axis=0)).astype(bf16)
    spread = jnp.where(lanes < 64, dot(pick_low, gap), dot(pick_high, gap))

    rest = jnp.sum(got, axis=0)
    pair = rest + jnp.concatenate([rest[8:16, :], rest[0:8, :]], axis=0)
    of_top = iota(rest.shape, 1) > MID_COUNT
    count = jnp.where(of_top, pair[:, TOP_COUNT:TOP_COUNT + 1], pair[:, MID_COUNT:MID_COUNT + 1])
    gap_rest = jnp.where(slot_lanes(rest.shape, 1), 0.0, (base_rest_ref[...] - rest) / (count + 1.0))
    spread = jnp.where(slot_lanes(flat.shape, 1), spread, 0.0).reshape(owners, 16, 128)
    back_ref[...] = (spread + gap_rest[None]).astype(bf16)


def finish_kernel(leaf_ref, shift_ref, places_ref, back_ref, out_ref, done_ref, sems):
    days, rows = leaf_ref.shape
    owners = back_ref.shape[0]
    slots, mids = owners * 16, owners * 8
    half = days // 2
    back = back_ref[...].astype(f32)
    day, lane = iota((days, 128), 0), iota((days, 128), 1)
    take = jnp.concatenate([ones_where(lane == day), ones_where(lane == day + 64), ones_where(lane == top_lane(day))], axis=0)
    taken = dot_nt(take, back.reshape(slots, 128).astype(bf16))
    tops = jnp.where(iota((days, slots), 0) // 3 == (iota((days, slots), 1) & 15), taken[2 * days:, :], 0.0).astype(bf16)
    tops = dot(tops, ones_where(iota((slots, TOP_ROWS), 0) >> 4 == iota((slots, TOP_ROWS), 1)))
    first, last = (back[:, at:at + 8, :].reshape(mids, 128).astype(bf16) for at in (0, 8))
    mid = dot_nt(ones_where((day < half) & (lane == lane_of(day))), first)
    mid = mid + dot_nt(ones_where((day >= half) & (lane == lane_of(day - half))), last)
    slot_count, width = rows // 256, min(128, mids)
    mid_count = mids // width
    taken = jnp.concatenate([taken[:days, :], taken[days:2 * days, :]], axis=1)
    slot_gaps = jnp.concatenate([taken[:, g * 256:(g + 1) * 256] for g in range(slot_count)], axis=0).astype(bf16)
    node_gaps = [jnp.concatenate([mid[:, g * width:(g + 1) * width], tops], axis=1) for g in range(mid_count)]
    node_gaps = jnp.concatenate(node_gaps, axis=0).astype(bf16)
    step = min(512, rows)
    copies = []
    for at in range(0, rows, step):
        place, mid, top = (places_ref[k:k + 1, at:at + step] for k in range(3))
        out = leaf_ref[:, at:at + step] + shift_ref[:, at:at + step]
        for gaps, hit, group, count in (
            (slot_gaps, hits(place & 255, 256), place >> 8, slot_count),
            (node_gaps, node_hits(mid, top, width), mid // width, mid_count),
        ):
            found = dot(gaps, hit)
            chosen = found[:days, :]
            for g in range(1, count):
                chosen = jnp.where(group == g, found[g * days:(g + 1) * days, :], chosen)
            out = out + chosen
        done_ref[:, at:at + step] = out
        copies.append(pltpu.make_async_copy(done_ref.at[:, at:at + step], out_ref.at[:, at:at + step], sems.at[at // step]))
        copies[-1].start()
    for copy in copies:
        copy.wait()


def per_device(leaf, seas, fine, mid, top, base_fine, base_mid, base_top):
    days, rows = leaf.shape
    owners = lax.axis_size("series")
    blocks = lax.axis_size("tm")
    quarter = (lax.axis_index("tm") // (blocks // 4)).astype(i32).reshape(1)
    vmem = pl.BlockSpec(memory_space=pltpu.VMEM)
    smem = pl.BlockSpec(memory_space=pltpu.SMEM)
    dense = (rows // 128, 128)

    sums, ids, base = pl.pallas_call(
        start_kernel,
        out_shape=(
            jax.ShapeDtypeStruct((blocks,) + dense, f32),
            jax.ShapeDtypeStruct((4, rows), i32),
            jax.ShapeDtypeStruct((16, days), f32),
        ),
        in_specs=[smem] + [vmem] * 6,
        compiler_params=PARAMS,
        name="start",
    )(quarter, leaf, *(ids.reshape(1, rows) for ids in (fine, mid, top)), base_mid.T, base_top.reshape(1, days))
    parts = lax.all_to_all(sums, "tm", 0, 0, tiled=True)
    slots, nodes, places, come_from, base_rest = pl.pallas_call(
        lambda *refs: sort_kernel(owners, *refs),
        out_shape=(
            jax.ShapeDtypeStruct((days + 8, rows), f32),
            jax.ShapeDtypeStruct((days + 8, owners * 8 + TOP_ROWS), f32),
            jax.ShapeDtypeStruct((4, rows), i32),
            jax.ShapeDtypeStruct((2,) + dense, i32),
            jax.ShapeDtypeStruct((16, 128), f32),
        ),
        compiler_params=PARAMS,
        cost_estimate=pl.CostEstimate(flops=2 * 104 * owners * 42 * rows, bytes_accessed=4 * days * rows, transcendentals=0),
        name="sort",
    )(leaf, ids, base)

    payload, shift = pl.pallas_call(
        send_kernel,
        out_shape=(jax.ShapeDtypeStruct((owners, 16, 128), bf16), jax.ShapeDtypeStruct((1, rows), f32)),
        compiler_params=PARAMS,
        name="pack",
    )(parts, seas, come_from, slots, nodes, places)
    got = lax.all_to_all(payload, "series", 0, 0, tiled=True)
    back = pl.pallas_call(
        owner_kernel,
        out_shape=jax.ShapeDtypeStruct((owners, 16, 128), bf16),
        compiler_params=PARAMS,
        name="gaps",
    )(got, base_fine, base_rest)
    back = lax.all_to_all(back, "series", 0, 0, tiled=True)
    return pl.pallas_call(
        finish_kernel,
        out_shape=jax.ShapeDtypeStruct((days, rows), f32),
        in_specs=[vmem] * 4,
        out_specs=pl.BlockSpec(memory_space=pl.ANY),
        scratch_shapes=[pltpu.VMEM((days, rows), f32), pltpu.SemaphoreType.DMA((max(1, rows // 512),))],
        compiler_params=PARAMS,
        name="finish",
    )(leaf, shift, places, back)


def solution(mesh):
    return jax.shard_map(
        per_device,
        mesh=mesh,
        in_specs=(
            P("tm", "series"),
            P(None, "series"),
            P("series", None),
            P("series", None),
            P("series", None),
            P("tm", "series"),
            P("tm", "series"),
            P("tm", "series"),
        ),
        out_specs=P("tm", "series"),
        check_vma=False,
    )
```

```python
import jax
import jax.numpy as jnp
from jax import lax
from jax.experimental import pallas as pl
from jax.experimental.pallas import tpu as pltpu
from jax.sharding import PartitionSpec as P

f32 = jnp.float32
bf16 = jnp.bfloat16
i32 = jnp.int32

PARAMS = pltpu.CompilerParams(vmem_limit_bytes=24 * 1024 * 1024)

ID = 48
ONE = 49
LOW = 50
MID_COUNT = 122
TOP_COUNT = 126
TOP_ROWS = 128


def iota(shape, dim):
    return lax.broadcasted_iota(i32, shape, dim)


def lane_of(x):
    return jnp.where(x < 15, x + 49, x + 98)


def top_lane(day):
    return lane_of(25 + day - 3 * (day // 3))


def ones_where(mask):
    return jnp.where(mask, 1.0, 0.0).astype(bf16)


def hits(codes, height):
    row = iota((height, 128), 0).astype(f32).astype(bf16)
    row = jnp.concatenate([row] * (codes.shape[1] // 128), axis=1)
    return jnp.where(row == codes.astype(f32).astype(bf16), jnp.ones((), bf16), jnp.zeros((), bf16))


def node_hits(mid, top, width):
    return jnp.concatenate([hits(mid & (width - 1), width), hits(top, TOP_ROWS)], axis=0)


def by_group(rows, group, count):
    return jnp.concatenate([rows * ones_where(group == g) for g in range(count)], axis=0)


def dot(a, b):
    return jnp.dot(a, b, preferred_element_type=f32)


def dot_nt(a, b, precision=None):
    return lax.dot_general(a, b, (((1,), (1,)), ((), ())), precision=precision, preferred_element_type=f32)


def dot_tn(a, b):
    return lax.dot_general(a, b, (((0,), (0,)), ((), ())), preferred_element_type=f32)


def spread_row(row, lanes):
    high = row.astype(bf16).astype(f32)
    parts = jnp.concatenate([high, row - high, jnp.zeros((14, row.shape[1]), f32)], axis=0).astype(bf16)
    return dot_tn(parts, ones_where(lanes & (iota(lanes.shape, 0) < 2)))


def slot_lanes(shape, dim):
    return (iota(shape, dim) & 63) <= ID


def row_of(dense):
    return jnp.concatenate([dense[at:at + 1, :] for at in range(dense.shape[0])], axis=1)


def dense_of(row):
    return jnp.concatenate([row[:, at:at + 128] for at in range(0, row.shape[1], 128)], axis=0)


def start_kernel(leaf_ref, sums_ref):
    sums = dense_of(jnp.sum(leaf_ref[...], axis=0, keepdims=True))
    sums_ref[...] = jnp.broadcast_to(sums[None], sums_ref.shape)


def ranks_of(owner, owners):
    rows = owner.shape[1]
    step = min(256, rows)
    before = ones_where(iota((step, step), 0) < iota((step, step), 1))
    base = jnp.zeros((owners, 1), f32)
    ranks = []
    for at in range(0, rows, step):
        hit = owner[:, at:at + step] == iota((owners, step), 0)
        hit_f = jnp.where(hit, 1.0, 0.0)
        seen = dot(hit_f.astype(bf16), before) + base
        ranks.append(jnp.sum(jnp.where(hit, seen, 0.0), axis=0, keepdims=True))
        base = base + jnp.sum(hit_f, axis=1, keepdims=True)
    return jnp.concatenate(ranks, axis=1).astype(i32)


def sort_kernel(
    owners, quarter_ref, fine_ref, mid_ref, top_ref, base_mid_ref, base_top_ref, leaf_ref,
    tiles_ref, mids_ref, tops_ref, places_ref, from_ref, rest_ref,
):
    days, rows = leaf_ref.shape
    fine, mid, top = fine_ref[...], mid_ref[...], top_ref[...]
    owner = fine >> 6
    rank = ranks_of(owner, owners)
    place = (rank >> 4) * (owners * 16) + owner * 16 + (rank & 15)
    places_ref[0:1, :] = place
    places_ref[1:2, :] = mid
    places_ref[2:3, :] = top
    places_ref[3:4, :] = jnp.zeros_like(mid) + quarter_ref[0]

    leaf = leaf_ref[...]
    high = leaf.astype(bf16).astype(f32)
    series = iota((1, rows), 1)
    ones = jnp.ones((1, rows), f32)
    known = [(fine & 63).astype(f32), ones, ones, (series >> 7).astype(f32), (series & 127).astype(f32)]
    zeros = [jnp.zeros((3, rows), f32), jnp.zeros((8, rows), f32)]
    ext = jnp.concatenate([high] + known + [zeros[0], leaf - high, zeros[1]], axis=0).astype(bf16)
    height = days + 8

    def add_low(part):
        return part[:height, :] + jnp.concatenate([part[height:height + days, :], jnp.zeros((8, part.shape[1]), f32)], axis=0)

    def turned(part):
        part = jnp.concatenate([part, jnp.zeros((64 - height, part.shape[1]), f32)], axis=0)
        step = min(128, part.shape[1])
        return jnp.concatenate([jnp.transpose(part[:, at:at + step]) for at in range(0, part.shape[1], step)], axis=0)

    count = rows // 256
    half = rows // 2
    sums = dot_nt(by_group(ext, place >> 8, count), hits(place & 255, 256))
    sums = jnp.concatenate([add_low(sums[g * 2 * height:(g + 1) * 2 * height, :]) for g in range(count)], axis=1)
    pad = jnp.zeros((64 - height, rows), f32)
    both = jnp.concatenate([sums, pad], axis=0)
    both = jnp.concatenate([both[:, :half], both[:, half:]], axis=0)
    tiles_ref[...] = jnp.concatenate([jnp.transpose(both[:, at:at + 128]) for at in range(0, half, 128)], axis=0)
    from_ref[0, :, :] = dense_of(sums[LOW + 1:LOW + 2, :]).astype(i32)
    from_ref[1, :, :] = dense_of(sums[LOW + 2:LOW + 3, :]).astype(i32)

    mids = owners * 8
    width = min(128, mids)
    count = mids // width
    sums = dot_nt(by_group(ext, mid // width, count), node_hits(mid, top, width))
    sums = [add_low(sums[g * 2 * height:(g + 1) * 2 * height, :]) for g in range(count)]
    mids_ref[...] = turned(jnp.concatenate([part[:, :width] for part in sums], axis=1))
    tops_ref[...] = turned(sum(part[:, width:] for part in sums))
    rest_ref[...] = rest_in_lanes(base_mid_ref[...], base_top_ref[...])


def rest_in_lanes(base_mid, base_top):
    days = base_mid.shape[1]
    half = days // 2
    day, lane = iota((days, 128), 0), iota((days, 128), 1)
    moves = (
        (day < half) & (lane == lane_of(day)),
        (day >= half) & (lane == lane_of(day - half)),
        lane == top_lane(day),
    )
    moves = [jnp.where(move, 1.0, 0.0) for move in moves]
    top = jnp.where(iota((16, days), 1) // 3 == iota((16, days), 0), base_top, 0.0)
    exact = lax.Precision.HIGHEST
    mids = [jnp.dot(base_mid, move, precision=exact, preferred_element_type=f32) for move in moves[:2]]
    return jnp.concatenate(mids, axis=0) + jnp.dot(top, moves[2], precision=exact, preferred_element_type=f32)


def split_count(sums):
    high = sums.astype(bf16).astype(f32)
    return jnp.where(iota(sums.shape, 1) == LOW, sums - high, high).astype(bf16)


def send_kernel(parts_ref, seas_ref, from_ref, tiles_ref, mids_ref, tops_ref, places_ref, pay_ref, shift_ref):
    owners = pay_ref.shape[0]
    rows = places_ref.shape[1]
    slots, mids = owners * 16, owners * 8
    days = 48
    season_days = days * 2
    parts = parts_ref[...]
    quarter = places_ref[3:4, 0:128]
    own = jnp.sum(jnp.where(iota(parts.shape, 0) >> 1 == quarter[None], parts, 0.0), axis=0)
    total = jnp.sum(parts, axis=0)
    seas = seas_ref[...]
    line = iota(seas.shape, 0)
    seas_own = jnp.sum(jnp.where(line == places_ref[3:4, :], seas, 0.0), axis=0, keepdims=True)
    seas_four = jnp.sum(jnp.where(line < 4, seas, 0.0), axis=0, keepdims=True)
    known = dense_of(0.5 * seas_own / season_days + 0.5 * (seas[4:5, :] - 0.5 * seas_four) / (season_days * 4))
    shift = known - (0.5 * own / season_days + 0.25 * total / (season_days * 4))
    shift_row = row_of(shift)
    shift_ref[...] = shift_row

    line, lane = from_ref[0, :, :], from_ref[1, :, :]
    moved = jnp.zeros(shift.shape, f32)
    for at in range(shift.shape[0]):
        taken = jnp.take_along_axis(
            jnp.broadcast_to(shift[at:at + 1, :], shift.shape), lane, axis=1, mode="promise_in_bounds"
        )
        moved = jnp.where(line == at, taken, moved)
    moved = row_of(moved)

    high = shift_row.astype(bf16).astype(f32)
    ext = jnp.concatenate([high, shift_row - high, jnp.zeros((14, rows), f32)], axis=0).astype(bf16)
    mid, top = places_ref[1:2, :], places_ref[2:3, :]
    width = min(128, mids)
    count = mids // width
    found = dot_nt(by_group(ext, mid // width, count), node_hits(mid, top, width))
    found = [jnp.sum(found[g * 16:(g + 1) * 16, :], axis=0, keepdims=True) for g in range(count)]
    lane = iota((16, 128), 1)
    is_day = iota((16, 64), 1) < days
    mid_sums = mids_ref[...] + spread_row(jnp.concatenate([part[:, :width] for part in found], axis=1), is_day)
    top_sums = tops_ref[...] + spread_row(sum(part[:, width:] for part in found), is_day)
    tiles = tiles_ref[...] + spread_row(moved[:, :slots], lane < days)
    tiles = tiles + spread_row(moved[:, slots:], (lane >= 64) & (lane < 64 + days))

    row, day = iota((slots, 64), 0) & 15, iota((slots, 64), 1)
    keep = ((day < days) & (day // 3 == row)) | ((day == ONE) & (row < 8)) | ((day == LOW) & (row >= 8))
    owner = ones_where(iota((slots, TOP_ROWS), 0) >> 4 == iota((slots, TOP_ROWS), 1))
    top = jnp.where(keep, dot(owner, split_count(top_sums)), 0.0).astype(bf16)
    half = days // 2
    day, lane = iota((64, 128), 0), iota((64, 128), 1)
    moves = (
        ((day < half) & (lane == lane_of(day))) | ((day == ONE) & (lane == MID_COUNT)),
        ((day >= half) & (day < days) & (lane == lane_of(day - half))) | ((day == LOW) & (lane == MID_COUNT)),
        ((day < days) & (lane == top_lane(day))) | (((day == ONE) | (day == LOW)) & (lane == TOP_COUNT)),
    )
    moves = [ones_where(move) for move in moves]
    own = split_count(mid_sums)
    extra = jnp.concatenate([dot(own, move).reshape(owners, 8, 128) for move in moves[:2]], axis=1)
    tiles = jnp.where(slot_lanes((slots, 128), 1), tiles, dot(top, moves[2]))
    pay_ref[...] = (tiles.reshape(owners, 16, 128) + extra).astype(bf16)


def owner_kernel(got_ref, base_fine_ref, base_rest_ref, back_ref):
    owners = got_ref.shape[0]
    days, nodes = base_fine_ref.shape
    got = got_ref[...].astype(f32)
    flat = got.reshape(owners * 16, 128)
    lanes = iota(flat.shape, 1)
    node = iota((owners * 16, nodes), 1).astype(f32)
    pick_low = ones_where(flat[:, ID:ID + 1] == node)
    pick_high = ones_where(flat[:, 64 + ID:65 + ID] == node)
    turned = jnp.transpose(jnp.where((lanes & 63) == ONE, 1.0, flat)).astype(bf16)
    totals = dot(turned[0:64, :], pick_low) + dot(turned[64:128, :], pick_high)
    gap = (base_fine_ref[...] - totals[0:days, :]) / (totals[ONE:ONE + 1, :] + 1.0)
    gap = jnp.concatenate([gap, jnp.zeros((64 - days, nodes), f32)], axis=0)
    gap = jnp.transpose(jnp.concatenate([gap, gap], axis=0)).astype(bf16)
    spread = jnp.where(lanes < 64, dot(pick_low, gap), dot(pick_high, gap))

    rest = jnp.sum(got, axis=0)
    pair = rest + jnp.concatenate([rest[8:16, :], rest[0:8, :]], axis=0)
    of_top = iota(rest.shape, 1) > MID_COUNT
    count = jnp.where(of_top, pair[:, TOP_COUNT:TOP_COUNT + 1], pair[:, MID_COUNT:MID_COUNT + 1])
    gap_rest = jnp.where(slot_lanes(rest.shape, 1), 0.0, (base_rest_ref[...] - rest) / (count + 1.0))
    spread = jnp.where(slot_lanes(flat.shape, 1), spread, 0.0).reshape(owners, 16, 128)
    back_ref[...] = (spread + gap_rest[None]).astype(bf16)


def finish_kernel(leaf_ref, shift_ref, places_ref, back_ref, out_ref, done_ref, sems):
    days, rows = leaf_ref.shape
    owners = back_ref.shape[0]
    slots, mids = owners * 16, owners * 8
    half = days // 2
    back = back_ref[...].astype(f32)
    day, lane = iota((days, 128), 0), iota((days, 128), 1)
    take = jnp.concatenate([ones_where(lane == day), ones_where(lane == day + 64), ones_where(lane == top_lane(day))], axis=0)
    taken = dot_nt(take, back.reshape(slots, 128).astype(bf16))
    tops = jnp.where(iota((days, slots), 0) // 3 == (iota((days, slots), 1) & 15), taken[2 * days:, :], 0.0).astype(bf16)
    tops = dot(tops, ones_where(iota((slots, TOP_ROWS), 0) >> 4 == iota((slots, TOP_ROWS), 1)))
    first, last = (back[:, at:at + 8, :].reshape(mids, 128).astype(bf16) for at in (0, 8))
    mid = dot_nt(ones_where((day < half) & (lane == lane_of(day))), first)
    mid = mid + dot_nt(ones_where((day >= half) & (lane == lane_of(day - half))), last)
    slot_count, width = rows // 256, min(128, mids)
    mid_count = mids // width
    taken = jnp.concatenate([taken[:days, :], taken[days:2 * days, :]], axis=1)
    slot_gaps = jnp.concatenate([taken[:, g * 256:(g + 1) * 256] for g in range(slot_count)], axis=0).astype(bf16)
    node_gaps = [jnp.concatenate([mid[:, g * width:(g + 1) * width], tops], axis=1) for g in range(mid_count)]
    node_gaps = jnp.concatenate(node_gaps, axis=0).astype(bf16)
    step = min(512, rows)
    copies = []
    for at in range(0, rows, step):
        place, mid, top = (places_ref[k:k + 1, at:at + step] for k in range(3))
        out = leaf_ref[:, at:at + step] + shift_ref[:, at:at + step]
        for gaps, hit, group, count in (
            (slot_gaps, hits(place & 255, 256), place >> 8, slot_count),
            (node_gaps, node_hits(mid, top, width), mid // width, mid_count),
        ):
            found = dot(gaps, hit)
            chosen = found[:days, :]
            for g in range(1, count):
                chosen = jnp.where(group == g, found[g * days:(g + 1) * days, :], chosen)
            out = out + chosen
        done_ref[:, at:at + step] = out
        copies.append(pltpu.make_async_copy(done_ref.at[:, at:at + step], out_ref.at[:, at:at + step], sems.at[at // step]))
        copies[-1].start()
    for copy in copies:
        copy.wait()


def per_device(leaf, seas, fine, mid, top, base_fine, base_mid, base_top):
    days, rows = leaf.shape
    owners = lax.axis_size("series")
    blocks = lax.axis_size("tm")
    quarter = (lax.axis_index("tm") // (blocks // 4)).astype(i32).reshape(1)
    vmem = pl.BlockSpec(memory_space=pltpu.VMEM)
    smem = pl.BlockSpec(memory_space=pltpu.SMEM)
    dense = (rows // 128, 128)

    sums = pl.pallas_call(
        start_kernel, out_shape=jax.ShapeDtypeStruct((blocks,) + dense, f32), compiler_params=PARAMS, name="day_sums"
    )(leaf)
    parts = lax.all_to_all(sums, "tm", 0, 0, tiled=True)
    tiles, mids, tops, places, come_from, base_rest = pl.pallas_call(
        lambda *refs: sort_kernel(owners, *refs),
        out_shape=(
            jax.ShapeDtypeStruct((owners * 16, 128), f32),
            jax.ShapeDtypeStruct((owners * 8, 64), f32),
            jax.ShapeDtypeStruct((TOP_ROWS, 64), f32),
            jax.ShapeDtypeStruct((4, rows), i32),
            jax.ShapeDtypeStruct((2,) + dense, i32),
            jax.ShapeDtypeStruct((16, 128), f32),
        ),
        in_specs=[smem] + [vmem] * 6,
        compiler_params=PARAMS,
        cost_estimate=pl.CostEstimate(flops=2 * 104 * owners * 42 * rows, bytes_accessed=4 * days * rows, transcendentals=0),
        name="sort",
    )(quarter, *(ids.reshape(1, rows) for ids in (fine, mid, top)), base_mid.T, base_top.reshape(1, days), leaf)

    payload, shift = pl.pallas_call(
        send_kernel,
        out_shape=(jax.ShapeDtypeStruct((owners, 16, 128), bf16), jax.ShapeDtypeStruct((1, rows), f32)),
        compiler_params=PARAMS,
        name="pack",
    )(parts, seas, come_from, tiles, mids, tops, places)
    got = lax.all_to_all(payload, "series", 0, 0, tiled=True)
    back = pl.pallas_call(
        owner_kernel,
        out_shape=jax.ShapeDtypeStruct((owners, 16, 128), bf16),
        compiler_params=PARAMS,
        name="gaps",
    )(got, base_fine, base_rest)
    back = lax.all_to_all(back, "series", 0, 0, tiled=True)
    return pl.pallas_call(
        finish_kernel,
        out_shape=jax.ShapeDtypeStruct((days, rows), f32),
        in_specs=[vmem] * 4,
        out_specs=pl.BlockSpec(memory_space=pl.ANY),
        scratch_shapes=[pltpu.VMEM((days, rows), f32), pltpu.SemaphoreType.DMA((max(1, rows // 512),))],
        compiler_params=PARAMS,
        name="finish",
    )(leaf, shift, places, back)


def solution(mesh):
    return jax.shard_map(
        per_device,
        mesh=mesh,
        in_specs=(
            P("tm", "series"),
            P(None, "series"),
            P("series", None),
            P("series", None),
            P("series", None),
            P("tm", "series"),
            P("tm", "series"),
            P("tm", "series"),
        ),
        out_specs=P("tm", "series"),
        check_vma=False,
    )
```

```python
import jax
import jax.numpy as jnp
from jax import lax
from jax.experimental import pallas as pl
from jax.experimental.pallas import tpu as pltpu
from jax.sharding import PartitionSpec as P

f32 = jnp.float32
bf16 = jnp.bfloat16
i32 = jnp.int32

PARAMS = pltpu.CompilerParams(vmem_limit_bytes=24 * 1024 * 1024)

ID = 48
ONE = 49
LOW = 50
MID_COUNT = 122
TOP_COUNT = 126
TOP_ROWS = 128


def iota(shape, dim):
    return lax.broadcasted_iota(i32, shape, dim)


def lane_of(x):
    return jnp.where(x < 15, x + 49, x + 98)


def top_lane(day):
    return lane_of(25 + day - 3 * (day // 3))


def ones_where(mask):
    return jnp.where(mask, 1.0, 0.0).astype(bf16)


def hits(codes, height):
    row = iota((height, 128), 0).astype(f32).astype(bf16)
    row = jnp.concatenate([row] * (codes.shape[1] // 128), axis=1)
    return jnp.where(row == codes.astype(f32).astype(bf16), jnp.ones((), bf16), jnp.zeros((), bf16))


def node_hits(mid, top, width):
    return jnp.concatenate([hits(mid & (width - 1), width), hits(top, TOP_ROWS)], axis=0)


def by_group(rows, group, count):
    return jnp.concatenate([rows * ones_where(group == g) for g in range(count)], axis=0)


def dot(a, b):
    return jnp.dot(a, b, preferred_element_type=f32)


def dot_nt(a, b, precision=None):
    return lax.dot_general(a, b, (((1,), (1,)), ((), ())), precision=precision, preferred_element_type=f32)


def slot_lanes(shape, dim):
    return (iota(shape, dim) & 63) <= ID


def row_of(dense):
    return jnp.concatenate([dense[at:at + 1, :] for at in range(dense.shape[0])], axis=1)


def dense_of(row):
    return jnp.concatenate([row[:, at:at + 128] for at in range(0, row.shape[1], 128)], axis=0)


def start_kernel(leaf_ref, sums_ref):
    sums = dense_of(jnp.sum(leaf_ref[...], axis=0, keepdims=True))
    sums_ref[...] = jnp.broadcast_to(sums[None], sums_ref.shape)


def ranks_of(owner, owners):
    rows = owner.shape[1]
    step = min(256, rows)
    before = ones_where(iota((step, step), 0) < iota((step, step), 1))
    base = jnp.zeros((owners, 1), f32)
    ranks = []
    for at in range(0, rows, step):
        hit = owner[:, at:at + step] == iota((owners, step), 0)
        hit_f = jnp.where(hit, 1.0, 0.0)
        seen = dot(hit_f.astype(bf16), before) + base
        ranks.append(jnp.sum(jnp.where(hit, seen, 0.0), axis=0, keepdims=True))
        base = base + jnp.sum(hit_f, axis=1, keepdims=True)
    return jnp.concatenate(ranks, axis=1).astype(i32)


def sort_kernel(
    owners, quarter_ref, fine_ref, mid_ref, top_ref, base_mid_ref, base_top_ref, seas_ref, leaf_ref,
    slots_ref, nodes_ref, places_ref, from_ref, rest_ref, known_ref,
):
    days, rows = leaf_ref.shape
    fine, mid, top = fine_ref[...], mid_ref[...], top_ref[...]
    owner = fine >> 6
    rank = ranks_of(owner, owners)
    place = (rank >> 4) * (owners * 16) + owner * 16 + (rank & 15)
    places_ref[0:1, :] = place
    places_ref[1:2, :] = mid
    places_ref[2:3, :] = top
    places_ref[3:4, :] = jnp.zeros_like(mid) + quarter_ref[0]

    leaf = leaf_ref[...]
    high = leaf.astype(bf16).astype(f32)
    series = iota((1, rows), 1)
    ones = jnp.ones((1, rows), f32)
    known = [(fine & 63).astype(f32), ones, ones, (series >> 7).astype(f32), (series & 127).astype(f32)]
    zeros = [jnp.zeros((3, rows), f32), jnp.zeros((8, rows), f32)]
    ext = jnp.concatenate([high] + known + [zeros[0], leaf - high, zeros[1]], axis=0).astype(bf16)
    height = days + 8

    def add_low(part):
        return part[:height, :] + jnp.concatenate([part[height:height + days, :], jnp.zeros((8, part.shape[1]), f32)], axis=0)

    count = rows // 256
    sums = dot_nt(by_group(ext, place >> 8, count), hits(place & 255, 256))
    for g in range(count):
        slots_ref[:, g * 256:(g + 1) * 256] = add_low(sums[g * 2 * height:(g + 1) * 2 * height, :])
    mids = owners * 8
    width = min(128, mids)
    count = mids // width
    sums = dot_nt(by_group(ext, mid // width, count), node_hits(mid, top, width))
    tops = jnp.zeros((height, TOP_ROWS), f32)
    for g in range(count):
        part = add_low(sums[g * 2 * height:(g + 1) * 2 * height, :])
        nodes_ref[:, g * width:(g + 1) * width] = part[:, :width]
        tops = tops + part[:, width:]
    nodes_ref[:, mids:] = tops
    from_ref[0, :, :] = dense_of(slots_ref[LOW + 1:LOW + 2, :]).astype(i32)
    from_ref[1, :, :] = dense_of(slots_ref[LOW + 2:LOW + 3, :]).astype(i32)
    seas = seas_ref[...]
    season_days = days * 2
    line = iota(seas.shape, 0)
    seas_own = jnp.sum(jnp.where(line == quarter_ref[0], seas, 0.0), axis=0, keepdims=True)
    seas_four = jnp.sum(jnp.where(line < 4, seas, 0.0), axis=0, keepdims=True)
    known_ref[...] = dense_of(0.5 * seas_own / season_days + 0.5 * (seas[4:5, :] - 0.5 * seas_four) / (season_days * 4))
    rest_ref[...] = rest_in_lanes(base_mid_ref[...], base_top_ref[...])


def rest_in_lanes(base_mid, base_top):
    days = base_mid.shape[1]
    half = days // 2
    day, lane = iota((days, 128), 0), iota((days, 128), 1)
    moves = (
        (day < half) & (lane == lane_of(day)),
        (day >= half) & (lane == lane_of(day - half)),
        lane == top_lane(day),
    )
    moves = [jnp.where(move, 1.0, 0.0) for move in moves]
    top = jnp.where(iota((16, days), 1) // 3 == iota((16, days), 0), base_top, 0.0)
    exact = lax.Precision.HIGHEST
    mids = [jnp.dot(base_mid, move, precision=exact, preferred_element_type=f32) for move in moves[:2]]
    return jnp.concatenate(mids, axis=0) + jnp.dot(top, moves[2], precision=exact, preferred_element_type=f32)


def split_count(sums):
    high = sums.astype(bf16).astype(f32)
    return jnp.where(iota(sums.shape, 0) == LOW, sums - high, high)


def send_kernel(parts_ref, known_ref, from_ref, slots_ref, nodes_ref, places_ref, pay_ref, shift_ref):
    owners = pay_ref.shape[0]
    rows = places_ref.shape[1]
    slots, mids = owners * 16, owners * 8
    days = slots_ref.shape[0] - 8
    season_days = days * 2
    parts = parts_ref[...]
    quarter = places_ref[3:4, 0:128]
    own = jnp.sum(jnp.where(iota(parts.shape, 0) >> 1 == quarter[None], parts, 0.0), axis=0)
    total = jnp.sum(parts, axis=0)
    shift = known_ref[...] - (0.5 * own / season_days + 0.25 * total / (season_days * 4))
    shift_row = row_of(shift)
    shift_ref[...] = shift_row

    line, lane = from_ref[0, :, :], from_ref[1, :, :]
    moved = jnp.zeros(shift.shape, f32)
    for at in range(shift.shape[0]):
        taken = jnp.take_along_axis(
            jnp.broadcast_to(shift[at:at + 1, :], shift.shape), lane, axis=1, mode="promise_in_bounds"
        )
        moved = jnp.where(line == at, taken, moved)
    moved = row_of(moved)

    high = shift_row.astype(bf16).astype(f32)
    ext = jnp.concatenate([high, shift_row - high, jnp.zeros((14, rows), f32)], axis=0).astype(bf16)
    mid, top = places_ref[1:2, :], places_ref[2:3, :]
    width = min(128, mids)
    count = mids // width
    found = dot_nt(by_group(ext, mid // width, count), node_hits(mid, top, width))
    found = [jnp.sum(found[g * 16:(g + 1) * 16, :], axis=0, keepdims=True) for g in range(count)]
    node_sums = jnp.concatenate([part[:, :width] for part in found] + [sum(part[:, width:] for part in found)], axis=1)
    is_day = iota((days + 8, 1), 0) < days
    pad = jnp.zeros((8, rows + mids + TOP_ROWS), f32)
    sums = jnp.concatenate([slots_ref[...], nodes_ref[...]], axis=1)
    sums = sums + jnp.where(is_day, jnp.concatenate([moved, node_sums], axis=1), 0.0)
    sums = jnp.concatenate([sums, pad], axis=0)

    tops = split_count(sums[:, 2 * slots + mids:]).astype(bf16)
    tops = dot(tops, ones_where(iota((TOP_ROWS, slots), 0) == iota((TOP_ROWS, slots), 1) >> 4))
    row, column = iota((64, slots), 0), iota((64, slots), 1) & 15
    keep = (
        ((row < days) & (row // 3 == column))
        | ((row == ONE) & (column < 8))
        | ((row == LOW) & (column >= 8))
    )
    tops = jnp.where(keep, tops, 0.0).astype(bf16)
    lane, day = iota((128, 64), 0), iota((128, 64), 1)
    top_move = ((day < days) & (lane == top_lane(day))) | (((day == ONE) | (day == LOW)) & (lane == TOP_COUNT))
    tops = dot(ones_where(top_move), tops)
    tiles = jnp.concatenate([sums[:, :slots], sums[:, slots:2 * slots]], axis=0)
    tiles = jnp.where(slot_lanes((128, slots), 0), tiles, tops)

    half = days // 2
    mid_sums = split_count(sums[:, 2 * slots:2 * slots + mids])
    day, lane = iota((64, 128), 0), iota((64, 128), 1)
    moves = (
        ((day < half) & (lane == lane_of(day))) | ((day == ONE) & (lane == MID_COUNT)),
        ((day >= half) & (day < days) & (lane == lane_of(day - half))) | ((day == LOW) & (lane == MID_COUNT)),
    )
    moves = [ones_where(move) for move in moves]
    group = min(16, owners)
    for g in range(owners // group):
        own = jnp.transpose(mid_sums[:, g * group * 8:(g + 1) * group * 8]).astype(bf16)
        extra = jnp.concatenate([dot(own, move).reshape(group, 8, 128) for move in moves], axis=1)
        start, stop = g * group * 16, (g + 1) * group * 16
        tile = jnp.concatenate([jnp.transpose(tiles[:, at:at + 128]) for at in range(start, stop, 128)], axis=0)
        pay_ref[g * group:(g + 1) * group, :, :] = (tile.reshape(group, 16, 128) + extra).astype(bf16)


def owner_kernel(got_ref, base_fine_ref, base_rest_ref, back_ref):
    owners = got_ref.shape[0]
    days, nodes = base_fine_ref.shape
    got = got_ref[...].astype(f32)
    flat = got.reshape(owners * 16, 128)
    lanes = iota(flat.shape, 1)
    node = iota((owners * 16, nodes), 1).astype(f32)
    pick_low = ones_where(flat[:, ID:ID + 1] == node)
    pick_high = ones_where(flat[:, 64 + ID:65 + ID] == node)
    turned = jnp.transpose(jnp.where((lanes & 63) == ONE, 1.0, flat)).astype(bf16)
    totals = dot(turned[0:64, :], pick_low) + dot(turned[64:128, :], pick_high)
    gap = (base_fine_ref[...] - totals[0:days, :]) / (totals[ONE:ONE + 1, :] + 1.0)
    gap = jnp.concatenate([gap, jnp.zeros((64 - days, nodes), f32)], axis=0)
    gap = jnp.transpose(jnp.concatenate([gap, gap], axis=0)).astype(bf16)
    spread = jnp.where(lanes < 64, dot(pick_low, gap), dot(pick_high, gap))

    rest = jnp.sum(got, axis=0)
    pair = rest + jnp.concatenate([rest[8:16, :], rest[0:8, :]], axis=0)
    of_top = iota(rest.shape, 1) > MID_COUNT
    count = jnp.where(of_top, pair[:, TOP_COUNT:TOP_COUNT + 1], pair[:, MID_COUNT:MID_COUNT + 1])
    gap_rest = jnp.where(slot_lanes(rest.shape, 1), 0.0, (base_rest_ref[...] - rest) / (count + 1.0))
    spread = jnp.where(slot_lanes(flat.shape, 1), spread, 0.0).reshape(owners, 16, 128)
    back_ref[...] = (spread + gap_rest[None]).astype(bf16)


def finish_kernel(leaf_ref, shift_ref, places_ref, back_ref, out_ref, done_ref, sems):
    days, rows = leaf_ref.shape
    owners = back_ref.shape[0]
    slots, mids = owners * 16, owners * 8
    half = days // 2
    back = back_ref[...].astype(f32)
    day, lane = iota((days, 128), 0), iota((days, 128), 1)
    take = jnp.concatenate([ones_where(lane == day), ones_where(lane == day + 64), ones_where(lane == top_lane(day))], axis=0)
    taken = dot_nt(take, back.reshape(slots, 128).astype(bf16))
    tops = jnp.where(iota((days, slots), 0) // 3 == (iota((days, slots), 1) & 15), taken[2 * days:, :], 0.0).astype(bf16)
    tops = dot(tops, ones_where(iota((slots, TOP_ROWS), 0) >> 4 == iota((slots, TOP_ROWS), 1)))
    first, last = (back[:, at:at + 8, :].reshape(mids, 128).astype(bf16) for at in (0, 8))
    mid = dot_nt(ones_where((day < half) & (lane == lane_of(day))), first)
    mid = mid + dot_nt(ones_where((day >= half) & (lane == lane_of(day - half))), last)
    slot_count, width = rows // 256, min(128, mids)
    mid_count = mids // width
    taken = jnp.concatenate([taken[:days, :], taken[days:2 * days, :]], axis=1)
    slot_gaps = jnp.concatenate([taken[:, g * 256:(g + 1) * 256] for g in range(slot_count)], axis=0).astype(bf16)
    node_gaps = [jnp.concatenate([mid[:, g * width:(g + 1) * width], tops], axis=1) for g in range(mid_count)]
    node_gaps = jnp.concatenate(node_gaps, axis=0).astype(bf16)
    step = min(512, rows)
    copies = []
    for at in range(0, rows, step):
        place, mid, top = (places_ref[k:k + 1, at:at + step] for k in range(3))
        out = leaf_ref[:, at:at + step] + shift_ref[:, at:at + step]
        for gaps, hit, group, count in (
            (slot_gaps, hits(place & 255, 256), place >> 8, slot_count),
            (node_gaps, node_hits(mid, top, width), mid // width, mid_count),
        ):
            found = dot(gaps, hit)
            chosen = found[:days, :]
            for g in range(1, count):
                chosen = jnp.where(group == g, found[g * days:(g + 1) * days, :], chosen)
            out = out + chosen
        done_ref[:, at:at + step] = out
        copies.append(pltpu.make_async_copy(done_ref.at[:, at:at + step], out_ref.at[:, at:at + step], sems.at[at // step]))
        copies[-1].start()
    for copy in copies:
        copy.wait()


def per_device(leaf, seas, fine, mid, top, base_fine, base_mid, base_top):
    days, rows = leaf.shape
    owners = lax.axis_size("series")
    blocks = lax.axis_size("tm")
    quarter = (lax.axis_index("tm") // (blocks // 4)).astype(i32).reshape(1)
    vmem = pl.BlockSpec(memory_space=pltpu.VMEM)
    smem = pl.BlockSpec(memory_space=pltpu.SMEM)
    dense = (rows // 128, 128)

    sums = pl.pallas_call(
        start_kernel, out_shape=jax.ShapeDtypeStruct((blocks,) + dense, f32), compiler_params=PARAMS, name="day_sums"
    )(leaf)
    parts = lax.all_to_all(sums, "tm", 0, 0, tiled=True)
    slots, nodes, places, come_from, base_rest, known = pl.pallas_call(
        lambda *refs: sort_kernel(owners, *refs),
        out_shape=(
            jax.ShapeDtypeStruct((days + 8, rows), f32),
            jax.ShapeDtypeStruct((days + 8, owners * 8 + TOP_ROWS), f32),
            jax.ShapeDtypeStruct((4, rows), i32),
            jax.ShapeDtypeStruct((2,) + dense, i32),
            jax.ShapeDtypeStruct((16, 128), f32),
            jax.ShapeDtypeStruct(dense, f32),
        ),
        in_specs=[smem] + [vmem] * 7,
        compiler_params=PARAMS,
        cost_estimate=pl.CostEstimate(flops=2 * 104 * owners * 42 * rows, bytes_accessed=4 * days * rows, transcendentals=0),
        name="sort",
    )(quarter, *(ids.reshape(1, rows) for ids in (fine, mid, top)), base_mid.T, base_top.reshape(1, days), seas, leaf)

    payload, shift = pl.pallas_call(
        send_kernel,
        out_shape=(jax.ShapeDtypeStruct((owners, 16, 128), bf16), jax.ShapeDtypeStruct((1, rows), f32)),
        compiler_params=PARAMS,
        name="pack",
    )(parts, known, come_from, slots, nodes, places)
    got = lax.all_to_all(payload, "series", 0, 0, tiled=True)
    back = pl.pallas_call(
        owner_kernel,
        out_shape=jax.ShapeDtypeStruct((owners, 16, 128), bf16),
        compiler_params=PARAMS,
        name="gaps",
    )(got, base_fine, base_rest)
    back = lax.all_to_all(back, "series", 0, 0, tiled=True)
    return pl.pallas_call(
        finish_kernel,
        out_shape=jax.ShapeDtypeStruct((days, rows), f32),
        in_specs=[vmem] * 4,
        out_specs=pl.BlockSpec(memory_space=pl.ANY),
        scratch_shapes=[pltpu.VMEM((days, rows), f32), pltpu.SemaphoreType.DMA((max(1, rows // 512),))],
        compiler_params=PARAMS,
        name="finish",
    )(leaf, shift, places, back)


def solution(mesh):
    return jax.shard_map(
        per_device,
        mesh=mesh,
        in_specs=(
            P("tm", "series"),
            P(None, "series"),
            P("series", None),
            P("series", None),
            P("series", None),
            P("tm", "series"),
            P("tm", "series"),
            P("tm", "series"),
        ),
        out_specs=P("tm", "series"),
        check_vma=False,
    )
```

```python
import jax
import jax.numpy as jnp
from jax import lax
from jax.experimental import pallas as pl
from jax.experimental.pallas import tpu as pltpu
from jax.sharding import PartitionSpec as P

f32 = jnp.float32
bf16 = jnp.bfloat16
i32 = jnp.int32

PARAMS = pltpu.CompilerParams(vmem_limit_bytes=24 * 1024 * 1024)

ID = 48
ONE = 49
LOW = 50
MID_COUNT = 122
TOP_COUNT = 126
TOP_ROWS = 128


def iota(shape, dim):
    return lax.broadcasted_iota(i32, shape, dim)


def lane_of(x):
    return jnp.where(x < 15, x + 49, x + 98)


def top_lane(day):
    return lane_of(25 + day - 3 * (day // 3))


def ones_where(mask):
    return jnp.where(mask, 1.0, 0.0).astype(bf16)


def hits(codes, height):
    row = iota((height, 128), 0).astype(f32).astype(bf16)
    row = jnp.concatenate([row] * (codes.shape[1] // 128), axis=1)
    return jnp.where(row == codes.astype(f32).astype(bf16), jnp.ones((), bf16), jnp.zeros((), bf16))


def node_hits(mid, top, width):
    return jnp.concatenate([hits(mid & (width - 1), width), hits(top, TOP_ROWS)], axis=0)


def by_group(rows, group, count):
    return jnp.concatenate([rows * ones_where(group == g) for g in range(count)], axis=0)


def dot(a, b):
    return jnp.dot(a, b, preferred_element_type=f32)


def dot_nt(a, b, precision=None):
    return lax.dot_general(a, b, (((1,), (1,)), ((), ())), precision=precision, preferred_element_type=f32)


def slot_lanes(shape, dim):
    return (iota(shape, dim) & 63) <= ID


def row_of(dense):
    return jnp.concatenate([dense[at:at + 1, :] for at in range(dense.shape[0])], axis=1)


def dense_of(row):
    return jnp.concatenate([row[:, at:at + 128] for at in range(0, row.shape[1], 128)], axis=0)


def start_kernel(leaf_ref, sums_ref):
    sums = dense_of(jnp.sum(leaf_ref[...], axis=0, keepdims=True))
    sums_ref[...] = jnp.broadcast_to(sums[None], sums_ref.shape)


def ranks_of(owner, owners):
    rows = owner.shape[1]
    step = min(256, rows)
    before = ones_where(iota((step, step), 0) < iota((step, step), 1))
    base = jnp.zeros((owners, 1), f32)
    ranks = []
    for at in range(0, rows, step):
        hit = owner[:, at:at + step] == iota((owners, step), 0)
        hit_f = jnp.where(hit, 1.0, 0.0)
        seen = dot(hit_f.astype(bf16), before) + base
        ranks.append(jnp.sum(jnp.where(hit, seen, 0.0), axis=0, keepdims=True))
        base = base + jnp.sum(hit_f, axis=1, keepdims=True)
    return jnp.concatenate(ranks, axis=1).astype(i32)


def sort_kernel(
    owners, quarter_ref, fine_ref, mid_ref, top_ref, base_mid_ref, base_top_ref, seas_ref, leaf_ref,
    parts_ref, slots_ref, nodes_ref, places_ref, from_ref, rest_ref, known_ref,
):
    days, rows = leaf_ref.shape
    fine, mid, top = fine_ref[...], mid_ref[...], top_ref[...]
    owner = fine >> 6
    rank = ranks_of(owner, owners)
    place = (rank >> 4) * (owners * 16) + owner * 16 + (rank & 15)
    places_ref[0:1, :] = place
    places_ref[1:2, :] = mid
    places_ref[2:3, :] = top
    places_ref[3:4, :] = jnp.zeros_like(mid) + quarter_ref[0]

    leaf = leaf_ref[...]
    high = leaf.astype(bf16).astype(f32)
    series = iota((1, rows), 1)
    ones = jnp.ones((1, rows), f32)
    known = [(fine & 63).astype(f32), ones, ones, (series >> 7).astype(f32), (series & 127).astype(f32)]
    zeros = [jnp.zeros((3, rows), f32), jnp.zeros((8, rows), f32)]
    ext = jnp.concatenate([high] + known + [zeros[0], leaf - high, zeros[1]], axis=0).astype(bf16)
    height = days + 8

    def add_low(part):
        return part[:height, :] + jnp.concatenate([part[height:height + days, :], jnp.zeros((8, part.shape[1]), f32)], axis=0)

    count = rows // 256
    sums = dot_nt(by_group(ext, place >> 8, count), hits(place & 255, 256))
    for g in range(count):
        slots_ref[:, g * 256:(g + 1) * 256] = add_low(sums[g * 2 * height:(g + 1) * 2 * height, :])
    mids = owners * 8
    width = min(128, mids)
    count = mids // width
    sums = dot_nt(by_group(ext, mid // width, count), node_hits(mid, top, width))
    tops = jnp.zeros((height, TOP_ROWS), f32)
    for g in range(count):
        part = add_low(sums[g * 2 * height:(g + 1) * 2 * height, :])
        nodes_ref[:, g * width:(g + 1) * width] = part[:, :width]
        tops = tops + part[:, width:]
    nodes_ref[:, mids:] = tops
    from_ref[0, :, :] = dense_of(slots_ref[LOW + 1:LOW + 2, :]).astype(i32)
    from_ref[1, :, :] = dense_of(slots_ref[LOW + 2:LOW + 3, :]).astype(i32)
    seas = seas_ref[...]
    season_days = days * 2
    line = iota(seas.shape, 0)
    seas_own = jnp.sum(jnp.where(line == quarter_ref[0], seas, 0.0), axis=0, keepdims=True)
    seas_four = jnp.sum(jnp.where(line < 4, seas, 0.0), axis=0, keepdims=True)
    parts = parts_ref[...]
    own = jnp.sum(jnp.where(iota(parts.shape, 0) >> 1 == quarter_ref[0], parts, 0.0), axis=0)
    total = jnp.sum(parts, axis=0)
    known = dense_of(0.5 * seas_own / season_days + 0.5 * (seas[4:5, :] - 0.5 * seas_four) / (season_days * 4))
    known_ref[...] = known - (0.5 * own / season_days + 0.25 * total / (season_days * 4))
    rest_ref[...] = rest_in_lanes(base_mid_ref[...], base_top_ref[...])


def rest_in_lanes(base_mid, base_top):
    days = base_mid.shape[1]
    half = days // 2
    day, lane = iota((days, 128), 0), iota((days, 128), 1)
    moves = (
        (day < half) & (lane == lane_of(day)),
        (day >= half) & (lane == lane_of(day - half)),
        lane == top_lane(day),
    )
    moves = [jnp.where(move, 1.0, 0.0) for move in moves]
    top = jnp.where(iota((16, days), 1) // 3 == iota((16, days), 0), base_top, 0.0)
    exact = lax.Precision.HIGHEST
    mids = [jnp.dot(base_mid, move, precision=exact, preferred_element_type=f32) for move in moves[:2]]
    return jnp.concatenate(mids, axis=0) + jnp.dot(top, moves[2], precision=exact, preferred_element_type=f32)


def split_count(sums):
    high = sums.astype(bf16).astype(f32)
    return jnp.where(iota(sums.shape, 0) == LOW, sums - high, high)


def send_kernel(shift_ref, from_ref, slots_ref, nodes_ref, places_ref, pay_ref, row_ref):
    owners = pay_ref.shape[0]
    rows = places_ref.shape[1]
    slots, mids = owners * 16, owners * 8
    days = slots_ref.shape[0] - 8
    shift = shift_ref[...]
    shift_row = row_of(shift)
    row_ref[...] = shift_row

    line, lane = from_ref[0, :, :], from_ref[1, :, :]
    moved = jnp.zeros(shift.shape, f32)
    for at in range(shift.shape[0]):
        taken = jnp.take_along_axis(
            jnp.broadcast_to(shift[at:at + 1, :], shift.shape), lane, axis=1, mode="promise_in_bounds"
        )
        moved = jnp.where(line == at, taken, moved)
    moved = row_of(moved)

    high = shift_row.astype(bf16).astype(f32)
    ext = jnp.concatenate([high, shift_row - high, jnp.zeros((14, rows), f32)], axis=0).astype(bf16)
    mid, top = places_ref[1:2, :], places_ref[2:3, :]
    width = min(128, mids)
    count = mids // width
    found = dot_nt(by_group(ext, mid // width, count), node_hits(mid, top, width))
    found = [jnp.sum(found[g * 16:(g + 1) * 16, :], axis=0, keepdims=True) for g in range(count)]
    node_sums = jnp.concatenate([part[:, :width] for part in found] + [sum(part[:, width:] for part in found)], axis=1)
    is_day = iota((days + 8, 1), 0) < days
    pad = jnp.zeros((8, rows + mids + TOP_ROWS), f32)
    sums = jnp.concatenate([slots_ref[...], nodes_ref[...]], axis=1)
    sums = sums + jnp.where(is_day, jnp.concatenate([moved, node_sums], axis=1), 0.0)
    sums = jnp.concatenate([sums, pad], axis=0)

    tops = split_count(sums[:, 2 * slots + mids:]).astype(bf16)
    tops = dot(tops, ones_where(iota((TOP_ROWS, slots), 0) == iota((TOP_ROWS, slots), 1) >> 4))
    row, column = iota((64, slots), 0), iota((64, slots), 1) & 15
    keep = (
        ((row < days) & (row // 3 == column))
        | ((row == ONE) & (column < 8))
        | ((row == LOW) & (column >= 8))
    )
    tops = jnp.where(keep, tops, 0.0).astype(bf16)
    lane, day = iota((128, 64), 0), iota((128, 64), 1)
    top_move = ((day < days) & (lane == top_lane(day))) | (((day == ONE) | (day == LOW)) & (lane == TOP_COUNT))
    tops = dot(ones_where(top_move), tops)
    tiles = jnp.concatenate([sums[:, :slots], sums[:, slots:2 * slots]], axis=0)
    tiles = jnp.where(slot_lanes((128, slots), 0), tiles, tops)

    half = days // 2
    mid_sums = split_count(sums[:, 2 * slots:2 * slots + mids])
    day, lane = iota((64, 128), 0), iota((64, 128), 1)
    moves = (
        ((day < half) & (lane == lane_of(day))) | ((day == ONE) & (lane == MID_COUNT)),
        ((day >= half) & (day < days) & (lane == lane_of(day - half))) | ((day == LOW) & (lane == MID_COUNT)),
    )
    moves = [ones_where(move) for move in moves]
    group = min(16, owners)
    for g in range(owners // group):
        own = jnp.transpose(mid_sums[:, g * group * 8:(g + 1) * group * 8]).astype(bf16)
        extra = jnp.concatenate([dot(own, move).reshape(group, 8, 128) for move in moves], axis=1)
        start, stop = g * group * 16, (g + 1) * group * 16
        tile = jnp.concatenate([jnp.transpose(tiles[:, at:at + 128]) for at in range(start, stop, 128)], axis=0)
        pay_ref[g * group:(g + 1) * group, :, :] = (tile.reshape(group, 16, 128) + extra).astype(bf16)


def owner_kernel(got_ref, base_fine_ref, base_rest_ref, back_ref):
    owners = got_ref.shape[0]
    days, nodes = base_fine_ref.shape
    got = got_ref[...].astype(f32)
    flat = got.reshape(owners * 16, 128)
    lanes = iota(flat.shape, 1)
    node = iota((owners * 16, nodes), 1).astype(f32)
    pick_low = ones_where(flat[:, ID:ID + 1] == node)
    pick_high = ones_where(flat[:, 64 + ID:65 + ID] == node)
    turned = jnp.transpose(jnp.where((lanes & 63) == ONE, 1.0, flat)).astype(bf16)
    totals = dot(turned[0:64, :], pick_low) + dot(turned[64:128, :], pick_high)
    gap = (base_fine_ref[...] - totals[0:days, :]) / (totals[ONE:ONE + 1, :] + 1.0)
    gap = jnp.concatenate([gap, jnp.zeros((64 - days, nodes), f32)], axis=0)
    gap = jnp.transpose(jnp.concatenate([gap, gap], axis=0)).astype(bf16)
    spread = jnp.where(lanes < 64, dot(pick_low, gap), dot(pick_high, gap))

    rest = jnp.sum(got, axis=0)
    pair = rest + jnp.concatenate([rest[8:16, :], rest[0:8, :]], axis=0)
    of_top = iota(rest.shape, 1) > MID_COUNT
    count = jnp.where(of_top, pair[:, TOP_COUNT:TOP_COUNT + 1], pair[:, MID_COUNT:MID_COUNT + 1])
    gap_rest = jnp.where(slot_lanes(rest.shape, 1), 0.0, (base_rest_ref[...] - rest) / (count + 1.0))
    spread = jnp.where(slot_lanes(flat.shape, 1), spread, 0.0).reshape(owners, 16, 128)
    back_ref[...] = (spread + gap_rest[None]).astype(bf16)


def finish_kernel(leaf_ref, shift_ref, places_ref, back_ref, out_ref, done_ref, sems):
    days, rows = leaf_ref.shape
    owners = back_ref.shape[0]
    slots, mids = owners * 16, owners * 8
    half = days // 2
    back = back_ref[...].astype(f32)
    day, lane = iota((days, 128), 0), iota((days, 128), 1)
    take = jnp.concatenate([ones_where(lane == day), ones_where(lane == day + 64), ones_where(lane == top_lane(day))], axis=0)
    taken = dot_nt(take, back.reshape(slots, 128).astype(bf16))
    tops = jnp.where(iota((days, slots), 0) // 3 == (iota((days, slots), 1) & 15), taken[2 * days:, :], 0.0).astype(bf16)
    tops = dot(tops, ones_where(iota((slots, TOP_ROWS), 0) >> 4 == iota((slots, TOP_ROWS), 1)))
    first, last = (back[:, at:at + 8, :].reshape(mids, 128).astype(bf16) for at in (0, 8))
    mid = dot_nt(ones_where((day < half) & (lane == lane_of(day))), first)
    mid = mid + dot_nt(ones_where((day >= half) & (lane == lane_of(day - half))), last)
    slot_count, width = rows // 256, min(128, mids)
    mid_count = mids // width
    taken = jnp.concatenate([taken[:days, :], taken[days:2 * days, :]], axis=1)
    slot_gaps = jnp.concatenate([taken[:, g * 256:(g + 1) * 256] for g in range(slot_count)], axis=0).astype(bf16)
    node_gaps = [jnp.concatenate([mid[:, g * width:(g + 1) * width], tops], axis=1) for g in range(mid_count)]
    node_gaps = jnp.concatenate(node_gaps, axis=0).astype(bf16)
    step = min(512, rows)
    copies = []
    for at in range(0, rows, step):
        place, mid, top = (places_ref[k:k + 1, at:at + step] for k in range(3))
        out = leaf_ref[:, at:at + step] + shift_ref[:, at:at + step]
        for gaps, hit, group, count in (
            (slot_gaps, hits(place & 255, 256), place >> 8, slot_count),
            (node_gaps, node_hits(mid, top, width), mid // width, mid_count),
        ):
            found = dot(gaps, hit)
            chosen = found[:days, :]
            for g in range(1, count):
                chosen = jnp.where(group == g, found[g * days:(g + 1) * days, :], chosen)
            out = out + chosen
        done_ref[:, at:at + step] = out
        copies.append(pltpu.make_async_copy(done_ref.at[:, at:at + step], out_ref.at[:, at:at + step], sems.at[at // step]))
        copies[-1].start()
    for copy in copies:
        copy.wait()


def per_device(leaf, seas, fine, mid, top, base_fine, base_mid, base_top):
    days, rows = leaf.shape
    owners = lax.axis_size("series")
    blocks = lax.axis_size("tm")
    quarter = (lax.axis_index("tm") // (blocks // 4)).astype(i32).reshape(1)
    vmem = pl.BlockSpec(memory_space=pltpu.VMEM)
    smem = pl.BlockSpec(memory_space=pltpu.SMEM)
    dense = (rows // 128, 128)

    sums = pl.pallas_call(
        start_kernel, out_shape=jax.ShapeDtypeStruct((blocks,) + dense, f32), compiler_params=PARAMS, name="day_sums"
    )(leaf)
    parts = lax.all_to_all(sums, "tm", 0, 0, tiled=True)
    slots, nodes, places, come_from, base_rest, known = pl.pallas_call(
        lambda *refs: sort_kernel(owners, *refs),
        out_shape=(
            jax.ShapeDtypeStruct((days + 8, rows), f32),
            jax.ShapeDtypeStruct((days + 8, owners * 8 + TOP_ROWS), f32),
            jax.ShapeDtypeStruct((4, rows), i32),
            jax.ShapeDtypeStruct((2,) + dense, i32),
            jax.ShapeDtypeStruct((16, 128), f32),
            jax.ShapeDtypeStruct(dense, f32),
        ),
        in_specs=[smem] + [vmem] * 8,
        compiler_params=PARAMS,
        cost_estimate=pl.CostEstimate(flops=2 * 104 * owners * 42 * rows, bytes_accessed=4 * days * rows, transcendentals=0),
        name="sort",
    )(quarter, *(ids.reshape(1, rows) for ids in (fine, mid, top)), base_mid.T, base_top.reshape(1, days), seas, leaf, parts)

    payload, shift = pl.pallas_call(
        send_kernel,
        out_shape=(jax.ShapeDtypeStruct((owners, 16, 128), bf16), jax.ShapeDtypeStruct((1, rows), f32)),
        compiler_params=PARAMS,
        name="pack",
    )(known, come_from, slots, nodes, places)
    got = lax.all_to_all(payload, "series", 0, 0, tiled=True)
    back = pl.pallas_call(
        owner_kernel,
        out_shape=jax.ShapeDtypeStruct((owners, 16, 128), bf16),
        compiler_params=PARAMS,
        name="gaps",
    )(got, base_fine, base_rest)
    back = lax.all_to_all(back, "series", 0, 0, tiled=True)
    return pl.pallas_call(
        finish_kernel,
        out_shape=jax.ShapeDtypeStruct((days, rows), f32),
        in_specs=[vmem] * 4,
        out_specs=pl.BlockSpec(memory_space=pl.ANY),
        scratch_shapes=[pltpu.VMEM((days, rows), f32), pltpu.SemaphoreType.DMA((max(1, rows // 512),))],
        compiler_params=PARAMS,
        name="finish",
    )(leaf, shift, places, back)


def solution(mesh):
    return jax.shard_map(
        per_device,
        mesh=mesh,
        in_specs=(
            P("tm", "series"),
            P(None, "series"),
            P("series", None),
            P("series", None),
            P("series", None),
            P("tm", "series"),
            P("tm", "series"),
            P("tm", "series"),
        ),
        out_specs=P("tm", "series"),
        check_vma=False,
    )
```

```python
import jax
import jax.numpy as jnp
from jax import lax
from jax.experimental import pallas as pl
from jax.experimental.pallas import tpu as pltpu
from jax.sharding import PartitionSpec as P

f32 = jnp.float32
bf16 = jnp.bfloat16
i32 = jnp.int32

PARAMS = pltpu.CompilerParams(vmem_limit_bytes=24 * 1024 * 1024)

ID = 48
ONE = 49
LOW = 50
MID_COUNT = 122
TOP_COUNT = 126
TOP_ROWS = 128


def iota(shape, dim):
    return lax.broadcasted_iota(i32, shape, dim)


def lane_of(x):
    return jnp.where(x < 15, x + 49, x + 98)


def top_lane(day):
    return lane_of(25 + day - 3 * (day // 3))


def ones_where(mask):
    return jnp.where(mask, 1.0, 0.0).astype(bf16)


def hits(codes, height):
    row = iota((height, 128), 0).astype(f32).astype(bf16)
    row = jnp.concatenate([row] * (codes.shape[1] // 128), axis=1)
    return jnp.where(row == codes.astype(f32).astype(bf16), jnp.ones((), bf16), jnp.zeros((), bf16))


def node_hits(mid, top, width):
    return jnp.concatenate([hits(mid & (width - 1), width), hits(top, TOP_ROWS)], axis=0)


def by_group(rows, group, count):
    return jnp.concatenate([rows * ones_where(group == g) for g in range(count)], axis=0)


def dot(a, b):
    return jnp.dot(a, b, preferred_element_type=f32)


def dot_nt(a, b, precision=None):
    return lax.dot_general(a, b, (((1,), (1,)), ((), ())), precision=precision, preferred_element_type=f32)


def slot_lanes(shape, dim):
    return (iota(shape, dim) & 63) <= ID


def row_of(dense):
    return jnp.concatenate([dense[at:at + 1, :] for at in range(dense.shape[0])], axis=1)


def dense_of(row):
    return jnp.concatenate([row[:, at:at + 128] for at in range(0, row.shape[1], 128)], axis=0)


def start_kernel(leaf_ref, sums_ref, here_ref, sems):
    strips = range(0, leaf_ref.shape[0], 8)
    copies = [
        pltpu.make_async_copy(leaf_ref.at[at:at + 8, :], here_ref.at[at:at + 8, :], sems.at[at // 8]) for at in strips
    ]
    for copy in copies:
        copy.start()
    total = jnp.zeros((8, leaf_ref.shape[1]), f32)
    for at, copy in zip(strips, copies):
        copy.wait()
        total = total + here_ref[at:at + 8, :]
    sums = dense_of(jnp.sum(total, axis=0, keepdims=True))
    sums_ref[...] = jnp.broadcast_to(sums[None], sums_ref.shape)


def ranks_of(owner, owners):
    rows = owner.shape[1]
    step = min(256, rows)
    before = ones_where(iota((step, step), 0) < iota((step, step), 1))
    base = jnp.zeros((owners, 1), f32)
    ranks = []
    for at in range(0, rows, step):
        hit = owner[:, at:at + step] == iota((owners, step), 0)
        hit_f = jnp.where(hit, 1.0, 0.0)
        seen = dot(hit_f.astype(bf16), before) + base
        ranks.append(jnp.sum(jnp.where(hit, seen, 0.0), axis=0, keepdims=True))
        base = base + jnp.sum(hit_f, axis=1, keepdims=True)
    return jnp.concatenate(ranks, axis=1).astype(i32)


def sort_kernel(
    owners, quarter_ref, fine_ref, mid_ref, top_ref, base_mid_ref, base_top_ref, seas_ref, leaf_ref,
    slots_ref, nodes_ref, places_ref, from_ref, rest_ref, known_ref,
):
    days, rows = leaf_ref.shape
    fine, mid, top = fine_ref[...], mid_ref[...], top_ref[...]
    owner = fine >> 6
    rank = ranks_of(owner, owners)
    place = (rank >> 4) * (owners * 16) + owner * 16 + (rank & 15)
    places_ref[0:1, :] = place
    places_ref[1:2, :] = mid
    places_ref[2:3, :] = top
    places_ref[3:4, :] = jnp.zeros_like(mid) + quarter_ref[0]

    leaf = leaf_ref[...]
    high = leaf.astype(bf16).astype(f32)
    series = iota((1, rows), 1)
    ones = jnp.ones((1, rows), f32)
    known = [(fine & 63).astype(f32), ones, ones, (series >> 7).astype(f32), (series & 127).astype(f32)]
    zeros = [jnp.zeros((3, rows), f32), jnp.zeros((8, rows), f32)]
    ext = jnp.concatenate([high] + known + [zeros[0], leaf - high, zeros[1]], axis=0).astype(bf16)
    height = days + 8

    def add_low(part):
        return part[:height, :] + jnp.concatenate([part[height:height + days, :], jnp.zeros((8, part.shape[1]), f32)], axis=0)

    count = rows // 256
    sums = dot_nt(by_group(ext, place >> 8, count), hits(place & 255, 256))
    for g in range(count):
        slots_ref[:, g * 256:(g + 1) * 256] = add_low(sums[g * 2 * height:(g + 1) * 2 * height, :])
    mids = owners * 8
    width = min(128, mids)
    count = mids // width
    sums = dot_nt(by_group(ext, mid // width, count), node_hits(mid, top, width))
    tops = jnp.zeros((height, TOP_ROWS), f32)
    for g in range(count):
        part = add_low(sums[g * 2 * height:(g + 1) * 2 * height, :])
        nodes_ref[:, g * width:(g + 1) * width] = part[:, :width]
        tops = tops + part[:, width:]
    nodes_ref[:, mids:] = tops
    from_ref[0, :, :] = dense_of(slots_ref[LOW + 1:LOW + 2, :]).astype(i32)
    from_ref[1, :, :] = dense_of(slots_ref[LOW + 2:LOW + 3, :]).astype(i32)
    seas = seas_ref[...]
    season_days = days * 2
    line = iota(seas.shape, 0)
    seas_own = jnp.sum(jnp.where(line == quarter_ref[0], seas, 0.0), axis=0, keepdims=True)
    seas_four = jnp.sum(jnp.where(line < 4, seas, 0.0), axis=0, keepdims=True)
    known_ref[...] = dense_of(0.5 * seas_own / season_days + 0.5 * (seas[4:5, :] - 0.5 * seas_four) / (season_days * 4))
    rest_ref[...] = rest_in_lanes(base_mid_ref[...], base_top_ref[...])


def rest_in_lanes(base_mid, base_top):
    days = base_mid.shape[1]
    half = days // 2
    day, lane = iota((days, 128), 0), iota((days, 128), 1)
    moves = (
        (day < half) & (lane == lane_of(day)),
        (day >= half) & (lane == lane_of(day - half)),
        lane == top_lane(day),
    )
    moves = [jnp.where(move, 1.0, 0.0) for move in moves]
    top = jnp.where(iota((16, days), 1) // 3 == iota((16, days), 0), base_top, 0.0)
    exact = lax.Precision.HIGHEST
    mids = [jnp.dot(base_mid, move, precision=exact, preferred_element_type=f32) for move in moves[:2]]
    return jnp.concatenate(mids, axis=0) + jnp.dot(top, moves[2], precision=exact, preferred_element_type=f32)


def split_count(sums):
    high = sums.astype(bf16).astype(f32)
    return jnp.where(iota(sums.shape, 0) == LOW, sums - high, high)


def send_kernel(parts_ref, known_ref, from_ref, slots_ref, nodes_ref, places_ref, pay_ref, shift_ref):
    owners = pay_ref.shape[0]
    rows = places_ref.shape[1]
    slots, mids = owners * 16, owners * 8
    days = slots_ref.shape[0] - 8
    season_days = days * 2
    parts = parts_ref[...]
    quarter = places_ref[3:4, 0:128]
    own = jnp.sum(jnp.where(iota(parts.shape, 0) >> 1 == quarter[None], parts, 0.0), axis=0)
    total = jnp.sum(parts, axis=0)
    shift = known_ref[...] - (0.5 * own / season_days + 0.25 * total / (season_days * 4))
    shift_row = row_of(shift)
    shift_ref[...] = shift_row

    line, lane = from_ref[0, :, :], from_ref[1, :, :]
    moved = jnp.zeros(shift.shape, f32)
    for at in range(shift.shape[0]):
        taken = jnp.take_along_axis(
            jnp.broadcast_to(shift[at:at + 1, :], shift.shape), lane, axis=1, mode="promise_in_bounds"
        )
        moved = jnp.where(line == at, taken, moved)
    moved = row_of(moved)

    high = shift_row.astype(bf16).astype(f32)
    ext = jnp.concatenate([high, shift_row - high, jnp.zeros((14, rows), f32)], axis=0).astype(bf16)
    mid, top = places_ref[1:2, :], places_ref[2:3, :]
    width = min(128, mids)
    count = mids // width
    found = dot_nt(by_group(ext, mid // width, count), node_hits(mid, top, width))
    found = [jnp.sum(found[g * 16:(g + 1) * 16, :], axis=0, keepdims=True) for g in range(count)]
    node_sums = jnp.concatenate([part[:, :width] for part in found] + [sum(part[:, width:] for part in found)], axis=1)
    is_day = iota((days + 8, 1), 0) < days
    pad = jnp.zeros((8, rows + mids + TOP_ROWS), f32)
    sums = jnp.concatenate([slots_ref[...], nodes_ref[...]], axis=1)
    sums = sums + jnp.where(is_day, jnp.concatenate([moved, node_sums], axis=1), 0.0)
    sums = jnp.concatenate([sums, pad], axis=0)

    tops = split_count(sums[:, 2 * slots + mids:]).astype(bf16)
    tops = dot(tops, ones_where(iota((TOP_ROWS, slots), 0) == iota((TOP_ROWS, slots), 1) >> 4))
    row, column = iota((64, slots), 0), iota((64, slots), 1) & 15
    keep = (
        ((row < days) & (row // 3 == column))
        | ((row == ONE) & (column < 8))
        | ((row == LOW) & (column >= 8))
    )
    tops = jnp.where(keep, tops, 0.0).astype(bf16)
    lane, day = iota((128, 64), 0), iota((128, 64), 1)
    top_move = ((day < days) & (lane == top_lane(day))) | (((day == ONE) | (day == LOW)) & (lane == TOP_COUNT))
    tops = dot(ones_where(top_move), tops)
    tiles = jnp.concatenate([sums[:, :slots], sums[:, slots:2 * slots]], axis=0)
    tiles = jnp.where(slot_lanes((128, slots), 0), tiles, tops)

    half = days // 2
    mid_sums = split_count(sums[:, 2 * slots:2 * slots + mids])
    day, lane = iota((64, 128), 0), iota((64, 128), 1)
    moves = (
        ((day < half) & (lane == lane_of(day))) | ((day == ONE) & (lane == MID_COUNT)),
        ((day >= half) & (day < days) & (lane == lane_of(day - half))) | ((day == LOW) & (lane == MID_COUNT)),
    )
    moves = [ones_where(move) for move in moves]
    group = min(16, owners)
    for g in range(owners // group):
        own = jnp.transpose(mid_sums[:, g * group * 8:(g + 1) * group * 8]).astype(bf16)
        extra = jnp.concatenate([dot(own, move).reshape(group, 8, 128) for move in moves], axis=1)
        start, stop = g * group * 16, (g + 1) * group * 16
        tile = jnp.concatenate([jnp.transpose(tiles[:, at:at + 128]) for at in range(start, stop, 128)], axis=0)
        pay_ref[g * group:(g + 1) * group, :, :] = (tile.reshape(group, 16, 128) + extra).astype(bf16)


def owner_kernel(got_ref, base_fine_ref, base_rest_ref, back_ref):
    owners = got_ref.shape[0]
    days, nodes = base_fine_ref.shape
    got = got_ref[...].astype(f32)
    flat = got.reshape(owners * 16, 128)
    lanes = iota(flat.shape, 1)
    node = iota((owners * 16, nodes), 1).astype(f32)
    pick_low = ones_where(flat[:, ID:ID + 1] == node)
    pick_high = ones_where(flat[:, 64 + ID:65 + ID] == node)
    same = ones_where(iota((128, 128), 0) == iota((128, 128), 1))
    turned = dot_nt(same, jnp.where((lanes & 63) == ONE, 1.0, flat).astype(bf16)).astype(bf16)
    totals = dot(turned[0:64, :], pick_low) + dot(turned[64:128, :], pick_high)
    gap = (base_fine_ref[...] - totals[0:days, :]) / (totals[ONE:ONE + 1, :] + 1.0)
    gap = jnp.concatenate([gap, jnp.zeros((64 - days, nodes), f32)], axis=0)
    gap = jnp.transpose(jnp.concatenate([gap, gap], axis=0)).astype(bf16)
    spread = jnp.where(lanes < 64, dot(pick_low, gap), dot(pick_high, gap))

    rest = jnp.sum(got, axis=0)
    pair = rest + jnp.concatenate([rest[8:16, :], rest[0:8, :]], axis=0)
    of_top = iota(rest.shape, 1) > MID_COUNT
    count = jnp.where(of_top, pair[:, TOP_COUNT:TOP_COUNT + 1], pair[:, MID_COUNT:MID_COUNT + 1])
    gap_rest = jnp.where(slot_lanes(rest.shape, 1), 0.0, (base_rest_ref[...] - rest) / (count + 1.0))
    spread = jnp.where(slot_lanes(flat.shape, 1), spread, 0.0).reshape(owners, 16, 128)
    back_ref[...] = (spread + gap_rest[None]).astype(bf16)


def finish_kernel(leaf_ref, shift_ref, places_ref, back_ref, out_ref, done_ref, sems):
    days, rows = leaf_ref.shape
    owners = back_ref.shape[0]
    slots, mids = owners * 16, owners * 8
    half = days // 2
    back = back_ref[...].astype(f32)
    day, lane = iota((days, 128), 0), iota((days, 128), 1)
    take = jnp.concatenate([ones_where(lane == day), ones_where(lane == day + 64), ones_where(lane == top_lane(day))], axis=0)
    taken = dot_nt(take, back.reshape(slots, 128).astype(bf16))
    tops = jnp.where(iota((days, slots), 0) // 3 == (iota((days, slots), 1) & 15), taken[2 * days:, :], 0.0).astype(bf16)
    tops = dot(tops, ones_where(iota((slots, TOP_ROWS), 0) >> 4 == iota((slots, TOP_ROWS), 1)))
    first, last = (back[:, at:at + 8, :].reshape(mids, 128).astype(bf16) for at in (0, 8))
    mid = dot_nt(ones_where((day < half) & (lane == lane_of(day))), first)
    mid = mid + dot_nt(ones_where((day >= half) & (lane == lane_of(day - half))), last)
    slot_count, width = rows // 256, min(128, mids)
    mid_count = mids // width
    taken = jnp.concatenate([taken[:days, :], taken[days:2 * days, :]], axis=1)
    slot_gaps = jnp.concatenate([taken[:, g * 256:(g + 1) * 256] for g in range(slot_count)], axis=0).astype(bf16)
    node_gaps = [jnp.concatenate([mid[:, g * width:(g + 1) * width], tops], axis=1) for g in range(mid_count)]
    node_gaps = jnp.concatenate(node_gaps, axis=0).astype(bf16)
    step = min(512, rows)
    copies = []
    for at in range(0, rows, step):
        place, mid, top = (places_ref[k:k + 1, at:at + step] for k in range(3))
        out = leaf_ref[:, at:at + step] + shift_ref[:, at:at + step]
        for gaps, hit, group, count in (
            (slot_gaps, hits(place & 255, 256), place >> 8, slot_count),
            (node_gaps, node_hits(mid, top, width), mid // width, mid_count),
        ):
            found = dot(gaps, hit)
            chosen = found[:days, :]
            for g in range(1, count):
                chosen = jnp.where(group == g, found[g * days:(g + 1) * days, :], chosen)
            out = out + chosen
        done_ref[:, at:at + step] = out
        copies.append(pltpu.make_async_copy(done_ref.at[:, at:at + step], out_ref.at[:, at:at + step], sems.at[at // step]))
        copies[-1].start()
    for copy in copies:
        copy.wait()


def per_device(leaf, seas, fine, mid, top, base_fine, base_mid, base_top):
    days, rows = leaf.shape
    owners = lax.axis_size("series")
    blocks = lax.axis_size("tm")
    quarter = (lax.axis_index("tm") // (blocks // 4)).astype(i32).reshape(1)
    vmem = pl.BlockSpec(memory_space=pltpu.VMEM)
    smem = pl.BlockSpec(memory_space=pltpu.SMEM)
    dense = (rows // 128, 128)

    sums = pl.pallas_call(
        start_kernel,
        out_shape=jax.ShapeDtypeStruct((blocks,) + dense, f32),
        in_specs=[pl.BlockSpec(memory_space=pltpu.HBM)],
        scratch_shapes=[pltpu.VMEM((days, rows), f32), pltpu.SemaphoreType.DMA((days // 8,))],
        compiler_params=pltpu.CompilerParams(vmem_limit_bytes=66900000),
        name="day_sums",
    )(leaf)
    parts = lax.all_to_all(sums, "tm", 0, 0, tiled=True)
    slots, nodes, places, come_from, base_rest, known = pl.pallas_call(
        lambda *refs: sort_kernel(owners, *refs),
        out_shape=(
            jax.ShapeDtypeStruct((days + 8, rows), f32),
            jax.ShapeDtypeStruct((days + 8, owners * 8 + TOP_ROWS), f32),
            jax.ShapeDtypeStruct((4, rows), i32),
            jax.ShapeDtypeStruct((2,) + dense, i32),
            jax.ShapeDtypeStruct((16, 128), f32),
            jax.ShapeDtypeStruct(dense, f32),
        ),
        in_specs=[smem] + [vmem] * 7,
        compiler_params=PARAMS,
        cost_estimate=pl.CostEstimate(flops=2 * 104 * owners * 42 * rows, bytes_accessed=4 * days * rows, transcendentals=0),
        name="sort",
    )(quarter, *(ids.reshape(1, rows) for ids in (fine, mid, top)), base_mid.T, base_top.reshape(1, days), seas, leaf)

    payload, shift = pl.pallas_call(
        send_kernel,
        out_shape=(jax.ShapeDtypeStruct((owners, 16, 128), bf16), jax.ShapeDtypeStruct((1, rows), f32)),
        compiler_params=PARAMS,
        name="pack",
    )(parts, known, come_from, slots, nodes, places)
    got = lax.all_to_all(payload, "series", 0, 0, tiled=True)
    back = pl.pallas_call(
        owner_kernel,
        out_shape=jax.ShapeDtypeStruct((owners, 16, 128), bf16),
        compiler_params=PARAMS,
        name="gaps",
    )(got, base_fine, base_rest)
    back = lax.all_to_all(back, "series", 0, 0, tiled=True)
    return pl.pallas_call(
        finish_kernel,
        out_shape=jax.ShapeDtypeStruct((days, rows), f32),
        in_specs=[vmem] * 4,
        out_specs=pl.BlockSpec(memory_space=pl.ANY),
        scratch_shapes=[pltpu.VMEM((days, rows), f32), pltpu.SemaphoreType.DMA((max(1, rows // 512),))],
        compiler_params=PARAMS,
        name="finish",
    )(leaf, shift, places, back)


def solution(mesh):
    return jax.shard_map(
        per_device,
        mesh=mesh,
        in_specs=(
            P("tm", "series"),
            P(None, "series"),
            P("series", None),
            P("series", None),
            P("series", None),
            P("tm", "series"),
            P("tm", "series"),
            P("tm", "series"),
        ),
        out_specs=P("tm", "series"),
        check_vma=False,
    )
```

```python
import jax
import jax.numpy as jnp
from jax import lax
from jax.experimental import pallas as pl
from jax.experimental.pallas import tpu as pltpu
from jax.sharding import Mesh
from jax.sharding import PartitionSpec as P

f32 = jnp.float32
bf16 = jnp.bfloat16
i32 = jnp.int32

PARAMS = pltpu.CompilerParams(vmem_limit_bytes=24 * 1024 * 1024)

ID = 48
ONE = 49
LOW = 50
MID_COUNT = 122
TOP_COUNT = 126
TOP_ROWS = 128


def iota(shape, dim):
    return lax.broadcasted_iota(i32, shape, dim)


def lane_of(x):
    return jnp.where(x < 15, x + 49, x + 98)


def top_lane(day):
    return lane_of(25 + day - 3 * (day // 3))


def ones_where(mask):
    return jnp.where(mask, 1.0, 0.0).astype(bf16)


def hits(codes, height):
    row = iota((height, 128), 0).astype(f32).astype(bf16)
    row = jnp.concatenate([row] * (codes.shape[1] // 128), axis=1)
    return jnp.where(row == codes.astype(f32).astype(bf16), jnp.ones((), bf16), jnp.zeros((), bf16))


def node_hits(mid, top, width):
    return jnp.concatenate([hits(mid & (width - 1), width), hits(top, TOP_ROWS)], axis=0)


def by_group(rows, group, count):
    return jnp.concatenate([rows * ones_where(group == g) for g in range(count)], axis=0)


def dot(a, b):
    return jnp.dot(a, b, preferred_element_type=f32)


def dot_nt(a, b, precision=None):
    return lax.dot_general(a, b, (((1,), (1,)), ((), ())), precision=precision, preferred_element_type=f32)


def slot_lanes(shape, dim):
    return (iota(shape, dim) & 63) <= ID


def row_of(dense):
    return jnp.concatenate([dense[at:at + 1, :] for at in range(dense.shape[0])], axis=1)


def dense_of(row):
    return jnp.concatenate([row[:, at:at + 128] for at in range(0, row.shape[1], 128)], axis=0)


def start_kernel(leaf_ref, sums_ref):
    sums = dense_of(jnp.sum(leaf_ref[...], axis=0, keepdims=True))
    sums_ref[...] = jnp.broadcast_to(sums[None], sums_ref.shape)


def halves_kernel(sums_ref, parts_ref, out_ref):
    out_ref[0, :, :] = sums_ref[0]
    out_ref[1, :, :] = jnp.sum(parts_ref[...], axis=0)


def ranks_of(owner, owners):
    rows = owner.shape[1]
    step = min(256, rows)
    before = ones_where(iota((step, step), 0) < iota((step, step), 1))
    base = jnp.zeros((owners, 1), f32)
    ranks = []
    for at in range(0, rows, step):
        hit = owner[:, at:at + step] == iota((owners, step), 0)
        hit_f = jnp.where(hit, 1.0, 0.0)
        seen = dot(hit_f.astype(bf16), before) + base
        ranks.append(jnp.sum(jnp.where(hit, seen, 0.0), axis=0, keepdims=True))
        base = base + jnp.sum(hit_f, axis=1, keepdims=True)
    return jnp.concatenate(ranks, axis=1).astype(i32)


def sort_kernel(
    owners, quarter_ref, fine_ref, mid_ref, top_ref, base_mid_ref, base_top_ref, seas_ref, leaf_ref,
    slots_ref, nodes_ref, places_ref, from_ref, rest_ref, known_ref,
):
    days, rows = leaf_ref.shape
    fine, mid, top = fine_ref[...], mid_ref[...], top_ref[...]
    owner = fine >> 6
    rank = ranks_of(owner, owners)
    place = (rank >> 4) * (owners * 16) + owner * 16 + (rank & 15)
    places_ref[0:1, :] = place
    places_ref[1:2, :] = mid
    places_ref[2:3, :] = top
    places_ref[3:4, :] = jnp.zeros_like(mid) + quarter_ref[0]

    leaf = leaf_ref[...]
    high = leaf.astype(bf16).astype(f32)
    series = iota((1, rows), 1)
    ones = jnp.ones((1, rows), f32)
    known = [(fine & 63).astype(f32), ones, ones, (series >> 7).astype(f32), (series & 127).astype(f32)]
    zeros = [jnp.zeros((3, rows), f32), jnp.zeros((8, rows), f32)]
    ext = jnp.concatenate([high] + known + [zeros[0], leaf - high, zeros[1]], axis=0).astype(bf16)
    height = days + 8

    def add_low(part):
        return part[:height, :] + jnp.concatenate([part[height:height + days, :], jnp.zeros((8, part.shape[1]), f32)], axis=0)

    count = rows // 256
    sums = dot_nt(by_group(ext, place >> 8, count), hits(place & 255, 256))
    for g in range(count):
        slots_ref[:, g * 256:(g + 1) * 256] = add_low(sums[g * 2 * height:(g + 1) * 2 * height, :])
    mids = owners * 8
    width = min(128, mids)
    count = mids // width
    sums = dot_nt(by_group(ext, mid // width, count), node_hits(mid, top, width))
    tops = jnp.zeros((height, TOP_ROWS), f32)
    for g in range(count):
        part = add_low(sums[g * 2 * height:(g + 1) * 2 * height, :])
        nodes_ref[:, g * width:(g + 1) * width] = part[:, :width]
        tops = tops + part[:, width:]
    nodes_ref[:, mids:] = tops
    from_ref[0, :, :] = dense_of(slots_ref[LOW + 1:LOW + 2, :]).astype(i32)
    from_ref[1, :, :] = dense_of(slots_ref[LOW + 2:LOW + 3, :]).astype(i32)
    seas = seas_ref[...]
    season_days = days * 2
    line = iota(seas.shape, 0)
    seas_own = jnp.sum(jnp.where(line == quarter_ref[0], seas, 0.0), axis=0, keepdims=True)
    seas_four = jnp.sum(jnp.where(line < 4, seas, 0.0), axis=0, keepdims=True)
    known_ref[...] = dense_of(0.5 * seas_own / season_days + 0.5 * (seas[4:5, :] - 0.5 * seas_four) / (season_days * 4))
    rest_ref[...] = rest_in_lanes(base_mid_ref[...], base_top_ref[...])


def rest_in_lanes(base_mid, base_top):
    days = base_mid.shape[1]
    half = days // 2
    day, lane = iota((days, 128), 0), iota((days, 128), 1)
    moves = (
        (day < half) & (lane == lane_of(day)),
        (day >= half) & (lane == lane_of(day - half)),
        lane == top_lane(day),
    )
    moves = [jnp.where(move, 1.0, 0.0) for move in moves]
    top = jnp.where(iota((16, days), 1) // 3 == iota((16, days), 0), base_top, 0.0)
    exact = lax.Precision.HIGHEST
    mids = [jnp.dot(base_mid, move, precision=exact, preferred_element_type=f32) for move in moves[:2]]
    return jnp.concatenate(mids, axis=0) + jnp.dot(top, moves[2], precision=exact, preferred_element_type=f32)


def split_count(sums):
    high = sums.astype(bf16).astype(f32)
    return jnp.where(iota(sums.shape, 0) == LOW, sums - high, high)


def send_kernel(here_ref, there_ref, known_ref, from_ref, slots_ref, nodes_ref, places_ref, pay_ref, shift_ref):
    owners = pay_ref.shape[0]
    rows = places_ref.shape[1]
    slots, mids = owners * 16, owners * 8
    days = slots_ref.shape[0] - 8
    season_days = days * 2
    own = here_ref[0, :, :] + there_ref[0, :, :]
    total = here_ref[1, :, :] + there_ref[1, :, :]
    shift = known_ref[...] - (0.5 * own / season_days + 0.25 * total / (season_days * 4))
    shift_row = row_of(shift)
    shift_ref[...] = shift_row

    line, lane = from_ref[0, :, :], from_ref[1, :, :]
    moved = jnp.zeros(shift.shape, f32)
    for at in range(shift.shape[0]):
        taken = jnp.take_along_axis(
            jnp.broadcast_to(shift[at:at + 1, :], shift.shape), lane, axis=1, mode="promise_in_bounds"
        )
        moved = jnp.where(line == at, taken, moved)
    moved = row_of(moved)

    high = shift_row.astype(bf16).astype(f32)
    ext = jnp.concatenate([high, shift_row - high, jnp.zeros((14, rows), f32)], axis=0).astype(bf16)
    mid, top = places_ref[1:2, :], places_ref[2:3, :]
    width = min(128, mids)
    count = mids // width
    found = dot_nt(by_group(ext, mid // width, count), node_hits(mid, top, width))
    found = [jnp.sum(found[g * 16:(g + 1) * 16, :], axis=0, keepdims=True) for g in range(count)]
    node_sums = jnp.concatenate([part[:, :width] for part in found] + [sum(part[:, width:] for part in found)], axis=1)
    is_day = iota((days + 8, 1), 0) < days
    pad = jnp.zeros((8, rows + mids + TOP_ROWS), f32)
    sums = jnp.concatenate([slots_ref[...], nodes_ref[...]], axis=1)
    sums = sums + jnp.where(is_day, jnp.concatenate([moved, node_sums], axis=1), 0.0)
    sums = jnp.concatenate([sums, pad], axis=0)

    tops = split_count(sums[:, 2 * slots + mids:]).astype(bf16)
    tops = dot(tops, ones_where(iota((TOP_ROWS, slots), 0) == iota((TOP_ROWS, slots), 1) >> 4))
    row, column = iota((64, slots), 0), iota((64, slots), 1) & 15
    keep = (
        ((row < days) & (row // 3 == column))
        | ((row == ONE) & (column < 8))
        | ((row == LOW) & (column >= 8))
    )
    tops = jnp.where(keep, tops, 0.0).astype(bf16)
    lane, day = iota((128, 64), 0), iota((128, 64), 1)
    top_move = ((day < days) & (lane == top_lane(day))) | (((day == ONE) | (day == LOW)) & (lane == TOP_COUNT))
    tops = dot(ones_where(top_move), tops)
    tiles = jnp.concatenate([sums[:, :slots], sums[:, slots:2 * slots]], axis=0)
    tiles = jnp.where(slot_lanes((128, slots), 0), tiles, tops)

    half = days // 2
    mid_sums = split_count(sums[:, 2 * slots:2 * slots + mids])
    day, lane = iota((64, 128), 0), iota((64, 128), 1)
    moves = (
        ((day < half) & (lane == lane_of(day))) | ((day == ONE) & (lane == MID_COUNT)),
        ((day >= half) & (day < days) & (lane == lane_of(day - half))) | ((day == LOW) & (lane == MID_COUNT)),
    )
    moves = [ones_where(move) for move in moves]
    group = min(16, owners)
    for g in range(owners // group):
        own = jnp.transpose(mid_sums[:, g * group * 8:(g + 1) * group * 8]).astype(bf16)
        extra = jnp.concatenate([dot(own, move).reshape(group, 8, 128) for move in moves], axis=1)
        start, stop = g * group * 16, (g + 1) * group * 16
        tile = jnp.concatenate([jnp.transpose(tiles[:, at:at + 128]) for at in range(start, stop, 128)], axis=0)
        pay_ref[g * group:(g + 1) * group, :, :] = (tile.reshape(group, 16, 128) + extra).astype(bf16)


def owner_kernel(got_ref, base_fine_ref, base_rest_ref, back_ref):
    owners = got_ref.shape[0]
    days, nodes = base_fine_ref.shape
    got = got_ref[...].astype(f32)
    flat = got.reshape(owners * 16, 128)
    lanes = iota(flat.shape, 1)
    node = iota((owners * 16, nodes), 1).astype(f32)
    pick_low = ones_where(flat[:, ID:ID + 1] == node)
    pick_high = ones_where(flat[:, 64 + ID:65 + ID] == node)
    turned = jnp.transpose(jnp.where((lanes & 63) == ONE, 1.0, flat)).astype(bf16)
    totals = dot(turned[0:64, :], pick_low) + dot(turned[64:128, :], pick_high)
    gap = (base_fine_ref[...] - totals[0:days, :]) / (totals[ONE:ONE + 1, :] + 1.0)
    gap = jnp.concatenate([gap, jnp.zeros((64 - days, nodes), f32)], axis=0)
    gap = jnp.transpose(jnp.concatenate([gap, gap], axis=0)).astype(bf16)
    spread = jnp.where(lanes < 64, dot(pick_low, gap), dot(pick_high, gap))

    rest = jnp.sum(got, axis=0)
    pair = rest + jnp.concatenate([rest[8:16, :], rest[0:8, :]], axis=0)
    of_top = iota(rest.shape, 1) > MID_COUNT
    count = jnp.where(of_top, pair[:, TOP_COUNT:TOP_COUNT + 1], pair[:, MID_COUNT:MID_COUNT + 1])
    gap_rest = jnp.where(slot_lanes(rest.shape, 1), 0.0, (base_rest_ref[...] - rest) / (count + 1.0))
    spread = jnp.where(slot_lanes(flat.shape, 1), spread, 0.0).reshape(owners, 16, 128)
    back_ref[...] = (spread + gap_rest[None]).astype(bf16)


def finish_kernel(leaf_ref, shift_ref, places_ref, back_ref, out_ref, done_ref, sems):
    days, rows = leaf_ref.shape
    owners = back_ref.shape[0]
    slots, mids = owners * 16, owners * 8
    half = days // 2
    back = back_ref[...].astype(f32)
    day, lane = iota((days, 128), 0), iota((days, 128), 1)
    take = jnp.concatenate([ones_where(lane == day), ones_where(lane == day + 64), ones_where(lane == top_lane(day))], axis=0)
    taken = dot_nt(take, back.reshape(slots, 128).astype(bf16))
    tops = jnp.where(iota((days, slots), 0) // 3 == (iota((days, slots), 1) & 15), taken[2 * days:, :], 0.0).astype(bf16)
    tops = dot(tops, ones_where(iota((slots, TOP_ROWS), 0) >> 4 == iota((slots, TOP_ROWS), 1)))
    first, last = (back[:, at:at + 8, :].reshape(mids, 128).astype(bf16) for at in (0, 8))
    mid = dot_nt(ones_where((day < half) & (lane == lane_of(day))), first)
    mid = mid + dot_nt(ones_where((day >= half) & (lane == lane_of(day - half))), last)
    slot_count, width = rows // 256, min(128, mids)
    mid_count = mids // width
    taken = jnp.concatenate([taken[:days, :], taken[days:2 * days, :]], axis=1)
    slot_gaps = jnp.concatenate([taken[:, g * 256:(g + 1) * 256] for g in range(slot_count)], axis=0).astype(bf16)
    node_gaps = [jnp.concatenate([mid[:, g * width:(g + 1) * width], tops], axis=1) for g in range(mid_count)]
    node_gaps = jnp.concatenate(node_gaps, axis=0).astype(bf16)
    step = min(512, rows)
    copies = []
    for at in range(0, rows, step):
        place, mid, top = (places_ref[k:k + 1, at:at + step] for k in range(3))
        out = leaf_ref[:, at:at + step] + shift_ref[:, at:at + step]
        for gaps, hit, group, count in (
            (slot_gaps, hits(place & 255, 256), place >> 8, slot_count),
            (node_gaps, node_hits(mid, top, width), mid // width, mid_count),
        ):
            found = dot(gaps, hit)
            chosen = found[:days, :]
            for g in range(1, count):
                chosen = jnp.where(group == g, found[g * days:(g + 1) * days, :], chosen)
            out = out + chosen
        done_ref[:, at:at + step] = out
        copies.append(pltpu.make_async_copy(done_ref.at[:, at:at + step], out_ref.at[:, at:at + step], sems.at[at // step]))
        copies[-1].start()
    for copy in copies:
        copy.wait()


def per_device(leaf, seas, fine, mid, top, base_fine, base_mid, base_top):
    days, rows = leaf.shape
    owners = lax.axis_size("series")
    chips = lax.axis_size("x")
    quarter = lax.axis_index("x").astype(i32).reshape(1)
    vmem = pl.BlockSpec(memory_space=pltpu.VMEM)
    smem = pl.BlockSpec(memory_space=pltpu.SMEM)
    dense = (rows // 128, 128)

    sums = pl.pallas_call(
        start_kernel, out_shape=jax.ShapeDtypeStruct((chips,) + dense, f32), compiler_params=PARAMS, name="day_sums"
    )(leaf)
    parts = lax.all_to_all(sums, "x", 0, 0, tiled=True)
    slots, nodes, places, come_from, base_rest, known = pl.pallas_call(
        lambda *refs: sort_kernel(owners, *refs),
        out_shape=(
            jax.ShapeDtypeStruct((days + 8, rows), f32),
            jax.ShapeDtypeStruct((days + 8, owners * 8 + TOP_ROWS), f32),
            jax.ShapeDtypeStruct((4, rows), i32),
            jax.ShapeDtypeStruct((2,) + dense, i32),
            jax.ShapeDtypeStruct((16, 128), f32),
            jax.ShapeDtypeStruct(dense, f32),
        ),
        in_specs=[smem] + [vmem] * 7,
        compiler_params=PARAMS,
        cost_estimate=pl.CostEstimate(flops=2 * 104 * owners * 42 * rows, bytes_accessed=4 * days * rows, transcendentals=0),
        name="sort",
    )(quarter, *(ids.reshape(1, rows) for ids in (fine, mid, top)), base_mid.T, base_top.reshape(1, days), seas, leaf)

    here = pl.pallas_call(
        halves_kernel, out_shape=jax.ShapeDtypeStruct((2,) + dense, f32), compiler_params=PARAMS, name="halves"
    )(sums, parts)
    there = lax.ppermute(here, "core", [(0, 1), (1, 0)])

    payload, shift = pl.pallas_call(
        send_kernel,
        out_shape=(jax.ShapeDtypeStruct((owners, 16, 128), bf16), jax.ShapeDtypeStruct((1, rows), f32)),
        compiler_params=PARAMS,
        name="pack",
    )(here, there, known, come_from, slots, nodes, places)
    got = lax.all_to_all(payload, "series", 0, 0, tiled=True)
    back = pl.pallas_call(
        owner_kernel,
        out_shape=jax.ShapeDtypeStruct((owners, 16, 128), bf16),
        compiler_params=PARAMS,
        name="gaps",
    )(got, base_fine, base_rest)
    back = lax.all_to_all(back, "series", 0, 0, tiled=True)
    return pl.pallas_call(
        finish_kernel,
        out_shape=jax.ShapeDtypeStruct((days, rows), f32),
        in_specs=[vmem] * 4,
        out_specs=pl.BlockSpec(memory_space=pl.ANY),
        scratch_shapes=[pltpu.VMEM((days, rows), f32), pltpu.SemaphoreType.DMA((max(1, rows // 512),))],
        compiler_params=PARAMS,
        name="finish",
    )(leaf, shift, places, back)


def solution(mesh):
    chips = mesh.devices.shape[0] // 2
    mesh = Mesh(mesh.devices.reshape(chips, 2, -1), ("x", "core", "series"))
    days = ("x", "core")
    return jax.shard_map(
        per_device,
        mesh=mesh,
        in_specs=(
            P(days, "series"),
            P(None, "series"),
            P("series", None),
            P("series", None),
            P("series", None),
            P(days, "series"),
            P(days, "series"),
            P(days, "series"),
        ),
        out_specs=P(days, "series"),
        check_vma=False,
    )
```

```python
import jax
import jax.numpy as jnp
from jax import lax
from jax.experimental import pallas as pl
from jax.experimental.pallas import tpu as pltpu
from jax.sharding import PartitionSpec as P

f32 = jnp.float32
bf16 = jnp.bfloat16
i32 = jnp.int32

PARAMS = pltpu.CompilerParams(vmem_limit_bytes=24 * 1024 * 1024)

ID = 48
ONE = 49
LOW = 50
MID_COUNT = 122
TOP_COUNT = 126
TOP_ROWS = 128


def iota(shape, dim):
    return lax.broadcasted_iota(i32, shape, dim)


def lane_of(x):
    return jnp.where(x < 15, x + 49, x + 98)


def top_lane(day):
    return lane_of(25 + day - 3 * (day // 3))


def ones_where(mask):
    return jnp.where(mask, 1.0, 0.0).astype(bf16)


def hits(codes, height):
    row = iota((height, 128), 0).astype(f32).astype(bf16)
    row = jnp.concatenate([row] * (codes.shape[1] // 128), axis=1)
    return jnp.where(row == codes.astype(f32).astype(bf16), jnp.ones((), bf16), jnp.zeros((), bf16))


def node_hits(mid, top, width):
    return jnp.concatenate([hits(mid & (width - 1), width), hits(top, TOP_ROWS)], axis=0)


def by_group(rows, group, count):
    return jnp.concatenate([rows * ones_where(group == g) for g in range(count)], axis=0)


def dot(a, b):
    return jnp.dot(a, b, preferred_element_type=f32)


def dot_nt(a, b, precision=None):
    return lax.dot_general(a, b, (((1,), (1,)), ((), ())), precision=precision, preferred_element_type=f32)


def slot_lanes(shape, dim):
    return (iota(shape, dim) & 63) <= ID


def row_of(dense):
    return jnp.concatenate([dense[at:at + 1, :] for at in range(dense.shape[0])], axis=1)


def dense_of(row):
    return jnp.concatenate([row[:, at:at + 128] for at in range(0, row.shape[1], 128)], axis=0)


def start_kernel(leaf_ref, sums_ref):
    sums = dense_of(jnp.sum(leaf_ref[...], axis=0, keepdims=True))
    sums_ref[...] = jnp.broadcast_to(sums[None], sums_ref.shape)


def ranks_of(owner, owners):
    rows = owner.shape[1]
    step = min(256, rows)
    before = ones_where(iota((step, step), 0) < iota((step, step), 1))
    base = jnp.zeros((owners, 1), f32)
    ranks = []
    for at in range(0, rows, step):
        hit = owner[:, at:at + step] == iota((owners, step), 0)
        hit_f = jnp.where(hit, 1.0, 0.0)
        seen = dot(hit_f.astype(bf16), before) + base
        ranks.append(jnp.sum(jnp.where(hit, seen, 0.0), axis=0, keepdims=True))
        base = base + jnp.sum(hit_f, axis=1, keepdims=True)
    return jnp.concatenate(ranks, axis=1).astype(i32)


def sort_kernel(
    owners, quarter_ref, fine_ref, mid_ref, top_ref, base_mid_ref, base_top_ref, seas_ref, leaf_ref,
    slots_ref, nodes_ref, places_ref, from_ref, rest_ref, known_ref,
):
    days, rows = leaf_ref.shape
    fine, mid, top = fine_ref[...], mid_ref[...], top_ref[...]
    owner = fine >> 6
    rank = ranks_of(owner, owners)
    place = (rank >> 4) * (owners * 16) + owner * 16 + (rank & 15)
    places_ref[0:1, :] = place
    places_ref[1:2, :] = mid
    places_ref[2:3, :] = top
    places_ref[3:4, :] = jnp.zeros_like(mid) + quarter_ref[0]

    leaf = leaf_ref[...]
    high = leaf.astype(bf16).astype(f32)
    series = iota((1, rows), 1)
    ones = jnp.ones((1, rows), f32)
    known = [(fine & 63).astype(f32), ones, ones, (series >> 7).astype(f32), (series & 127).astype(f32)]
    zeros = [jnp.zeros((3, rows), f32), jnp.zeros((8, rows), f32)]
    ext = jnp.concatenate([high] + known + [zeros[0], leaf - high, zeros[1]], axis=0).astype(bf16)
    height = days + 8

    def add_low(part):
        return part[:height, :] + jnp.concatenate([part[height:height + days, :], jnp.zeros((8, part.shape[1]), f32)], axis=0)

    count = rows // 256
    sums = dot_nt(by_group(ext, place >> 8, count), hits(place & 255, 256))
    for g in range(count):
        slots_ref[:, g * 256:(g + 1) * 256] = add_low(sums[g * 2 * height:(g + 1) * 2 * height, :])
    mids = owners * 8
    width = min(128, mids)
    count = mids // width
    sums = dot_nt(by_group(ext, mid // width, count), node_hits(mid, top, width))
    tops = jnp.zeros((height, TOP_ROWS), f32)
    for g in range(count):
        part = add_low(sums[g * 2 * height:(g + 1) * 2 * height, :])
        nodes_ref[:, g * width:(g + 1) * width] = part[:, :width]
        tops = tops + part[:, width:]
    nodes_ref[:, mids:] = tops
    from_ref[0, :, :] = dense_of(slots_ref[LOW + 1:LOW + 2, :]).astype(i32)
    from_ref[1, :, :] = dense_of(slots_ref[LOW + 2:LOW + 3, :]).astype(i32)
    seas = seas_ref[...]
    season_days = days * 2
    line = iota(seas.shape, 0)
    seas_own = jnp.sum(jnp.where(line == quarter_ref[0], seas, 0.0), axis=0, keepdims=True)
    seas_four = jnp.sum(jnp.where(line < 4, seas, 0.0), axis=0, keepdims=True)
    known_ref[...] = dense_of(0.5 * seas_own / season_days + 0.5 * (seas[4:5, :] - 0.5 * seas_four) / (season_days * 4))
    rest_ref[...] = rest_in_lanes(base_mid_ref[...], base_top_ref[...])


def rest_in_lanes(base_mid, base_top):
    days = base_mid.shape[1]
    half = days // 2
    day, lane = iota((days, 128), 0), iota((days, 128), 1)
    moves = (
        (day < half) & (lane == lane_of(day)),
        (day >= half) & (lane == lane_of(day - half)),
        lane == top_lane(day),
    )
    moves = [jnp.where(move, 1.0, 0.0) for move in moves]
    top = jnp.where(iota((16, days), 1) // 3 == iota((16, days), 0), base_top, 0.0)
    exact = lax.Precision.HIGHEST
    mids = [jnp.dot(base_mid, move, precision=exact, preferred_element_type=f32) for move in moves[:2]]
    return jnp.concatenate(mids, axis=0) + jnp.dot(top, moves[2], precision=exact, preferred_element_type=f32)


def split_count(sums):
    high = sums.astype(bf16).astype(f32)
    return jnp.where(iota(sums.shape, 0) == LOW, sums - high, high)


def send_kernel(parts_ref, known_ref, from_ref, slots_ref, nodes_ref, places_ref, pay_ref, shift_ref):
    owners = pay_ref.shape[0]
    rows = places_ref.shape[1]
    slots, mids = owners * 16, owners * 8
    days = slots_ref.shape[0] - 8
    season_days = days * 2
    parts = parts_ref[...]
    quarter = places_ref[3:4, 0:128]
    own = jnp.sum(jnp.where(iota(parts.shape, 0) >> 1 == quarter[None], parts, 0.0), axis=0)
    total = jnp.sum(parts, axis=0)
    shift = known_ref[...] - (0.5 * own / season_days + 0.25 * total / (season_days * 4))
    shift_row = row_of(shift)
    shift_ref[...] = shift_row

    line, lane = from_ref[0, :, :], from_ref[1, :, :]
    moved = jnp.zeros(shift.shape, f32)
    for at in range(shift.shape[0]):
        taken = jnp.take_along_axis(
            jnp.broadcast_to(shift[at:at + 1, :], shift.shape), lane, axis=1, mode="promise_in_bounds"
        )
        moved = jnp.where(line == at, taken, moved)
    moved = row_of(moved)

    high = shift_row.astype(bf16).astype(f32)
    ext = jnp.concatenate([high, shift_row - high, jnp.zeros((14, rows), f32)], axis=0).astype(bf16)
    mid, top = places_ref[1:2, :], places_ref[2:3, :]
    width = min(128, mids)
    count = mids // width
    found = dot_nt(by_group(ext, mid // width, count), node_hits(mid, top, width))
    found = [jnp.sum(found[g * 16:(g + 1) * 16, :], axis=0, keepdims=True) for g in range(count)]
    node_sums = jnp.concatenate([part[:, :width] for part in found] + [sum(part[:, width:] for part in found)], axis=1)
    is_day = iota((days + 8, 1), 0) < days
    pad = jnp.zeros((8, rows + mids + TOP_ROWS), f32)
    sums = jnp.concatenate([slots_ref[...], nodes_ref[...]], axis=1)
    sums = sums + jnp.where(is_day, jnp.concatenate([moved, node_sums], axis=1), 0.0)
    sums = jnp.concatenate([sums, pad], axis=0)

    tops = split_count(sums[:, 2 * slots + mids:]).astype(bf16)
    tops = dot(tops, ones_where(iota((TOP_ROWS, slots), 0) == iota((TOP_ROWS, slots), 1) >> 4))
    row, column = iota((64, slots), 0), iota((64, slots), 1) & 15
    keep = (
        ((row < days) & (row // 3 == column))
        | ((row == ONE) & (column < 8))
        | ((row == LOW) & (column >= 8))
    )
    tops = jnp.where(keep, tops, 0.0).astype(bf16)
    lane, day = iota((128, 64), 0), iota((128, 64), 1)
    top_move = ((day < days) & (lane == top_lane(day))) | (((day == ONE) | (day == LOW)) & (lane == TOP_COUNT))
    tops = dot(ones_where(top_move), tops)
    tiles = jnp.concatenate([sums[:, :slots], sums[:, slots:2 * slots]], axis=0)
    tiles = jnp.where(slot_lanes((128, slots), 0), tiles, tops)

    half = days // 2
    mid_sums = split_count(sums[:, 2 * slots:2 * slots + mids])
    day, lane = iota((64, 128), 0), iota((64, 128), 1)
    moves = (
        ((day < half) & (lane == lane_of(day))) | ((day == ONE) & (lane == MID_COUNT)),
        ((day >= half) & (day < days) & (lane == lane_of(day - half))) | ((day == LOW) & (lane == MID_COUNT)),
    )
    moves = [ones_where(move) for move in moves]
    group = min(16, owners)
    for g in range(owners // group):
        own = jnp.transpose(mid_sums[:, g * group * 8:(g + 1) * group * 8]).astype(bf16)
        extra = jnp.concatenate([dot(own, move).reshape(group, 8, 128) for move in moves], axis=1)
        start, stop = g * group * 16, (g + 1) * group * 16
        tile = jnp.concatenate([jnp.transpose(tiles[:, at:at + 128]) for at in range(start, stop, 128)], axis=0)
        pay_ref[g * group:(g + 1) * group, :, :] = (tile.reshape(group, 16, 128) + extra).astype(bf16)


def owner_kernel(got_ref, base_fine_ref, base_rest_ref, back_ref):
    owners = got_ref.shape[0]
    days, nodes = base_fine_ref.shape
    got = got_ref[...].astype(f32)
    flat = got.reshape(owners * 16, 128)
    lanes = iota(flat.shape, 1)
    node = iota((owners * 16, nodes), 1).astype(f32)
    pick_low = ones_where(flat[:, ID:ID + 1] == node)
    pick_high = ones_where(flat[:, 64 + ID:65 + ID] == node)
    turned = jnp.transpose(jnp.where((lanes & 63) == ONE, 1.0, flat)).astype(bf16)
    totals = dot(turned[0:64, :], pick_low) + dot(turned[64:128, :], pick_high)
    gap = (base_fine_ref[...] - totals[0:days, :]) / (totals[ONE:ONE + 1, :] + 1.0)
    gap = jnp.concatenate([gap, jnp.zeros((64 - days, nodes), f32)], axis=0)
    gap = jnp.transpose(jnp.concatenate([gap, gap], axis=0)).astype(bf16)
    spread = jnp.where(lanes < 64, dot(pick_low, gap), dot(pick_high, gap))

    rest = jnp.sum(got, axis=0)
    pair = rest + jnp.concatenate([rest[8:16, :], rest[0:8, :]], axis=0)
    of_top = iota(rest.shape, 1) > MID_COUNT
    count = jnp.where(of_top, pair[:, TOP_COUNT:TOP_COUNT + 1], pair[:, MID_COUNT:MID_COUNT + 1])
    gap_rest = jnp.where(slot_lanes(rest.shape, 1), 0.0, (base_rest_ref[...] - rest) / (count + 1.0))
    spread = jnp.where(slot_lanes(flat.shape, 1), spread, 0.0).reshape(owners, 16, 128)
    back_ref[...] = (spread + gap_rest[None]).astype(bf16)


def finish_kernel(leaf_ref, shift_ref, places_ref, back_ref, out_ref, done_ref, sems):
    days, rows = leaf_ref.shape
    owners = back_ref.shape[0]
    slots, mids = owners * 16, owners * 8
    half = days // 2
    back = back_ref[...].astype(f32)
    day, lane = iota((days, 128), 0), iota((days, 128), 1)
    flat = back.reshape(slots, 128)
    turned = jnp.concatenate([jnp.transpose(flat[at:at + 128, :]) for at in range(0, slots, 128)], axis=1)
    tops = dot(ones_where(lane == top_lane(day)), turned.astype(bf16))
    tops = jnp.where(iota((days, slots), 0) // 3 == (iota((days, slots), 1) & 15), tops, 0.0).astype(bf16)
    tops = dot(tops, ones_where(iota((slots, TOP_ROWS), 0) >> 4 == iota((slots, TOP_ROWS), 1)))
    first, last = (back[:, at:at + 8, :].reshape(mids, 128).astype(bf16) for at in (0, 8))
    mid = dot_nt(ones_where((day < half) & (lane == lane_of(day))), first)
    mid = mid + dot_nt(ones_where((day >= half) & (lane == lane_of(day - half))), last)
    slot_count, width = rows // 256, min(128, mids)
    mid_count = mids // width
    taken = jnp.concatenate([turned[:days, :], turned[64:64 + days, :]], axis=1)
    slot_gaps = jnp.concatenate([taken[:, g * 256:(g + 1) * 256] for g in range(slot_count)], axis=0).astype(bf16)
    node_gaps = [jnp.concatenate([mid[:, g * width:(g + 1) * width], tops], axis=1) for g in range(mid_count)]
    node_gaps = jnp.concatenate(node_gaps, axis=0).astype(bf16)
    step = min(256, rows)
    copies = []
    for at in range(0, rows, step):
        place, mid, top = (places_ref[k:k + 1, at:at + step] for k in range(3))
        out = leaf_ref[:, at:at + step] + shift_ref[:, at:at + step]
        for gaps, hit, group, count in (
            (slot_gaps, hits(place & 255, 256), place >> 8, slot_count),
            (node_gaps, node_hits(mid, top, width), mid // width, mid_count),
        ):
            found = dot(gaps, hit)
            chosen = found[:days, :]
            for g in range(1, count):
                chosen = jnp.where(group == g, found[g * days:(g + 1) * days, :], chosen)
            out = out + chosen
        done_ref[:, at:at + step] = out
        copies.append(pltpu.make_async_copy(done_ref.at[:, at:at + step], out_ref.at[:, at:at + step], sems.at[at // step]))
        copies[-1].start()
    for copy in copies:
        copy.wait()


def per_device(leaf, seas, fine, mid, top, base_fine, base_mid, base_top):
    days, rows = leaf.shape
    owners = lax.axis_size("series")
    blocks = lax.axis_size("tm")
    quarter = (lax.axis_index("tm") // (blocks // 4)).astype(i32).reshape(1)
    vmem = pl.BlockSpec(memory_space=pltpu.VMEM)
    smem = pl.BlockSpec(memory_space=pltpu.SMEM)
    dense = (rows // 128, 128)

    sums = pl.pallas_call(
        start_kernel, out_shape=jax.ShapeDtypeStruct((blocks,) + dense, f32), compiler_params=PARAMS, name="day_sums"
    )(leaf)
    parts = lax.all_to_all(sums, "tm", 0, 0, tiled=True)
    slots, nodes, places, come_from, base_rest, known = pl.pallas_call(
        lambda *refs: sort_kernel(owners, *refs),
        out_shape=(
            jax.ShapeDtypeStruct((days + 8, rows), f32),
            jax.ShapeDtypeStruct((days + 8, owners * 8 + TOP_ROWS), f32),
            jax.ShapeDtypeStruct((4, rows), i32),
            jax.ShapeDtypeStruct((2,) + dense, i32),
            jax.ShapeDtypeStruct((16, 128), f32),
            jax.ShapeDtypeStruct(dense, f32),
        ),
        in_specs=[smem] + [vmem] * 7,
        compiler_params=PARAMS,
        cost_estimate=pl.CostEstimate(flops=2 * 104 * owners * 42 * rows, bytes_accessed=4 * days * rows, transcendentals=0),
        name="sort",
    )(quarter, *(ids.reshape(1, rows) for ids in (fine, mid, top)), base_mid.T, base_top.reshape(1, days), seas, leaf)

    payload, shift = pl.pallas_call(
        send_kernel,
        out_shape=(jax.ShapeDtypeStruct((owners, 16, 128), bf16), jax.ShapeDtypeStruct((1, rows), f32)),
        compiler_params=PARAMS,
        name="pack",
    )(parts, known, come_from, slots, nodes, places)
    got = lax.all_to_all(payload, "series", 0, 0, tiled=True)
    back = pl.pallas_call(
        owner_kernel,
        out_shape=jax.ShapeDtypeStruct((owners, 16, 128), bf16),
        compiler_params=PARAMS,
        name="gaps",
    )(got, base_fine, base_rest)
    back = lax.all_to_all(back, "series", 0, 0, tiled=True)
    return pl.pallas_call(
        finish_kernel,
        out_shape=jax.ShapeDtypeStruct((days, rows), f32),
        in_specs=[vmem] * 4,
        out_specs=pl.BlockSpec(memory_space=pl.ANY),
        scratch_shapes=[pltpu.VMEM((days, rows), f32), pltpu.SemaphoreType.DMA((max(1, rows // 256),))],
        compiler_params=PARAMS,
        name="finish",
    )(leaf, shift, places, back)


def solution(mesh):
    return jax.shard_map(
        per_device,
        mesh=mesh,
        in_specs=(
            P("tm", "series"),
            P(None, "series"),
            P("series", None),
            P("series", None),
            P("series", None),
            P("tm", "series"),
            P("tm", "series"),
            P("tm", "series"),
        ),
        out_specs=P("tm", "series"),
        check_vma=False,
    )
```

```python
import math

import jax
import jax.numpy as jnp
from jax import lax
from jax.experimental import pallas as pl
from jax.experimental.pallas import tpu as pltpu
from jax.sharding import Mesh
from jax.sharding import PartitionSpec as P

f32 = jnp.float32
bf16 = jnp.bfloat16
i32 = jnp.int32

PARAMS = pltpu.CompilerParams(vmem_limit_bytes=24 * 1024 * 1024)

ID = 48
ONE = 49
LOW = 50
MID_COUNT = 122
TOP_COUNT = 126
TOP_ROWS = 128


def iota(shape, dim):
    return lax.broadcasted_iota(i32, shape, dim)


def lane_of(x):
    return jnp.where(x < 15, x + 49, x + 98)


def top_lane(day):
    return lane_of(25 + day - 3 * (day // 3))


def ones_where(mask):
    return jnp.where(mask, 1.0, 0.0).astype(bf16)


def hits(codes, height):
    row = iota((height, 128), 0).astype(f32).astype(bf16)
    row = jnp.concatenate([row] * (codes.shape[1] // 128), axis=1)
    return jnp.where(row == codes.astype(f32).astype(bf16), jnp.ones((), bf16), jnp.zeros((), bf16))


def node_hits(mid, top, width):
    return jnp.concatenate([hits(mid & (width - 1), width), hits(top, TOP_ROWS)], axis=0)


def by_group(rows, group, count):
    return jnp.concatenate([rows * ones_where(group == g) for g in range(count)], axis=0)


def dot(a, b):
    return jnp.dot(a, b, preferred_element_type=f32)


def dot_nt(a, b, precision=None):
    return lax.dot_general(a, b, (((1,), (1,)), ((), ())), precision=precision, preferred_element_type=f32)


def slot_lanes(shape, dim):
    return (iota(shape, dim) & 63) <= ID


def row_of(dense):
    return jnp.concatenate([dense[at:at + 1, :] for at in range(dense.shape[0])], axis=1)


def dense_of(row):
    return jnp.concatenate([row[:, at:at + 128] for at in range(0, row.shape[1], 128)], axis=0)


def start_kernel(leaf_ref, sums_ref):
    sums = dense_of(jnp.sum(leaf_ref[...], axis=0, keepdims=True))
    sums_ref[...] = jnp.broadcast_to(sums[None], sums_ref.shape)


def ranks_of(owner, owners):
    rows = owner.shape[1]
    step = min(256, rows)
    before = ones_where(iota((step, step), 0) < iota((step, step), 1))
    base = jnp.zeros((owners, 1), f32)
    ranks = []
    for at in range(0, rows, step):
        hit = owner[:, at:at + step] == iota((owners, step), 0)
        hit_f = jnp.where(hit, 1.0, 0.0)
        seen = dot(hit_f.astype(bf16), before) + base
        ranks.append(jnp.sum(jnp.where(hit, seen, 0.0), axis=0, keepdims=True))
        base = base + jnp.sum(hit_f, axis=1, keepdims=True)
    return jnp.concatenate(ranks, axis=1).astype(i32)


def sort_kernel(
    owners, quarter_ref, fine_ref, mid_ref, top_ref, base_mid_ref, base_top_ref, seas_ref, leaf_ref,
    slots_ref, nodes_ref, places_ref, from_ref, rest_ref, known_ref,
):
    days, rows = leaf_ref.shape
    side = math.isqrt(owners)
    fine, mid, top = fine_ref[...], mid_ref[...], top_ref[...]
    owner, mid_owner = fine >> 6, mid >> 3
    owner = (owner % side) * side + owner // side
    mid = ((mid_owner % side) * side + mid_owner // side) * 8 + (mid & 7)
    top = (top % side) * side + top // side
    rank = ranks_of(owner, owners)
    place = (rank >> 4) * (owners * 16) + owner * 16 + (rank & 15)
    places_ref[0:1, :] = place
    places_ref[1:2, :] = mid
    places_ref[2:3, :] = top
    places_ref[3:4, :] = jnp.zeros_like(mid) + quarter_ref[0]

    leaf = leaf_ref[...]
    high = leaf.astype(bf16).astype(f32)
    series = iota((1, rows), 1)
    ones = jnp.ones((1, rows), f32)
    known = [(fine & 63).astype(f32), ones, ones, (series >> 7).astype(f32), (series & 127).astype(f32)]
    zeros = [jnp.zeros((3, rows), f32), jnp.zeros((8, rows), f32)]
    ext = jnp.concatenate([high] + known + [zeros[0], leaf - high, zeros[1]], axis=0).astype(bf16)
    height = days + 8

    def add_low(part):
        return part[:height, :] + jnp.concatenate([part[height:height + days, :], jnp.zeros((8, part.shape[1]), f32)], axis=0)

    count = rows // 256
    sums = dot_nt(by_group(ext, place >> 8, count), hits(place & 255, 256))
    for g in range(count):
        slots_ref[:, g * 256:(g + 1) * 256] = add_low(sums[g * 2 * height:(g + 1) * 2 * height, :])
    mids = owners * 8
    width = min(128, mids)
    count = mids // width
    sums = dot_nt(by_group(ext, mid // width, count), node_hits(mid, top, width))
    tops = jnp.zeros((height, TOP_ROWS), f32)
    for g in range(count):
        part = add_low(sums[g * 2 * height:(g + 1) * 2 * height, :])
        nodes_ref[:, g * width:(g + 1) * width] = part[:, :width]
        tops = tops + part[:, width:]
    nodes_ref[:, mids:] = tops
    from_ref[0, :, :] = dense_of(slots_ref[LOW + 1:LOW + 2, :]).astype(i32)
    from_ref[1, :, :] = dense_of(slots_ref[LOW + 2:LOW + 3, :]).astype(i32)
    seas = seas_ref[...]
    season_days = days * 2
    line = iota(seas.shape, 0)
    seas_own = jnp.sum(jnp.where(line == quarter_ref[0], seas, 0.0), axis=0, keepdims=True)
    seas_four = jnp.sum(jnp.where(line < 4, seas, 0.0), axis=0, keepdims=True)
    known_ref[...] = dense_of(0.5 * seas_own / season_days + 0.5 * (seas[4:5, :] - 0.5 * seas_four) / (season_days * 4))
    rest_ref[...] = rest_in_lanes(base_mid_ref[...], base_top_ref[...])


def rest_in_lanes(base_mid, base_top):
    days = base_mid.shape[1]
    half = days // 2
    day, lane = iota((days, 128), 0), iota((days, 128), 1)
    moves = (
        (day < half) & (lane == lane_of(day)),
        (day >= half) & (lane == lane_of(day - half)),
        lane == top_lane(day),
    )
    moves = [jnp.where(move, 1.0, 0.0) for move in moves]
    top = jnp.where(iota((16, days), 1) // 3 == iota((16, days), 0), base_top, 0.0)
    exact = lax.Precision.HIGHEST
    mids = [jnp.dot(base_mid, move, precision=exact, preferred_element_type=f32) for move in moves[:2]]
    return jnp.concatenate(mids, axis=0) + jnp.dot(top, moves[2], precision=exact, preferred_element_type=f32)


def split_count(sums):
    high = sums.astype(bf16).astype(f32)
    return jnp.where(iota(sums.shape, 0) == LOW, sums - high, high)


def send_kernel(parts_ref, known_ref, from_ref, slots_ref, nodes_ref, places_ref, pay_ref, shift_ref):
    owners = pay_ref.shape[0]
    rows = places_ref.shape[1]
    slots, mids = owners * 16, owners * 8
    days = slots_ref.shape[0] - 8
    season_days = days * 2
    parts = parts_ref[...]
    quarter = places_ref[3:4, 0:128]
    own = jnp.sum(jnp.where(iota(parts.shape, 0) >> 1 == quarter[None], parts, 0.0), axis=0)
    total = jnp.sum(parts, axis=0)
    shift = known_ref[...] - (0.5 * own / season_days + 0.25 * total / (season_days * 4))
    shift_row = row_of(shift)
    shift_ref[...] = shift_row

    line, lane = from_ref[0, :, :], from_ref[1, :, :]
    moved = jnp.zeros(shift.shape, f32)
    for at in range(shift.shape[0]):
        taken = jnp.take_along_axis(
            jnp.broadcast_to(shift[at:at + 1, :], shift.shape), lane, axis=1, mode="promise_in_bounds"
        )
        moved = jnp.where(line == at, taken, moved)
    moved = row_of(moved)

    high = shift_row.astype(bf16).astype(f32)
    ext = jnp.concatenate([high, shift_row - high, jnp.zeros((14, rows), f32)], axis=0).astype(bf16)
    mid, top = places_ref[1:2, :], places_ref[2:3, :]
    width = min(128, mids)
    count = mids // width
    found = dot_nt(by_group(ext, mid // width, count), node_hits(mid, top, width))
    found = [jnp.sum(found[g * 16:(g + 1) * 16, :], axis=0, keepdims=True) for g in range(count)]
    node_sums = jnp.concatenate([part[:, :width] for part in found] + [sum(part[:, width:] for part in found)], axis=1)
    is_day = iota((days + 8, 1), 0) < days
    pad = jnp.zeros((8, rows + mids + TOP_ROWS), f32)
    sums = jnp.concatenate([slots_ref[...], nodes_ref[...]], axis=1)
    sums = sums + jnp.where(is_day, jnp.concatenate([moved, node_sums], axis=1), 0.0)
    sums = jnp.concatenate([sums, pad], axis=0)

    tops = split_count(sums[:, 2 * slots + mids:]).astype(bf16)
    tops = dot(tops, ones_where(iota((TOP_ROWS, slots), 0) == iota((TOP_ROWS, slots), 1) >> 4))
    row, column = iota((64, slots), 0), iota((64, slots), 1) & 15
    keep = (
        ((row < days) & (row // 3 == column))
        | ((row == ONE) & (column < 8))
        | ((row == LOW) & (column >= 8))
    )
    tops = jnp.where(keep, tops, 0.0).astype(bf16)
    lane, day = iota((128, 64), 0), iota((128, 64), 1)
    top_move = ((day < days) & (lane == top_lane(day))) | (((day == ONE) | (day == LOW)) & (lane == TOP_COUNT))
    tops = dot(ones_where(top_move), tops)
    tiles = jnp.concatenate([sums[:, :slots], sums[:, slots:2 * slots]], axis=0)
    tiles = jnp.where(slot_lanes((128, slots), 0), tiles, tops)

    half = days // 2
    mid_sums = split_count(sums[:, 2 * slots:2 * slots + mids])
    day, lane = iota((64, 128), 0), iota((64, 128), 1)
    moves = (
        ((day < half) & (lane == lane_of(day))) | ((day == ONE) & (lane == MID_COUNT)),
        ((day >= half) & (day < days) & (lane == lane_of(day - half))) | ((day == LOW) & (lane == MID_COUNT)),
    )
    moves = [ones_where(move) for move in moves]
    group = min(16, owners)
    for g in range(owners // group):
        own = jnp.transpose(mid_sums[:, g * group * 8:(g + 1) * group * 8]).astype(bf16)
        extra = jnp.concatenate([dot(own, move).reshape(group, 8, 128) for move in moves], axis=1)
        start, stop = g * group * 16, (g + 1) * group * 16
        tile = jnp.concatenate([jnp.transpose(tiles[:, at:at + 128]) for at in range(start, stop, 128)], axis=0)
        pay_ref[g * group:(g + 1) * group, :, :] = (tile.reshape(group, 16, 128) + extra).astype(bf16)


def owner_kernel(got_ref, base_fine_ref, base_rest_ref, back_ref):
    owners = got_ref.shape[0]
    days, nodes = base_fine_ref.shape
    got = got_ref[...].astype(f32)
    flat = got.reshape(owners * 16, 128)
    lanes = iota(flat.shape, 1)
    node = iota((owners * 16, nodes), 1).astype(f32)
    pick_low = ones_where(flat[:, ID:ID + 1] == node)
    pick_high = ones_where(flat[:, 64 + ID:65 + ID] == node)
    turned = jnp.transpose(jnp.where((lanes & 63) == ONE, 1.0, flat)).astype(bf16)
    totals = dot(turned[0:64, :], pick_low) + dot(turned[64:128, :], pick_high)
    gap = (base_fine_ref[...] - totals[0:days, :]) / (totals[ONE:ONE + 1, :] + 1.0)
    gap = jnp.concatenate([gap, jnp.zeros((64 - days, nodes), f32)], axis=0)
    gap = jnp.transpose(jnp.concatenate([gap, gap], axis=0)).astype(bf16)
    spread = jnp.where(lanes < 64, dot(pick_low, gap), dot(pick_high, gap))

    rest = jnp.sum(got, axis=0)
    pair = rest + jnp.concatenate([rest[8:16, :], rest[0:8, :]], axis=0)
    of_top = iota(rest.shape, 1) > MID_COUNT
    count = jnp.where(of_top, pair[:, TOP_COUNT:TOP_COUNT + 1], pair[:, MID_COUNT:MID_COUNT + 1])
    gap_rest = jnp.where(slot_lanes(rest.shape, 1), 0.0, (base_rest_ref[...] - rest) / (count + 1.0))
    spread = jnp.where(slot_lanes(flat.shape, 1), spread, 0.0).reshape(owners, 16, 128)
    back_ref[...] = (spread + gap_rest[None]).astype(bf16)


def finish_kernel(leaf_ref, shift_ref, places_ref, back_ref, out_ref, done_ref, sems):
    days, rows = leaf_ref.shape
    owners = back_ref.shape[0]
    slots, mids = owners * 16, owners * 8
    half = days // 2
    back = back_ref[...].astype(f32)
    day, lane = iota((days, 128), 0), iota((days, 128), 1)
    take = jnp.concatenate([ones_where(lane == day), ones_where(lane == day + 64), ones_where(lane == top_lane(day))], axis=0)
    taken = dot_nt(take, back.reshape(slots, 128).astype(bf16))
    tops = jnp.where(iota((days, slots), 0) // 3 == (iota((days, slots), 1) & 15), taken[2 * days:, :], 0.0).astype(bf16)
    tops = dot(tops, ones_where(iota((slots, TOP_ROWS), 0) >> 4 == iota((slots, TOP_ROWS), 1)))
    first, last = (back[:, at:at + 8, :].reshape(mids, 128).astype(bf16) for at in (0, 8))
    mid = dot_nt(ones_where((day < half) & (lane == lane_of(day))), first)
    mid = mid + dot_nt(ones_where((day >= half) & (lane == lane_of(day - half))), last)
    slot_count, width = rows // 256, min(128, mids)
    mid_count = mids // width
    taken = jnp.concatenate([taken[:days, :], taken[days:2 * days, :]], axis=1)
    slot_gaps = jnp.concatenate([taken[:, g * 256:(g + 1) * 256] for g in range(slot_count)], axis=0).astype(bf16)
    node_gaps = [jnp.concatenate([mid[:, g * width:(g + 1) * width], tops], axis=1) for g in range(mid_count)]
    node_gaps = jnp.concatenate(node_gaps, axis=0).astype(bf16)
    step = min(512, rows)
    copies = []
    for at in range(0, rows, step):
        place, mid, top = (places_ref[k:k + 1, at:at + step] for k in range(3))
        out = leaf_ref[:, at:at + step] + shift_ref[:, at:at + step]
        for gaps, hit, group, count in (
            (slot_gaps, hits(place & 255, 256), place >> 8, slot_count),
            (node_gaps, node_hits(mid, top, width), mid // width, mid_count),
        ):
            found = dot(gaps, hit)
            chosen = found[:days, :]
            for g in range(1, count):
                chosen = jnp.where(group == g, found[g * days:(g + 1) * days, :], chosen)
            out = out + chosen
        done_ref[:, at:at + step] = out
        copies.append(pltpu.make_async_copy(done_ref.at[:, at:at + step], out_ref.at[:, at:at + step], sems.at[at // step]))
        copies[-1].start()
    for copy in copies:
        copy.wait()


def per_device(leaf, seas, fine, mid, top, base_fine, base_mid, base_top):
    days, rows = leaf.shape
    owners = lax.axis_size("y") * lax.axis_size("z")
    blocks = lax.axis_size("tm")
    quarter = (lax.axis_index("tm") // (blocks // 4)).astype(i32).reshape(1)
    vmem = pl.BlockSpec(memory_space=pltpu.VMEM)
    smem = pl.BlockSpec(memory_space=pltpu.SMEM)
    dense = (rows // 128, 128)

    sums = pl.pallas_call(
        start_kernel, out_shape=jax.ShapeDtypeStruct((blocks,) + dense, f32), compiler_params=PARAMS, name="day_sums"
    )(leaf)
    parts = lax.all_to_all(sums, "tm", 0, 0, tiled=True)
    slots, nodes, places, come_from, base_rest, known = pl.pallas_call(
        lambda *refs: sort_kernel(owners, *refs),
        out_shape=(
            jax.ShapeDtypeStruct((days + 8, rows), f32),
            jax.ShapeDtypeStruct((days + 8, owners * 8 + TOP_ROWS), f32),
            jax.ShapeDtypeStruct((4, rows), i32),
            jax.ShapeDtypeStruct((2,) + dense, i32),
            jax.ShapeDtypeStruct((16, 128), f32),
            jax.ShapeDtypeStruct(dense, f32),
        ),
        in_specs=[smem] + [vmem] * 7,
        compiler_params=PARAMS,
        cost_estimate=pl.CostEstimate(flops=2 * 104 * owners * 42 * rows, bytes_accessed=4 * days * rows, transcendentals=0),
        name="sort",
    )(quarter, *(ids.reshape(1, rows) for ids in (fine, mid, top)), base_mid.T, base_top.reshape(1, days), seas, leaf)

    payload, shift = pl.pallas_call(
        send_kernel,
        out_shape=(jax.ShapeDtypeStruct((owners, 16, 128), bf16), jax.ShapeDtypeStruct((1, rows), f32)),
        compiler_params=PARAMS,
        name="pack",
    )(parts, known, come_from, slots, nodes, places)
    got = lax.all_to_all(payload, ("z", "y"), 0, 0, tiled=True)
    back = pl.pallas_call(
        owner_kernel,
        out_shape=jax.ShapeDtypeStruct((owners, 16, 128), bf16),
        compiler_params=PARAMS,
        name="gaps",
    )(got, base_fine, base_rest)
    back = lax.all_to_all(back, ("z", "y"), 0, 0, tiled=True)
    return pl.pallas_call(
        finish_kernel,
        out_shape=jax.ShapeDtypeStruct((days, rows), f32),
        in_specs=[vmem] * 4,
        out_specs=pl.BlockSpec(memory_space=pl.ANY),
        scratch_shapes=[pltpu.VMEM((days, rows), f32), pltpu.SemaphoreType.DMA((max(1, rows // 512),))],
        compiler_params=PARAMS,
        name="finish",
    )(leaf, shift, places, back)


def solution(mesh):
    blocks, places = mesh.devices.shape
    side = math.isqrt(places)
    mesh = Mesh(mesh.devices.reshape(blocks, side, side), ("tm", "y", "z"))
    series = ("y", "z")
    return jax.shard_map(
        per_device,
        mesh=mesh,
        in_specs=(
            P("tm", series),
            P(None, series),
            P(series, None),
            P(series, None),
            P(series, None),
            P("tm", series),
            P("tm", series),
            P("tm", series),
        ),
        out_specs=P("tm", series),
        check_vma=False,
    )
```

```python
import math

import jax
import jax.numpy as jnp
from jax import lax
from jax.experimental import pallas as pl
from jax.experimental.pallas import tpu as pltpu
from jax.sharding import Mesh
from jax.sharding import PartitionSpec as P

f32 = jnp.float32
bf16 = jnp.bfloat16
i32 = jnp.int32

PARAMS = pltpu.CompilerParams(vmem_limit_bytes=24 * 1024 * 1024)

ID = 48
ONE = 49
LOW = 50
MID_COUNT = 122
TOP_COUNT = 126
TOP_ROWS = 128


def iota(shape, dim):
    return lax.broadcasted_iota(i32, shape, dim)


def lane_of(x):
    return jnp.where(x < 15, x + 49, x + 98)


def top_lane(day):
    return lane_of(25 + day - 3 * (day // 3))


def ones_where(mask):
    return jnp.where(mask, 1.0, 0.0).astype(bf16)


def hits(codes, height):
    row = iota((height, 128), 0).astype(f32).astype(bf16)
    row = jnp.concatenate([row] * (codes.shape[1] // 128), axis=1)
    return jnp.where(row == codes.astype(f32).astype(bf16), jnp.ones((), bf16), jnp.zeros((), bf16))


def node_hits(mid, top, width):
    return jnp.concatenate([hits(mid & (width - 1), width), hits(top, TOP_ROWS)], axis=0)


def by_group(rows, group, count):
    return jnp.concatenate([rows * ones_where(group == g) for g in range(count)], axis=0)


def dot(a, b):
    return jnp.dot(a, b, preferred_element_type=f32)


def dot_nt(a, b, precision=None):
    return lax.dot_general(a, b, (((1,), (1,)), ((), ())), precision=precision, preferred_element_type=f32)


def slot_lanes(shape, dim):
    return (iota(shape, dim) & 63) <= ID


def row_of(dense):
    return jnp.concatenate([dense[at:at + 1, :] for at in range(dense.shape[0])], axis=1)


def dense_of(row):
    return jnp.concatenate([row[:, at:at + 128] for at in range(0, row.shape[1], 128)], axis=0)


def start_kernel(leaf_ref, sums_ref):
    sums = dense_of(jnp.sum(leaf_ref[...], axis=0, keepdims=True))
    sums_ref[...] = jnp.broadcast_to(sums[None], sums_ref.shape)


def ranks_of(owner, owners):
    rows = owner.shape[1]
    step = min(256, rows)
    before = ones_where(iota((step, step), 0) < iota((step, step), 1))
    base = jnp.zeros((owners, 1), f32)
    ranks = []
    for at in range(0, rows, step):
        hit = owner[:, at:at + step] == iota((owners, step), 0)
        hit_f = jnp.where(hit, 1.0, 0.0)
        seen = dot(hit_f.astype(bf16), before) + base
        ranks.append(jnp.sum(jnp.where(hit, seen, 0.0), axis=0, keepdims=True))
        base = base + jnp.sum(hit_f, axis=1, keepdims=True)
    return jnp.concatenate(ranks, axis=1).astype(i32)


def sort_kernel(
    owners, quarter_ref, fine_ref, mid_ref, top_ref, base_mid_ref, base_top_ref, seas_ref, leaf_ref,
    slots_ref, nodes_ref, places_ref, from_ref, rest_ref, known_ref,
):
    days, rows = leaf_ref.shape
    side = math.isqrt(owners)
    fine, mid, top = fine_ref[...], mid_ref[...], top_ref[...]
    owner, mid_owner = fine >> 6, mid >> 3
    owner = (owner % side) * side + owner // side
    mid = ((mid_owner % side) * side + mid_owner // side) * 8 + (mid & 7)
    top = (top % side) * side + top // side
    rank = ranks_of(owner, owners)
    place = (rank >> 4) * (owners * 16) + owner * 16 + (rank & 15)
    places_ref[0:1, :] = place
    places_ref[1:2, :] = mid
    places_ref[2:3, :] = top
    places_ref[3:4, :] = jnp.zeros_like(mid) + quarter_ref[0]

    leaf = leaf_ref[...]
    high = leaf.astype(bf16).astype(f32)
    series = iota((1, rows), 1)
    ones = jnp.ones((1, rows), f32)
    known = [(fine & 63).astype(f32), ones, ones, (series >> 7).astype(f32), (series & 127).astype(f32)]
    zeros = [jnp.zeros((3, rows), f32), jnp.zeros((8, rows), f32)]
    ext = jnp.concatenate([high] + known + [zeros[0], leaf - high, zeros[1]], axis=0).astype(bf16)
    height = days + 8

    def add_low(part):
        return part[:height, :] + jnp.concatenate([part[height:height + days, :], jnp.zeros((8, part.shape[1]), f32)], axis=0)

    count = rows // 256
    sums = dot_nt(by_group(ext, place >> 8, count), hits(place & 255, 256))
    for g in range(count):
        slots_ref[:, g * 256:(g + 1) * 256] = add_low(sums[g * 2 * height:(g + 1) * 2 * height, :])
    mids = owners * 8
    width = min(128, mids)
    count = mids // width
    sums = dot_nt(by_group(ext, mid // width, count), node_hits(mid, top, width))
    tops = jnp.zeros((height, TOP_ROWS), f32)
    for g in range(count):
        part = add_low(sums[g * 2 * height:(g + 1) * 2 * height, :])
        nodes_ref[:, g * width:(g + 1) * width] = part[:, :width]
        tops = tops + part[:, width:]
    nodes_ref[:, mids:] = tops
    from_ref[0, :, :] = dense_of(slots_ref[LOW + 1:LOW + 2, :]).astype(i32)
    from_ref[1, :, :] = dense_of(slots_ref[LOW + 2:LOW + 3, :]).astype(i32)
    seas = seas_ref[...]
    season_days = days * 2
    line = iota(seas.shape, 0)
    seas_own = jnp.sum(jnp.where(line == quarter_ref[0], seas, 0.0), axis=0, keepdims=True)
    seas_four = jnp.sum(jnp.where(line < 4, seas, 0.0), axis=0, keepdims=True)
    known_ref[...] = dense_of(0.5 * seas_own / season_days + 0.5 * (seas[4:5, :] - 0.5 * seas_four) / (season_days * 4))
    rest_ref[...] = rest_in_lanes(base_mid_ref[...], base_top_ref[...])


def rest_in_lanes(base_mid, base_top):
    days = base_mid.shape[1]
    half = days // 2
    day, lane = iota((days, 128), 0), iota((days, 128), 1)
    moves = (
        (day < half) & (lane == lane_of(day)),
        (day >= half) & (lane == lane_of(day - half)),
        lane == top_lane(day),
    )
    moves = [jnp.where(move, 1.0, 0.0) for move in moves]
    top = jnp.where(iota((16, days), 1) // 3 == iota((16, days), 0), base_top, 0.0)
    exact = lax.Precision.HIGHEST
    mids = [jnp.dot(base_mid, move, precision=exact, preferred_element_type=f32) for move in moves[:2]]
    return jnp.concatenate(mids, axis=0) + jnp.dot(top, moves[2], precision=exact, preferred_element_type=f32)


def split_count(sums):
    high = sums.astype(bf16).astype(f32)
    return jnp.where(iota(sums.shape, 0) == LOW, sums - high, high)


def send_kernel(parts_ref, known_ref, from_ref, slots_ref, nodes_ref, places_ref, pay_ref, shift_ref):
    owners = pay_ref.shape[0]
    rows = places_ref.shape[1]
    slots, mids = owners * 16, owners * 8
    days = slots_ref.shape[0] - 8
    season_days = days * 2
    parts = parts_ref[...]
    quarter = places_ref[3:4, 0:128]
    own = jnp.sum(jnp.where((iota(parts.shape, 0) & 3) == quarter[None], parts, 0.0), axis=0)
    total = jnp.sum(parts, axis=0)
    shift = known_ref[...] - (0.5 * own / season_days + 0.25 * total / (season_days * 4))
    shift_row = row_of(shift)
    shift_ref[...] = shift_row

    line, lane = from_ref[0, :, :], from_ref[1, :, :]
    moved = jnp.zeros(shift.shape, f32)
    for at in range(shift.shape[0]):
        taken = jnp.take_along_axis(
            jnp.broadcast_to(shift[at:at + 1, :], shift.shape), lane, axis=1, mode="promise_in_bounds"
        )
        moved = jnp.where(line == at, taken, moved)
    moved = row_of(moved)

    high = shift_row.astype(bf16).astype(f32)
    ext = jnp.concatenate([high, shift_row - high, jnp.zeros((14, rows), f32)], axis=0).astype(bf16)
    mid, top = places_ref[1:2, :], places_ref[2:3, :]
    width = min(128, mids)
    count = mids // width
    found = dot_nt(by_group(ext, mid // width, count), node_hits(mid, top, width))
    found = [jnp.sum(found[g * 16:(g + 1) * 16, :], axis=0, keepdims=True) for g in range(count)]
    node_sums = jnp.concatenate([part[:, :width] for part in found] + [sum(part[:, width:] for part in found)], axis=1)
    is_day = iota((days + 8, 1), 0) < days
    pad = jnp.zeros((8, rows + mids + TOP_ROWS), f32)
    sums = jnp.concatenate([slots_ref[...], nodes_ref[...]], axis=1)
    sums = sums + jnp.where(is_day, jnp.concatenate([moved, node_sums], axis=1), 0.0)
    sums = jnp.concatenate([sums, pad], axis=0)

    tops = split_count(sums[:, 2 * slots + mids:]).astype(bf16)
    tops = dot(tops, ones_where(iota((TOP_ROWS, slots), 0) == iota((TOP_ROWS, slots), 1) >> 4))
    row, column = iota((64, slots), 0), iota((64, slots), 1) & 15
    keep = (
        ((row < days) & (row // 3 == column))
        | ((row == ONE) & (column < 8))
        | ((row == LOW) & (column >= 8))
    )
    tops = jnp.where(keep, tops, 0.0).astype(bf16)
    lane, day = iota((128, 64), 0), iota((128, 64), 1)
    top_move = ((day < days) & (lane == top_lane(day))) | (((day == ONE) | (day == LOW)) & (lane == TOP_COUNT))
    tops = dot(ones_where(top_move), tops)
    tiles = jnp.concatenate([sums[:, :slots], sums[:, slots:2 * slots]], axis=0)
    tiles = jnp.where(slot_lanes((128, slots), 0), tiles, tops)

    half = days // 2
    mid_sums = split_count(sums[:, 2 * slots:2 * slots + mids])
    day, lane = iota((64, 128), 0), iota((64, 128), 1)
    moves = (
        ((day < half) & (lane == lane_of(day))) | ((day == ONE) & (lane == MID_COUNT)),
        ((day >= half) & (day < days) & (lane == lane_of(day - half))) | ((day == LOW) & (lane == MID_COUNT)),
    )
    moves = [ones_where(move) for move in moves]
    group = min(16, owners)
    for g in range(owners // group):
        own = jnp.transpose(mid_sums[:, g * group * 8:(g + 1) * group * 8]).astype(bf16)
        extra = jnp.concatenate([dot(own, move).reshape(group, 8, 128) for move in moves], axis=1)
        start, stop = g * group * 16, (g + 1) * group * 16
        tile = jnp.concatenate([jnp.transpose(tiles[:, at:at + 128]) for at in range(start, stop, 128)], axis=0)
        pay_ref[g * group:(g + 1) * group, :, :] = (tile.reshape(group, 16, 128) + extra).astype(bf16)


def owner_kernel(got_ref, base_fine_ref, base_rest_ref, back_ref):
    owners = got_ref.shape[0]
    days, nodes = base_fine_ref.shape
    got = got_ref[...].astype(f32)
    flat = got.reshape(owners * 16, 128)
    lanes = iota(flat.shape, 1)
    node = iota((owners * 16, nodes), 1).astype(f32)
    pick_low = ones_where(flat[:, ID:ID + 1] == node)
    pick_high = ones_where(flat[:, 64 + ID:65 + ID] == node)
    turned = jnp.transpose(jnp.where((lanes & 63) == ONE, 1.0, flat)).astype(bf16)
    totals = dot(turned[0:64, :], pick_low) + dot(turned[64:128, :], pick_high)
    gap = (base_fine_ref[...] - totals[0:days, :]) / (totals[ONE:ONE + 1, :] + 1.0)
    gap = jnp.concatenate([gap, jnp.zeros((64 - days, nodes), f32)], axis=0)
    gap = jnp.transpose(jnp.concatenate([gap, gap], axis=0)).astype(bf16)
    spread = jnp.where(lanes < 64, dot(pick_low, gap), dot(pick_high, gap))

    rest = jnp.sum(got, axis=0)
    pair = rest + jnp.concatenate([rest[8:16, :], rest[0:8, :]], axis=0)
    of_top = iota(rest.shape, 1) > MID_COUNT
    count = jnp.where(of_top, pair[:, TOP_COUNT:TOP_COUNT + 1], pair[:, MID_COUNT:MID_COUNT + 1])
    gap_rest = jnp.where(slot_lanes(rest.shape, 1), 0.0, (base_rest_ref[...] - rest) / (count + 1.0))
    spread = jnp.where(slot_lanes(flat.shape, 1), spread, 0.0).reshape(owners, 16, 128)
    back_ref[...] = (spread + gap_rest[None]).astype(bf16)


def finish_kernel(leaf_ref, shift_ref, places_ref, back_ref, out_ref, done_ref, sems):
    days, rows = leaf_ref.shape
    owners = back_ref.shape[0]
    slots, mids = owners * 16, owners * 8
    half = days // 2
    back = back_ref[...].astype(f32)
    day, lane = iota((days, 128), 0), iota((days, 128), 1)
    take = jnp.concatenate([ones_where(lane == day), ones_where(lane == day + 64), ones_where(lane == top_lane(day))], axis=0)
    taken = dot_nt(take, back.reshape(slots, 128).astype(bf16))
    tops = jnp.where(iota((days, slots), 0) // 3 == (iota((days, slots), 1) & 15), taken[2 * days:, :], 0.0).astype(bf16)
    tops = dot(tops, ones_where(iota((slots, TOP_ROWS), 0) >> 4 == iota((slots, TOP_ROWS), 1)))
    first, last = (back[:, at:at + 8, :].reshape(mids, 128).astype(bf16) for at in (0, 8))
    mid = dot_nt(ones_where((day < half) & (lane == lane_of(day))), first)
    mid = mid + dot_nt(ones_where((day >= half) & (lane == lane_of(day - half))), last)
    slot_count, width = rows // 256, min(128, mids)
    mid_count = mids // width
    taken = jnp.concatenate([taken[:days, :], taken[days:2 * days, :]], axis=1)
    slot_gaps = jnp.concatenate([taken[:, g * 256:(g + 1) * 256] for g in range(slot_count)], axis=0).astype(bf16)
    node_gaps = [jnp.concatenate([mid[:, g * width:(g + 1) * width], tops], axis=1) for g in range(mid_count)]
    node_gaps = jnp.concatenate(node_gaps, axis=0).astype(bf16)
    step = min(512, rows)
    copies = []
    for at in range(0, rows, step):
        place, mid, top = (places_ref[k:k + 1, at:at + step] for k in range(3))
        out = leaf_ref[:, at:at + step] + shift_ref[:, at:at + step]
        for gaps, hit, group, count in (
            (slot_gaps, hits(place & 255, 256), place >> 8, slot_count),
            (node_gaps, node_hits(mid, top, width), mid // width, mid_count),
        ):
            found = dot(gaps, hit)
            chosen = found[:days, :]
            for g in range(1, count):
                chosen = jnp.where(group == g, found[g * days:(g + 1) * days, :], chosen)
            out = out + chosen
        done_ref[:, at:at + step] = out
        copies.append(pltpu.make_async_copy(done_ref.at[:, at:at + step], out_ref.at[:, at:at + step], sems.at[at // step]))
        copies[-1].start()
    for copy in copies:
        copy.wait()


def per_device(leaf, seas, fine, mid, top, base_fine, base_mid, base_top):
    days, rows = leaf.shape
    owners = lax.axis_size("y") * lax.axis_size("z")
    blocks = lax.axis_size("x") * lax.axis_size("core")
    quarter = lax.axis_index("x").astype(i32).reshape(1)
    vmem = pl.BlockSpec(memory_space=pltpu.VMEM)
    smem = pl.BlockSpec(memory_space=pltpu.SMEM)
    dense = (rows // 128, 128)

    sums = pl.pallas_call(
        start_kernel, out_shape=jax.ShapeDtypeStruct((blocks,) + dense, f32), compiler_params=PARAMS, name="day_sums"
    )(leaf)
    parts = lax.all_to_all(sums, ("core", "x"), 0, 0, tiled=True)
    slots, nodes, places, come_from, base_rest, known = pl.pallas_call(
        lambda *refs: sort_kernel(owners, *refs),
        out_shape=(
            jax.ShapeDtypeStruct((days + 8, rows), f32),
            jax.ShapeDtypeStruct((days + 8, owners * 8 + TOP_ROWS), f32),
            jax.ShapeDtypeStruct((4, rows), i32),
            jax.ShapeDtypeStruct((2,) + dense, i32),
            jax.ShapeDtypeStruct((16, 128), f32),
            jax.ShapeDtypeStruct(dense, f32),
        ),
        in_specs=[smem] + [vmem] * 7,
        compiler_params=PARAMS,
        cost_estimate=pl.CostEstimate(flops=2 * 104 * owners * 42 * rows, bytes_accessed=4 * days * rows, transcendentals=0),
        name="sort",
    )(quarter, *(ids.reshape(1, rows) for ids in (fine, mid, top)), base_mid.T, base_top.reshape(1, days), seas, leaf)

    payload, shift = pl.pallas_call(
        send_kernel,
        out_shape=(jax.ShapeDtypeStruct((owners, 16, 128), bf16), jax.ShapeDtypeStruct((1, rows), f32)),
        compiler_params=PARAMS,
        name="pack",
    )(parts, known, come_from, slots, nodes, places)
    got = lax.all_to_all(payload, ("z", "y"), 0, 0, tiled=True)
    back = pl.pallas_call(
        owner_kernel,
        out_shape=jax.ShapeDtypeStruct((owners, 16, 128), bf16),
        compiler_params=PARAMS,
        name="gaps",
    )(got, base_fine, base_rest)
    back = lax.all_to_all(back, ("z", "y"), 0, 0, tiled=True)
    return pl.pallas_call(
        finish_kernel,
        out_shape=jax.ShapeDtypeStruct((days, rows), f32),
        in_specs=[vmem] * 4,
        out_specs=pl.BlockSpec(memory_space=pl.ANY),
        scratch_shapes=[pltpu.VMEM((days, rows), f32), pltpu.SemaphoreType.DMA((max(1, rows // 512),))],
        compiler_params=PARAMS,
        name="finish",
    )(leaf, shift, places, back)


def solution(mesh):
    blocks, places = mesh.devices.shape
    side = math.isqrt(places)
    mesh = Mesh(mesh.devices.reshape(blocks // 2, 2, side, side), ("x", "core", "y", "z"))
    days = ("x", "core")
    series = ("y", "z")
    return jax.shard_map(
        per_device,
        mesh=mesh,
        in_specs=(
            P(days, series),
            P(None, series),
            P(series, None),
            P(series, None),
            P(series, None),
            P(days, series),
            P(days, series),
            P(days, series),
        ),
        out_specs=P(days, series),
        check_vma=False,
    )
```
